32 devices in a mesh: ctx: 8 (over z, y), head: 4 (over x, core).
Axes of the slice: x: 2, y: 2, z: 4, core: 2. Of those that a mesh axis runs over, the one named last changes fastest.
Arguments:
- features: bfloat16 [8192, 16384], P('ctx', 'head'), may hold values from -6 to 6
- gates: bfloat16 [8192, 16384], P('ctx', 'head'), may hold values from -6 to 6
- state_io: bfloat16 [8192, 2, 2048], P('ctx', None, 'head'), may hold values from -6 to 6
- step_size: float32 [256, 8192], P('head', 'ctx'), may hold values from 0.004 to 0.02
- log_decay: float32 [256, 8192], P('head', 'ctx'), may hold values from -2 to 0, as said below
- conv_feat: bfloat16 [4, 16384], P(None, 'head'), may hold values from -3 to 3
- conv_state: bfloat16 [4, 2, 2048], P(None, None, 'head'), may hold values from -3 to 3
- skip_gain: float32 [256], P('head'), may hold values from 0.5 to 1.5
- norm_gain: float32 [16384], P('head'), may hold values from 0.25 to 1.75
Outputs:
- mixed: bfloat16 [8192, 16384], P(('ctx', 'head'))
The draws below stay inside these ranges and needn't reach their ends.
Inputs may be any that keep to these rules, and one draw needn't show every extreme that they name: `log_decay`: every entry is negative.
All inputs are finite; a program needn't handle non-finite values.
Results may differ from the reference program's by a relative error of at most 0.0034.
Values may be sent and summed in bfloat16 or wider, within the bound.
No kernel may reach another device: no remote copies, remote signals or barrier semaphores. Data moves between devices by JAX's collectives and lax.ppermute only.
A program may use at most 256 MiB of HBM per device.

```python
import math
import jax
import jax.numpy as jnp
from jax import lax

MIXER_HEADS = 256
HEADDIM = 64
STATE = 256
GROUPS = 8
CONV = 4
SPAN = 128
TOK_DEV = 1024
INNER = 16384
RESPONSE_TOKENS = 8192


def draw_log_decay(key, part):
    random_split_keys = jax.random.split(key, 7)
    slow_share = 0.6
    slow_heads = jax.random.uniform(random_split_keys[0], (MIXER_HEADS, 1)) < slow_share
    fast_rate = jnp.exp(jax.random.uniform(random_split_keys[1], (MIXER_HEADS, 1), minval=math.log(0.02), maxval=math.log(0.035)))
    slow_rate = jnp.exp(jax.random.uniform(random_split_keys[2], (MIXER_HEADS, 1), minval=math.log(0.05), maxval=math.log(0.3))) / RESPONSE_TOKENS
    baseline_decay_rate = jnp.where(slow_heads, slow_rate, fast_rate)
    blocks = RESPONSE_TOKENS // TOK_DEV
    block_multiplier = jnp.exp(jax.random.uniform(random_split_keys[3], (MIXER_HEADS, blocks, 1), minval=math.log(0.5), maxval=math.log(2.0)))
    block_multiplier = jnp.broadcast_to(block_multiplier, (MIXER_HEADS, blocks, TOK_DEV)).reshape(MIXER_HEADS, RESPONSE_TOKENS)
    decay_jitter = jnp.exp(jax.random.uniform(random_split_keys[4], (MIXER_HEADS, RESPONSE_TOKENS), minval=-0.5, maxval=0.5))
    spike_position = jax.random.randint(random_split_keys[5], (3, 1), 0, RESPONSE_TOKENS)
    spike_decay_drop = jax.random.uniform(random_split_keys[6], (3, MIXER_HEADS, 1), minval=0.2, maxval=0.3)
    token_positions = jnp.arange(RESPONSE_TOKENS, dtype=jnp.int32)[None, :]
    decay_spikes = jnp.zeros((MIXER_HEADS, RESPONSE_TOKENS), jnp.float32)
    for spike_index in range(3):
        decay_spikes = decay_spikes + jnp.where(token_positions == spike_position[spike_index], jnp.log(1.0 - spike_decay_drop[spike_index]), 0.0)
    return (-baseline_decay_rate * block_multiplier * decay_jitter + decay_spikes).astype(jnp.float32)


def shard_levels(key, shape, cuts, low, top_value):
    gain, own = 1.0, jax.random.fold_in(key, 6)
    for dim, shards_of in cuts:
        steps = jnp.exp(jax.random.uniform(jax.random.fold_in(own, dim), (shards_of,), jnp.float32, low / len(cuts), top_value / len(cuts)))
        gain = gain * jnp.repeat(steps, shape[dim] // shards_of).reshape([-1 if axis == dim else 1 for axis in range(len(shape))])
    return gain


def bell_draw(stream_key, extent, deviation, limit, shards=(), kind=jnp.bfloat16):
    array = deviation * jax.random.normal(stream_key, extent, jnp.float32)
    if shards:
        array = array * shard_levels(stream_key, extent, shards, -0.22, 0.18)
    return jnp.clip(array, -limit, limit).astype(kind)


def setup_inputs(seed: int = 0) -> dict:
    arg_keys = jax.random.split(jax.random.key(seed), 10)
    return {
        "features": bell_draw(arg_keys[0], (RESPONSE_TOKENS, INNER), 1.0, 6.0, ((0, 8), (1, 4))),
        "gates": bell_draw(arg_keys[1], (RESPONSE_TOKENS, INNER), 1.0, 6.0, ((0, 8), (1, 4))),
        "state_io": bell_draw(arg_keys[2], (RESPONSE_TOKENS, 2, GROUPS * STATE), 1.0, 6.0, ((0, 8), (2, 4))),
        "step_size": jnp.clip(jnp.exp(math.log(0.02) - 1.6094378 * jax.random.uniform(arg_keys[3], (MIXER_HEADS, RESPONSE_TOKENS), jnp.float32) ** shard_levels(arg_keys[3], (MIXER_HEADS, RESPONSE_TOKENS), ((0, 4), (1, 8)), -0.2, 0.2)), 0.004, 0.02),
        "log_decay": draw_log_decay(jax.random.fold_in(arg_keys[9], 71), 0),
        "conv_feat": bell_draw(arg_keys[5], (CONV, INNER), CONV ** -0.5, 3.0, ((1, 4),)),
        "conv_state": bell_draw(arg_keys[6], (CONV, 2, GROUPS * STATE), CONV ** -0.5, 3.0, ((2, 4),)),
        "skip_gain": jnp.clip(0.5 + 1.0 * jax.random.uniform(arg_keys[7], (MIXER_HEADS,), jnp.float32) ** shard_levels(arg_keys[7], (MIXER_HEADS,), ((0, 4),), -0.2, 0.2), 0.5, 1.5),
        "norm_gain": jnp.clip(1.0 + 0.15 * jax.random.normal(arg_keys[8], (INNER,), jnp.float32), 0.25, 1.75),
    }


def causal_conv(values, kernel):
    taps = kernel.shape[0]
    length = values.shape[0]
    padding = [(taps - 1, 0)] + [(0, 0)] * (values.ndim - 1)
    padded = jnp.pad(values, padding)
    summed = jnp.zeros(values.shape, jnp.float32)
    for offset in range(taps):
        summed = summed + kernel[offset].astype(jnp.float32) * padded[offset:offset + length].astype(jnp.float32)
    return jax.nn.silu(summed).astype(jnp.bfloat16)

def group_scan(pieces):
    feat_group, in_group, out_group, step_group, decay_group = pieces
    span_count = RESPONSE_TOKENS // SPAN
    per_group = step_group.shape[0]
    feat_spans = feat_group.reshape(span_count, SPAN, per_group, HEADDIM)
    in_spans = in_group.reshape(span_count, SPAN, STATE)
    out_spans = out_group.reshape(span_count, SPAN, STATE)
    step_spans = step_group.reshape(per_group, span_count, SPAN).transpose(1, 0, 2)
    decay_spans = decay_group.reshape(per_group, span_count, SPAN).transpose(1, 0, 2)
    lower_mask = jnp.tril(jnp.ones((SPAN, SPAN), dtype=bool))

    def advance(carried, span):
        feats, in_maps, out_maps, steps, decays = span
        cumulated = jnp.cumsum(decays, axis=1)
        scores = jnp.dot(out_maps, in_maps.T, preferred_element_type=jnp.float32)
        gaps = cumulated[:, :, None] - cumulated[:, None, :]
        weights = (scores[None] * jnp.exp(jnp.where(lower_mask, gaps, -jnp.inf)) * steps[:, None, :]).astype(jnp.bfloat16)
        weights = lax.optimization_barrier(weights)
        output_diag = jnp.einsum('hts,shp->thp', weights.astype(jnp.float32), feats.astype(jnp.float32))
        state_low = lax.optimization_barrier(carried.astype(jnp.bfloat16))
        output_carried = jnp.einsum('tn,hpn->thp', out_maps.astype(jnp.float32), state_low.astype(jnp.float32)) * jnp.exp(cumulated).T[:, :, None]
        weighting = jnp.exp(cumulated[:, -1:] - cumulated) * steps
        scaled_in = (weighting.T[:, :, None] * feats.astype(jnp.float32)).astype(jnp.bfloat16)
        scaled_in = lax.optimization_barrier(scaled_in)
        local_state = jnp.einsum('shp,sn->hpn', scaled_in.astype(jnp.float32), in_maps.astype(jnp.float32))
        carried = jnp.exp(cumulated[:, -1])[:, None, None] * carried + local_state
        return (carried, output_diag + output_carried)
    zero_state = jnp.zeros((per_group, HEADDIM, STATE), jnp.float32)
    _, outputs = lax.scan(advance, zero_state, (feat_spans, in_spans, out_spans, step_spans, decay_spans))
    return outputs.reshape(RESPONSE_TOKENS, per_group, HEADDIM)

def reference(features, gates, state_io, step_size, log_decay, conv_feat, conv_state, skip_gain, norm_gain):
    per_group = MIXER_HEADS // GROUPS
    conv_out = causal_conv(features, conv_feat)
    conv_io = causal_conv(state_io, conv_state)
    feat_groups = conv_out.reshape(RESPONSE_TOKENS, GROUPS, per_group, HEADDIM).transpose(1, 0, 2, 3)
    in_groups = conv_io[:, 0].reshape(RESPONSE_TOKENS, GROUPS, STATE).transpose(1, 0, 2)
    out_groups = conv_io[:, 1].reshape(RESPONSE_TOKENS, GROUPS, STATE).transpose(1, 0, 2)
    step_groups = step_size.reshape(GROUPS, per_group, RESPONSE_TOKENS)
    decay_groups = log_decay.reshape(GROUPS, per_group, RESPONSE_TOKENS)
    state_out = lax.map(group_scan, (feat_groups, in_groups, out_groups, step_groups, decay_groups))
    state_out = state_out.transpose(1, 0, 2, 3).reshape(RESPONSE_TOKENS, INNER)
    skip_cols = jnp.repeat(skip_gain, HEADDIM)
    mixed_in = state_out + skip_cols[None, :] * conv_out.astype(jnp.float32)
    gated_out = mixed_in * jax.nn.silu(gates.astype(jnp.float32))
    grouped = gated_out.reshape(RESPONSE_TOKENS, GROUPS, INNER // GROUPS)
    mean_square = lax.optimization_barrier(jnp.mean(grouped * grouped, axis=2, keepdims=True))
    normed = (grouped * lax.rsqrt(mean_square + 1e-05)).reshape(RESPONSE_TOKENS, INNER) * norm_gain[None, :]
    return normed.astype(jnp.bfloat16)
```

```python
import functools

import jax
import jax.numpy as jnp
import numpy as np
from jax import lax
from jax.experimental import pallas as pl
from jax.experimental.pallas import tpu as pltpu
from jax.sharding import PartitionSpec as P

STATE = 256
SPAN = 128
HALO = 16
EPS = 1e-05
F32 = jnp.float32
BF16 = jnp.bfloat16
VMEM_BYTES = 48 * 1024 * 1024


def dot(a, b):
    return jnp.dot(a, b, preferred_element_type=F32)


def silu(v):
    half = 0.5 * v
    return half * jnp.tanh(half) + half


def params(limit=VMEM_BYTES):
    return pltpu.CompilerParams(vmem_limit_bytes=limit)


def shift_table(taps):
    table = np.zeros(((taps - 1) * SPAN, HALO + SPAN), np.float32)
    for k in range(1, taps):
        for t in range(SPAN):
            table[(k - 1) * SPAN + t, HALO + t - k] = 1.0
    return table


def spread_table(heads, head_dim):
    head = np.arange(2 * heads) % heads
    return (head[:, None] == (np.arange(heads * head_dim) // head_dim)[None, :]).astype(np.float32)


def decay_kernel(log_ref, step_ref, col_ref, row_ref, loc_ref, dev_ref, ecum_ref, edev_ref):
    heads, tokens = log_ref.shape
    spans = tokens // SPAN
    r = lax.broadcasted_iota(jnp.int32, (SPAN, SPAN), 0)
    c = lax.broadcasted_iota(jnp.int32, (SPAN, SPAN), 1)
    upper = (r <= c).astype(F32)
    cums = []
    for k in range(spans):
        cums.append(
            jnp.dot(
                log_ref[:, k * SPAN : (k + 1) * SPAN],
                upper,
                precision=lax.Precision.HIGHEST,
                preferred_element_type=F32,
            )
        )
    totals = [cum[:, SPAN - 1 :] for cum in cums]
    before = [jnp.zeros_like(totals[0])]
    for k in range(spans - 1):
        before.append(before[-1] + totals[k])
    after = [jnp.zeros_like(totals[0])]
    for k in range(spans - 1, 0, -1):
        after.insert(0, after[0] + totals[k])

    def put(ref, k, value):
        high = value.astype(BF16).astype(F32)
        both = jnp.concatenate([high, value - high], axis=0)
        ref[k * SPAN : (k + 1) * SPAN, :] = both.T.astype(BF16)

    for k in range(spans):
        cum = cums[k]
        step = step_ref[:, k * SPAN : (k + 1) * SPAN]
        col_ref[k * SPAN : (k + 1) * SPAN, :] = jnp.concatenate([cum, cum], axis=0).T
        row_ref[:, k * SPAN : (k + 1) * SPAN] = cum - jnp.log(step)
        to_end = totals[k] - cum
        put(loc_ref, k, jnp.exp(to_end) * step)
        put(dev_ref, k, jnp.exp(to_end + after[k]) * step)
        put(ecum_ref, k, jnp.exp(cum))
        put(edev_ref, k, jnp.exp(cum + before[k]))


def decay_tables(log_decay, step_size):
    heads, tokens = log_decay.shape
    wide = jax.ShapeDtypeStruct((tokens, 2 * heads), BF16)
    return pl.pallas_call(
        decay_kernel,
        out_shape=(
            jax.ShapeDtypeStruct((tokens, 2 * heads), F32),
            jax.ShapeDtypeStruct((heads, tokens), F32),
            wide,
            wide,
            wide,
            wide,
        ),
        compiler_params=params(),
        name="decays",
        cost_estimate=pl.CostEstimate(flops=10**8, bytes_accessed=3 * 10**6, transcendentals=4 * heads * tokens),
    )(log_decay, step_size)


def conv_rows(x_ref, halo, taps, shifts, store):
    rows = x_ref.shape[0]
    count = taps.shape[0]
    for b in range(rows // SPAN):
        own = x_ref[b * SPAN : (b + 1) * SPAN, :]
        prev = halo if b == 0 else x_ref[b * SPAN - HALO : b * SPAN, :]
        moved = dot(shifts, jnp.concatenate([prev, own], axis=0))
        total = own.astype(F32) * taps[count - 1 : count]
        for k in range(1, count):
            total = total + moved[(k - 1) * SPAN : k * SPAN] * taps[count - 1 - k : count - k]
        store(b, silu(total).astype(BF16))


def front_kernel(
    feat_ref, halo_ref, taps_ref, in_ref, in_halo_ref, in_taps_ref, out_ref, out_halo_ref, out_taps_ref,
    dev_ref, spread_ref, shift_ref, xh_ref, in_map_ref, out_map_ref, state_ref, in_turned, scaled,
):
    shifts = shift_ref[...]

    @pl.when(pl.program_id(0) == 0)
    def _():
        def put_in(b, value):
            in_map_ref[b * SPAN : (b + 1) * SPAN, :] = value
            in_turned[:, b * SPAN : (b + 1) * SPAN] = value.T

        def put_out(b, value):
            out_map_ref[b * SPAN : (b + 1) * SPAN, :] = value

        conv_rows(in_ref, in_halo_ref[...], in_taps_ref[...].astype(F32), shifts, put_in)
        conv_rows(out_ref, out_halo_ref[...], out_taps_ref[...].astype(F32), shifts, put_out)

    spread = spread_ref[...]

    def put_feat(b, value):
        rows = slice(b * SPAN, (b + 1) * SPAN)
        xh_ref[rows, :] = value
        scaled[rows, :] = (value.astype(F32) * dot(dev_ref[rows, :], spread)).astype(BF16)

    conv_rows(feat_ref, halo_ref[...], taps_ref[...].astype(F32), shifts, put_feat)
    state_ref[...] = dot(in_turned[...], scaled[...])


def front(group, width, features, halo, conv_feat, maps, map_halos, map_taps, dev_table, spread, shifts):
    tokens = features.shape[0]
    block = min(512, width)
    steps = width // block
    count = conv_feat.shape[0]
    heads2 = dev_table.shape[1]

    def cols(j):
        return (0, group * steps + j)

    def mine(j):
        return (0, group)

    def same(j):
        return (0, 0)

    map_specs = [
        pl.BlockSpec((tokens, STATE), mine),
        pl.BlockSpec((HALO, STATE), mine),
        pl.BlockSpec((count, STATE), mine),
    ]
    return pl.pallas_call(
        front_kernel,
        grid=(steps,),
        in_specs=[
            pl.BlockSpec((tokens, block), cols),
            pl.BlockSpec((HALO, block), cols),
            pl.BlockSpec((count, block), cols),
            *map_specs,
            *map_specs,
            pl.BlockSpec((tokens, heads2), same),
            pl.BlockSpec((heads2, block), cols),
            pl.BlockSpec(shifts.shape, same),
        ],
        out_specs=[
            pl.BlockSpec((tokens, block), lambda j: (0, j)),
            pl.BlockSpec((tokens, STATE), same),
            pl.BlockSpec((tokens, STATE), same),
            pl.BlockSpec((STATE, block), lambda j: (0, j)),
        ],
        out_shape=(
            jax.ShapeDtypeStruct((tokens, width), BF16),
            jax.ShapeDtypeStruct((tokens, STATE), BF16),
            jax.ShapeDtypeStruct((tokens, STATE), BF16),
            jax.ShapeDtypeStruct((STATE, width), F32),
        ),
        scratch_shapes=[pltpu.VMEM((STATE, tokens), BF16), pltpu.VMEM((tokens, block), BF16)],
        compiler_params=params(),
        name=f"front{group}",
        cost_estimate=pl.CostEstimate(
            flops=8 * 10**9, bytes_accessed=tokens * width * 4, transcendentals=tokens * width
        ),
    )(
        features, halo, conv_feat, maps[0], map_halos[0], map_taps[0], maps[1], map_halos[1], map_taps[1],
        dev_table, spread, shifts,
    )


def span_kernel(
    first_head, xh_ref, in_ref, out_ref, col_ref, row_ref, loc_ref, ecum_ref, spread_ref, skip_ref, halves_ref,
    y_ref, state, scaled,
):
    width = xh_ref.shape[1]
    per_group = row_ref.shape[0]
    head_dim = width // per_group

    @pl.when(pl.program_id(0) == 0)
    def _():
        state[...] = jnp.zeros_like(state)

    in_map = in_ref[...]
    out_map = out_ref[...]
    scores = lax.dot_general(out_map, in_map, (((1,), (1,)), ((), ())), preferred_element_type=F32)
    t = lax.broadcasted_iota(jnp.int32, (SPAN, SPAN), 0)
    s = lax.broadcasted_iota(jnp.int32, (SPAN, SPAN), 1)
    scores = jnp.where(s <= t, scores, 0.0)
    in_turned = in_map.T
    first = halves_ref[0:1, :]
    second = halves_ref[1:2, :]
    block = 256
    for q in range(width // block):
        cols = slice(q * block, (q + 1) * block)
        spread = spread_ref[:, cols]
        feats = xh_ref[:, cols]
        feats32 = feats.astype(F32)
        scaled[:, cols] = (feats32 * dot(loc_ref[...], spread)).astype(BF16)
        ecum = dot(ecum_ref[...], spread)
        pairs = []
        for p in range(block // 128):
            weights = []
            for i in range(2):
                h = (q * block + p * 128) // head_dim + i
                gap = col_ref[:, first_head + h : first_head + h + 1] - row_ref[h : h + 1, :]
                weights.append((scores * jnp.exp(jnp.minimum(gap, 0.0))).astype(BF16))
            pair = feats[:, p * 128 : (p + 1) * 128]
            stacked = jnp.concatenate([pair * first, pair * second], axis=0)
            pairs.append(dot(jnp.concatenate(weights, axis=1), stacked))
        diag = jnp.concatenate(pairs, axis=1)
        held = state[:, cols]
        carried = dot(out_map, held.astype(BF16)) * ecum
        y_ref[:, cols] = diag + carried + skip_ref[:, cols] * feats32
        state[:, cols] = ecum[SPAN - 1 :] * held + dot(in_turned, scaled[:, cols])


def spans_of(group, per_group, xh, in_map, out_map, col, row, loc, ecum, spread, skip_row, halves):
    tokens, width = xh.shape
    heads2 = loc.shape[1]
    return pl.pallas_call(
        functools.partial(span_kernel, group * per_group),
        grid=(tokens // SPAN,),
        in_specs=[
            pl.BlockSpec((SPAN, width), lambda k: (k, 0)),
            pl.BlockSpec((SPAN, STATE), lambda k: (k, 0)),
            pl.BlockSpec((SPAN, STATE), lambda k: (k, 0)),
            pl.BlockSpec((SPAN, heads2), lambda k: (k, 0)),
            pl.BlockSpec((per_group, SPAN), lambda k: (group, k)),
            pl.BlockSpec((SPAN, heads2), lambda k: (k, 0)),
            pl.BlockSpec((SPAN, heads2), lambda k: (k, 0)),
            pl.BlockSpec((heads2, width), lambda k: (0, group)),
            pl.BlockSpec((1, width), lambda k: (0, group)),
            pl.BlockSpec(halves.shape, lambda k: (0, 0)),
        ],
        out_specs=pl.BlockSpec((SPAN, width), lambda k: (k, 0)),
        out_shape=jax.ShapeDtypeStruct((tokens, width), F32),
        scratch_shapes=[pltpu.VMEM((STATE, width), F32), pltpu.VMEM((SPAN, width), BF16)],
        compiler_params=params(),
        name=f"spans{group}",
        cost_estimate=pl.CostEstimate(
            flops=8 * 10**9, bytes_accessed=tokens * width * 6, transcendentals=tokens * per_group * SPAN
        ),
    )(xh, in_map, out_map, col, row, loc, ecum, spread, skip_row, halves)


def back_kernel(
    blk_ref, y_ref, out_ref, edev_ref, spread_ref, low_ref, high_ref, gate_ref, gain_ref, o_ref, gated
):
    rows, width = y_ref.shape
    out_map = out_ref[...]
    edev = edev_ref[...]
    block = 256
    half = low_ref.shape[1]
    squares = jnp.zeros((rows, block), F32)
    for q in range(width // block):
        cols = slice(q * block, (q + 1) * block)
        if q * block < half:
            state = low_ref[:, cols]
        else:
            state = high_ref[:, q * block - half : (q + 1) * block - half]
        carried = dot(out_map, state) * dot(edev, spread_ref[:, cols])
        value = (y_ref[:, cols] + carried) * silu(gate_ref[:, cols].astype(F32))
        squares = squares + value * value
        gated[:, cols] = value
    mean = jnp.sum(squares, axis=1, keepdims=True) * (1.0 / width)
    scale = lax.rsqrt(mean + EPS)
    for q in range(width // block):
        cols = slice(q * block, (q + 1) * block)
        o_ref[:, cols] = (gated[:, cols] * scale * gain_ref[:, cols]).astype(BF16)


def back(group, blk, rows, y, out_map, edev, spread, low, high, gates, gain_row):
    width = y.shape[1]
    heads2 = edev.shape[1]
    tile = 128
    steps = rows // tile

    def at(i, blk):
        return (blk[0] * steps + i, 0)

    grid_spec = pltpu.PrefetchScalarGridSpec(
        num_scalar_prefetch=1,
        grid=(steps,),
        in_specs=[
            pl.BlockSpec((tile, width), at),
            pl.BlockSpec((tile, STATE), at),
            pl.BlockSpec((tile, heads2), at),
            pl.BlockSpec((heads2, width), lambda i, blk: (0, group)),
            pl.BlockSpec((STATE, low.shape[1]), lambda i, blk: (0, 0)),
            pl.BlockSpec((STATE, high.shape[1]), lambda i, blk: (0, 0)),
            pl.BlockSpec((tile, width), lambda i, blk: (blk[0] * steps + i, group)),
            pl.BlockSpec((1, width), lambda i, blk: (0, group)),
        ],
        out_specs=pl.BlockSpec((tile, width), lambda i, blk: (i, 0)),
        scratch_shapes=[pltpu.VMEM((tile, width), F32)],
    )
    return pl.pallas_call(
        back_kernel,
        grid_spec=grid_spec,
        out_shape=jax.ShapeDtypeStruct((rows, width), BF16),
        compiler_params=params(),
        name=f"back{group}",
        cost_estimate=pl.CostEstimate(
            flops=10**9, bytes_accessed=rows * width * 8 + 3 * STATE * width, transcendentals=rows * width
        ),
    )(blk, y, out_map, edev, spread, low, high, gates, gain_row)


def shifted(value, pairs, steps):
    return lax.ppermute(
        value,
        "ctx",
        [(2 * q + y, 2 * (q + steps) + y) for q in range(pairs - steps) for y in range(2)],
    )


def swapped(value, pairs):
    return lax.ppermute(value, "ctx", [(2 * q + y, 2 * q + 1 - y) for q in range(pairs) for y in range(2)])


def incoming(state, own_decay, pair_decay, odd, pairs):
    half = state.shape[1] // 2
    halves = (state[:, :half], state[:, half:])
    keep = jnp.where(odd, halves[1], halves[0])
    got = swapped(jnp.where(odd, halves[0], halves[1]).astype(BF16), pairs).astype(F32)
    keep_own = own_decay
    keep_partner, keep_before = pair_decay
    even_state = jnp.where(odd, got, keep)
    total = jnp.where(odd, keep_own * got + keep, keep_partner * keep + got)
    total_decay = keep_own * keep_partner
    carried = shifted(total.astype(BF16), pairs, 1).astype(F32)
    decay = keep_before
    reach = 1
    while reach < pairs - 1:
        inclusive = total + total_decay * carried
        far = shifted(inclusive.astype(BF16), pairs, reach + 1).astype(F32)
        far_decay = shifted(total_decay * decay, pairs, reach + 1)
        carried = carried + decay * far
        decay = decay * far_decay
        reach = 2 * reach + 1
    return carried, even_state


def shards(
    features, gates, state_io, step_size, log_decay, conv_feat, conv_state, skip_gain, norm_gain
):
    tokens, channels = features.shape
    heads = step_size.shape[0]
    head_dim = channels // heads
    map_cols = state_io.shape[2]
    groups = map_cols // STATE
    per_group = heads // groups
    width = channels // groups
    half = width // 2
    count = conv_feat.shape[0]
    rim = count - 1
    ctx_size = lax.axis_size("ctx")
    head_size = lax.axis_size("head")
    pairs = ctx_size // 2
    rows = tokens // head_size
    me = lax.axis_index("head")
    odd = lax.axis_index("ctx") % 2 == 1

    tail = jnp.concatenate(
        [features[tokens - rim :], state_io[tokens - rim :, 0], state_io[tokens - rim :, 1]], axis=1
    )
    before = lax.ppermute(tail, "ctx", [(i, i + 1) for i in range(ctx_size - 1)])
    maps = (state_io[:, 0], state_io[:, 1])
    map_taps = (conv_state[:, 0], conv_state[:, 1])
    spread = jnp.asarray(spread_table(heads, head_dim), BF16)
    shifts = jnp.asarray(shift_table(count), BF16)
    halves = jnp.asarray(np.arange(128)[None, :] // head_dim == np.arange(2)[:, None], BF16)
    col, row, loc, dev, ecum, edev = decay_tables(log_decay, step_size)
    skip_row = jnp.repeat(skip_gain, head_dim)[None]
    gain_row = norm_gain[None]

    own_decay = jnp.repeat(jnp.exp(jnp.sum(log_decay, axis=1)), head_dim)[None]
    kept = [slice(g * width, g * width + half) for g in range(groups)]
    rest = [slice(g * width + half, (g + 1) * width) for g in range(groups)]
    partner_decay = swapped(own_decay, pairs)
    before_decay = shifted(own_decay * partner_decay, pairs, 1)

    def kept_half(value, g):
        return jnp.where(odd, value[:, rest[g]], value[:, kept[g]])

    before = jnp.pad(before, ((HALO - rim, 0), (0, 0)))
    halo = before[:, :channels]
    map_halos = (before[:, channels : channels + map_cols], before[:, channels + map_cols :])

    fronts = [
        front(g, width, features, halo, conv_feat, maps, map_halos, map_taps, dev, spread, shifts)
        for g in range(groups)
    ]
    states = []
    for g in range(groups):
        state = fronts[g][3]
        carried, even_state = incoming(
            state,
            kept_half(own_decay, g),
            (kept_half(partner_decay, g), kept_half(before_decay, g)),
            odd,
            pairs,
        )
        through = kept_half(own_decay, g) * carried + even_state
        mine = jnp.where(odd, kept_half(partner_decay, g) * carried + even_state, carried)
        other = swapped(jnp.where(odd, carried, through).astype(BF16), pairs)
        mine = mine.astype(BF16)
        states.append((jnp.where(odd, other, mine), jnp.where(odd, mine, other)))
    locals_ = [
        spans_of(
            g, per_group, fronts[g][0], fronts[g][1], fronts[g][2], col, row, loc, ecum, spread, skip_row, halves
        )
        for g in range(groups)
    ]
    order = list(range(head_size - 1, -1, -1))
    out = jnp.zeros((rows, channels * head_size), BF16)
    pieces = []
    for cross in (True, False):
        for g in range(groups):
            for r in order:
                if (r >= 2) != cross:
                    continue
                blk = (me ^ r).astype(jnp.int32)
                made = back(
                    g, blk[None], rows, locals_[g], fronts[g][2], edev, spread, states[g][0], states[g][1],
                    gates, gain_row,
                )
                if r:
                    made = lax.ppermute(made, "head", [(i, i ^ r) for i in range(head_size)])
                pieces.append((made, blk * channels + g * width))
    for made, start in pieces:
        out = lax.dynamic_update_slice(out, made, (jnp.int32(0), start))
    return out


def solution(mesh):
    in_specs = (
        P("ctx", "head"),
        P("ctx", "head"),
        P("ctx", None, "head"),
        P("head", "ctx"),
        P("head", "ctx"),
        P(None, "head"),
        P(None, None, "head"),
        P("head"),
        P("head"),
    )
    out_specs = P(("ctx", "head"), None)
    return jax.shard_map(shards, mesh=mesh, in_specs=in_specs, out_specs=out_specs, check_vma=False)
```

```python
import functools

import jax
import jax.numpy as jnp
import numpy as np
from jax import lax
from jax.experimental import pallas as pl
from jax.experimental.pallas import tpu as pltpu
from jax.sharding import PartitionSpec as P

STATE = 256
SPAN = 128
HALO = 16
EPS = 1e-05
F32 = jnp.float32
BF16 = jnp.bfloat16
VMEM_BYTES = 60 * 1024 * 1024
MSG = STATE + 16
KEPT = STATE + 8


def dot(a, b):
    return jnp.dot(a, b, preferred_element_type=F32)


def silu(v):
    half = 0.5 * v
    return half * jnp.tanh(half) + half


def params(limit=VMEM_BYTES):
    return pltpu.CompilerParams(vmem_limit_bytes=limit)


def shift_table(taps):
    table = np.zeros(((taps - 1) * SPAN, HALO + SPAN), np.float32)
    for k in range(1, taps):
        for t in range(SPAN):
            table[(k - 1) * SPAN + t, HALO + t - k] = 1.0
    return table


def spread_table(heads, head_dim):
    head = np.arange(2 * heads) % heads
    return (head[:, None] == (np.arange(heads * head_dim) // head_dim)[None, :]).astype(np.float32)


def decay_kernel(log_ref, step_ref, col_ref, row_ref, loc_ref, dev_ref, ecum_ref, edev_ref):
    heads, tokens = log_ref.shape
    spans = tokens // SPAN
    r = lax.broadcasted_iota(jnp.int32, (SPAN, SPAN), 0)
    c = lax.broadcasted_iota(jnp.int32, (SPAN, SPAN), 1)
    upper = (r <= c).astype(F32)
    cums = []
    for k in range(spans):
        cums.append(
            jnp.dot(
                log_ref[:, k * SPAN : (k + 1) * SPAN],
                upper,
                precision=lax.Precision.HIGHEST,
                preferred_element_type=F32,
            )
        )
    totals = [cum[:, SPAN - 1 :] for cum in cums]
    before = [jnp.zeros_like(totals[0])]
    for k in range(spans - 1):
        before.append(before[-1] + totals[k])
    after = [jnp.zeros_like(totals[0])]
    for k in range(spans - 1, 0, -1):
        after.insert(0, after[0] + totals[k])

    def put(ref, k, value):
        high = value.astype(BF16).astype(F32)
        both = jnp.concatenate([high, value - high], axis=0)
        ref[k * SPAN : (k + 1) * SPAN, :] = both.T.astype(BF16)

    for k in range(spans):
        cum = cums[k]
        step = step_ref[:, k * SPAN : (k + 1) * SPAN]
        col_ref[k * SPAN : (k + 1) * SPAN, :] = jnp.concatenate([cum, cum], axis=0).T
        row_ref[:, k * SPAN : (k + 1) * SPAN] = cum - jnp.log(step)
        to_end = totals[k] - cum
        put(loc_ref, k, jnp.exp(to_end) * step)
        put(dev_ref, k, jnp.exp(to_end + after[k]) * step)
        put(ecum_ref, k, jnp.exp(cum))
        put(edev_ref, k, jnp.exp(cum + before[k]))


def behind(count):
    return [pl.BlockSpec(memory_space=pl.ANY)] * count


def decay_tables(log_decay, step_size):
    heads, tokens = log_decay.shape
    wide = jax.ShapeDtypeStruct((tokens, 2 * heads), BF16)
    return pl.pallas_call(
        decay_kernel,
        out_shape=(
            jax.ShapeDtypeStruct((tokens, 2 * heads), F32),
            jax.ShapeDtypeStruct((heads, tokens), F32),
            wide,
            wide,
            wide,
            wide,
        ),
        compiler_params=params(),
        name="decays",
        cost_estimate=pl.CostEstimate(flops=10**8, bytes_accessed=3 * 10**6, transcendentals=4 * heads * tokens),
    )(log_decay, step_size)


def conv_rows(read, rows, halo, taps, shifts, store):
    count = taps.shape[0]
    for b in range(rows // SPAN):
        own = read(b * SPAN, (b + 1) * SPAN)
        prev = halo if b == 0 else read(b * SPAN - HALO, b * SPAN)
        moved = dot(shifts, jnp.concatenate([prev, own], axis=0))
        total = own.astype(F32) * taps[count - 1 : count]
        for k in range(1, count):
            total = total + moved[(k - 1) * SPAN : k * SPAN] * taps[count - 1 - k : count - k]
        store(b, silu(total).astype(BF16))


def read_state(ref):
    if ref.dtype == F32:
        return ref[:STATE, :], ref[STATE : STATE + 1, :]
    tail = ref[STATE:MSG, :].astype(F32)
    return ref[:STATE, :].astype(F32), tail[0:1] + tail[8:9]


def write_kept(ref, value, decay):
    ref[:STATE, :] = value
    ref[STATE:KEPT, :] = jnp.broadcast_to(decay, (KEPT - STATE, decay.shape[1]))


def write_sent(ref, value, decay):
    ref[:STATE, :] = value.astype(BF16)
    high = decay.astype(BF16).astype(F32)
    shape = (8, decay.shape[1])
    rows = jnp.concatenate([jnp.broadcast_to(high, shape), jnp.broadcast_to(decay - high, shape)], axis=0)
    ref[STATE:MSG, :] = rows.astype(BF16)


def front_kernel(with_maps, order, blocks, odd_ref, feat_ref, halo_ref, taps_ref, dev_ref, edev_ref, spread_ref, shift_ref, *refs):
    if with_maps:
        io_ref, io_halo_ref, io_taps_ref, *refs = refs
    else:
        in_ref, *refs = refs
    refs = refs[order:]
    if with_maps:
        xh_ref, sent_ref, kept_ref, in_map_ref, out_map_ref, in_turned, scaled = refs
    else:
        xh_ref, sent_ref, kept_ref, in_turned, scaled = refs
    tokens = feat_ref.shape[0]
    shifts = shift_ref[...]
    j = pl.program_id(0)

    @pl.when(j == 0)
    def _():
        if with_maps:

            def put_in(b, value):
                in_map_ref[b * SPAN : (b + 1) * SPAN, :] = value
                in_turned[:, b * SPAN : (b + 1) * SPAN] = value.T

            def put_out(b, value):
                out_map_ref[b * SPAN : (b + 1) * SPAN, :] = value

            for i, put in ((0, put_in), (1, put_out)):
                conv_rows(
                    lambda lo, hi: io_ref[lo:hi, i, :], tokens, io_halo_ref[:, i, :],
                    io_taps_ref[:, i, :].astype(F32), shifts, put,
                )
        else:
            for b in range(tokens // SPAN):
                in_turned[:, b * SPAN : (b + 1) * SPAN] = in_ref[b * SPAN : (b + 1) * SPAN, :].T

    spread = spread_ref[...]

    def put_feat(b, value):
        rows = slice(b * SPAN, (b + 1) * SPAN)
        xh_ref[rows, :] = value
        scaled[rows, :] = (value.astype(F32) * dot(dev_ref[rows, :], spread)).astype(BF16)

    conv_rows(
        lambda lo, hi: feat_ref[lo:hi, :], tokens, halo_ref[...], taps_ref[...].astype(F32), shifts, put_feat
    )
    state = dot(in_turned[...], scaled[...])
    decay = dot(edev_ref[...], spread)[15:16]

    @pl.when(j < blocks)
    def _():
        write_sent(sent_ref, state, decay)

    @pl.when(j >= blocks)
    def _():
        write_kept(kept_ref, state, decay)


def front(chunk, group, odd, features, halo, conv_feat, dev, edev, spread, shifts, io, in_map, after):
    tokens = features.shape[0]
    start, width = chunk
    half = width // 2
    block = min(512, half)
    blocks = half // block
    base = start // block
    count = conv_feat.shape[0]
    heads2 = dev.shape[1]
    with_maps = io is not None

    def place(j, odd):
        sending = (j < blocks).astype(jnp.int32)
        which = sending * (1 - odd[0]) + (1 - sending) * odd[0]
        return which * blocks + j - (1 - sending) * blocks

    def cols(j, odd):
        return (0, base + place(j, odd))

    def same(j, odd):
        return (0, 0)

    if with_maps:
        extra_specs = [
            pl.BlockSpec((tokens, 2, STATE), lambda j, odd: (0, 0, group)),
            pl.BlockSpec((HALO, 2, STATE), lambda j, odd: (0, 0, group)),
            pl.BlockSpec((count, 2, STATE), lambda j, odd: (0, 0, group)),
        ]
        extra = io
        map_specs = [pl.BlockSpec((tokens, STATE), same)] * 2
        map_shapes = [jax.ShapeDtypeStruct((tokens, STATE), BF16)] * 2
    else:
        extra_specs = [pl.BlockSpec((tokens, STATE), same)]
        extra = (in_map,)
        map_specs = []
        map_shapes = []
    return pl.pallas_call(
        functools.partial(front_kernel, with_maps, len(after), blocks),
        grid_spec=pltpu.PrefetchScalarGridSpec(
            num_scalar_prefetch=1,
            grid=(2 * blocks,),
            in_specs=[
                pl.BlockSpec((tokens, block), cols),
                pl.BlockSpec((HALO, block), cols),
                pl.BlockSpec((count, block), cols),
                pl.BlockSpec((tokens, heads2), same),
                pl.BlockSpec((16, heads2), lambda j, odd: (tokens // 16 - 1, 0)),
                pl.BlockSpec((heads2, block), cols),
                pl.BlockSpec(shifts.shape, same),
                *extra_specs,
                *behind(len(after)),
            ],
            out_specs=[
                pl.BlockSpec((tokens, block), lambda j, odd: (0, place(j, odd))),
                pl.BlockSpec((MSG, block), lambda j, odd: (0, jnp.minimum(j, blocks - 1))),
                pl.BlockSpec((KEPT, block), lambda j, odd: (0, jnp.maximum(j - blocks, 0))),
                *map_specs,
            ],
            scratch_shapes=[pltpu.VMEM((STATE, tokens), BF16), pltpu.VMEM((tokens, block), BF16)],
        ),
        out_shape=[
            jax.ShapeDtypeStruct((tokens, width), BF16),
            jax.ShapeDtypeStruct((MSG, half), BF16),
            jax.ShapeDtypeStruct((KEPT, half), F32),
            *map_shapes,
        ],
        compiler_params=params(),
        name="front",
        cost_estimate=pl.CostEstimate(flops=6 * 10**9, bytes_accessed=tokens * width * 4, transcendentals=tokens * width),
    )(odd, features, halo, conv_feat, dev, edev, spread, shifts, *extra, *after)


def span_kernel(
    first_head, order, xh_ref, in_ref, out_ref, col_ref, row_ref, loc_ref, ecum_ref, spread_ref, skip_ref, halves_ref,
    *refs,
):
    y_ref, state, scaled = refs[order:]
    width = xh_ref.shape[1]
    head_dim = width // row_ref.shape[0]

    @pl.when(pl.program_id(0) == 0)
    def _():
        state[...] = jnp.zeros_like(state)

    in_map = in_ref[...]
    out_map = out_ref[...]
    scores = lax.dot_general(out_map, in_map, (((1,), (1,)), ((), ())), preferred_element_type=F32)
    t = lax.broadcasted_iota(jnp.int32, (SPAN, SPAN), 0)
    s = lax.broadcasted_iota(jnp.int32, (SPAN, SPAN), 1)
    scores = jnp.where(s <= t, scores, 0.0)
    in_turned = in_map.T
    first = halves_ref[0:1, :]
    second = halves_ref[1:2, :]
    block = 256
    for q in range(width // block):
        cols = slice(q * block, (q + 1) * block)
        spread = spread_ref[:, cols]
        feats = xh_ref[:, cols]
        feats32 = feats.astype(F32)
        scaled[:, cols] = (feats32 * dot(loc_ref[...], spread)).astype(BF16)
        ecum = dot(ecum_ref[...], spread)
        pairs = []
        for p in range(block // 128):
            weights = []
            for i in range(2):
                h = (q * block + p * 128) // head_dim + i
                gap = col_ref[:, first_head + h : first_head + h + 1] - row_ref[h : h + 1, :]
                weights.append((scores * jnp.exp(jnp.minimum(gap, 0.0))).astype(BF16))
            pair = feats[:, p * 128 : (p + 1) * 128]
            stacked = jnp.concatenate([pair * first, pair * second], axis=0)
            pairs.append(dot(jnp.concatenate(weights, axis=1), stacked))
        diag = jnp.concatenate(pairs, axis=1)
        held = state[:, cols]
        carried = dot(out_map, held.astype(BF16)) * ecum
        y_ref[:, cols] = diag + carried + skip_ref[:, cols] * feats32
        state[:, cols] = ecum[SPAN - 1 :] * held + dot(in_turned, scaled[:, cols])


def spans_of(chunk, head_dim, xh, in_map, out_map, col, row, loc, ecum, spread, skip_row, halves, after):
    tokens, width = xh.shape
    index = chunk[0] // width
    some = width // head_dim
    heads2 = loc.shape[1]
    return pl.pallas_call(
        functools.partial(span_kernel, index * some, len(after)),
        grid=(tokens // SPAN,),
        in_specs=[
            pl.BlockSpec((SPAN, width), lambda k: (k, 0)),
            pl.BlockSpec((SPAN, STATE), lambda k: (k, 0)),
            pl.BlockSpec((SPAN, STATE), lambda k: (k, 0)),
            pl.BlockSpec((SPAN, heads2), lambda k: (k, 0)),
            pl.BlockSpec((some, SPAN), lambda k: (index, k)),
            pl.BlockSpec((SPAN, heads2), lambda k: (k, 0)),
            pl.BlockSpec((SPAN, heads2), lambda k: (k, 0)),
            pl.BlockSpec((heads2, width), lambda k: (0, index)),
            pl.BlockSpec((1, width), lambda k: (0, index)),
            pl.BlockSpec(halves.shape, lambda k: (0, 0)),
            *behind(len(after)),
        ],
        out_specs=pl.BlockSpec((SPAN, width), lambda k: (k, 0)),
        out_shape=jax.ShapeDtypeStruct((tokens, width), F32),
        scratch_shapes=[pltpu.VMEM((STATE, width), F32), pltpu.VMEM((SPAN, width), BF16)],
        compiler_params=params(),
        name="spans",
        cost_estimate=pl.CostEstimate(
            flops=8 * 10**9, bytes_accessed=tokens * width * 6, transcendentals=tokens * some * SPAN
        ),
    )(xh, in_map, out_map, col, row, loc, ecum, spread, skip_row, halves, *after)


def pair_kernel(odd_ref, kept_ref, got_ref, *refs):
    total_ref, sent_ref = refs[-2:]
    kept, kept_decay = read_state(kept_ref)
    got, got_decay = read_state(got_ref)

    def put(first, second, decay):
        total = decay * first + second
        write_kept(total_ref, total, kept_decay * got_decay)
        write_sent(sent_ref, total, kept_decay * got_decay)

    @pl.when(odd_ref[0] == 0)
    def _():
        put(kept, got, got_decay)

    @pl.when(odd_ref[0] == 1)
    def _():
        put(got, kept, kept_decay)


def inclusive_kernel(total_ref, before_ref, *refs):
    sent_ref = refs[-1]
    total, decay = read_state(total_ref)
    before, before_decay = read_state(before_ref)
    write_sent(sent_ref, total + decay * before, decay * before_decay)


def extend_kernel(before_ref, far_ref, *refs):
    before, decay = read_state(before_ref)
    far, far_decay = read_state(far_ref)
    write_kept(refs[-1], before + decay * far, decay * far_decay)


def last_kernel(odd_ref, before_ref, far_ref, kept_ref, got_ref, *refs):
    mine_ref, sent_ref = refs[-2:]
    before, before_decay = read_state(before_ref)
    far, _ = read_state(far_ref)
    carried = before + before_decay * far

    @pl.when(odd_ref[0] == 0)
    def _():
        kept, decay = read_state(kept_ref)
        mine_ref[...] = carried.astype(BF16)
        sent_ref[...] = (decay * carried + kept).astype(BF16)

    @pl.when(odd_ref[0] == 1)
    def _():
        got, decay = read_state(got_ref)
        mine_ref[...] = (decay * carried + got).astype(BF16)
        sent_ref[...] = carried.astype(BF16)


def join(kernel, name, odd, operands, outs, after):
    width = operands[0].shape[1]
    shapes = {
        "kept": jax.ShapeDtypeStruct((KEPT, width), F32),
        "sent": jax.ShapeDtypeStruct((MSG, width), BF16),
        "state": jax.ShapeDtypeStruct((STATE, width), BF16),
    }
    scalars = [] if odd is None else [odd]
    return pl.pallas_call(
        kernel,
        in_specs=[pl.BlockSpec(memory_space=pltpu.SMEM)] * len(scalars)
        + [pl.BlockSpec(memory_space=pltpu.VMEM)] * len(operands)
        + behind(len(after)),
        out_specs=[pl.BlockSpec(memory_space=pltpu.VMEM)] * len(outs),
        out_shape=[shapes[out] for out in outs],
        compiler_params=params(),
        name=name,
        cost_estimate=pl.CostEstimate(flops=10**9, bytes_accessed=STATE * width * 12, transcendentals=0),
    )(*scalars, *operands, *after)


def back_kernel(mode, count, order, place_ref, out_ref, edev_ref, *refs):
    chunks = [refs[6 * i : 6 * i + 6] for i in range(count)]
    refs = refs[6 * count :]
    if mode == "rest":
        squares_ref, *refs = refs
    refs = refs[order:]
    if mode == "first":
        o_ref, squares_ref = refs
    else:
        o_ref, gated = refs
    out_map = out_ref[...]
    edev = edev_ref[...]
    rows = out_map.shape[0]
    block = 256
    odd = place_ref[1] == 1
    squares = squares_ref[...] if mode == "rest" else jnp.zeros((rows, 128), F32)
    at = 0
    gains = []
    for y_ref, mine_ref, other_ref, spread_ref, gate_ref, gain_ref in chunks:
        half = mine_ref.shape[1]
        for q in range(2 * half // block):
            cols = slice(q * block, (q + 1) * block)
            inner = slice(q * block % half, q * block % half + block)
            mine = mine_ref[:, inner]
            other = other_ref[:, inner]
            state = jnp.where(odd, other, mine) if q * block < half else jnp.where(odd, mine, other)
            carried = dot(out_map, state) * dot(edev, spread_ref[:, cols])
            value = (y_ref[:, cols] + carried) * silu(gate_ref[:, cols].astype(F32))
            square = value * value
            squares = squares + square[:, :128] + square[:, 128:]
            if mode == "first":
                o_ref[:, cols] = (value * gain_ref[:, cols]).astype(BF16)
            else:
                gated[:, at : at + block] = value * gain_ref[:, cols]
            at += block
    if mode == "first":
        squares_ref[...] = squares
        return
    width = at if mode == "whole" else 2 * at
    mean = jnp.sum(squares, axis=1, keepdims=True) * (1.0 / width)
    scale = lax.rsqrt(mean + EPS)
    for q in range(at // block):
        cols = slice(q * block, (q + 1) * block)
        o_ref[:, cols] = (gated[:, cols] * scale).astype(BF16)
    if mode == "rest":
        high = scale.astype(BF16).astype(F32)
        lane = lax.broadcasted_iota(jnp.int32, (rows, 128), 1)
        o_ref[:, at:] = jnp.where(lane < 64, high, scale - high).astype(BF16)


def back(mode, place, rows, chunks, out_map, edev, spread, gates, gain_row, squares, after, own=None):
    heads2 = edev.shape[1]
    tile = 128
    steps = rows // tile

    def at(i, place):
        return (place[0] * steps + i, 0)

    specs = [pl.BlockSpec((tile, STATE), at), pl.BlockSpec((tile, heads2), at)]
    operands = [out_map, edev]
    total = 0
    for (start, width), y, mine, other in chunks:
        index = start // width
        half = width // 2
        total += width
        specs += [
            pl.BlockSpec((tile, width), at),
            pl.BlockSpec((STATE, half), lambda i, place: (0, 0)),
            pl.BlockSpec((STATE, half), lambda i, place: (0, 0)),
            pl.BlockSpec((heads2, width), lambda i, place, index=index: (0, index)),
            pl.BlockSpec((tile, width), lambda i, place, index=index: (place[0] * steps + i, index)),
            pl.BlockSpec((1, width), lambda i, place, index=index: (0, index)),
        ]
        operands += [y, mine, other, spread, gates, gain_row]
    if mode == "rest":
        specs.append(pl.BlockSpec((tile, 128), lambda i, place: (i, 0)))
        operands.append(squares)
    aliases = {}
    if own is not None and own[2] is not None:
        after = [own[2], *after]
        aliases = {1 + len(operands): 0}
    specs += behind(len(after))
    operands += after
    scratch = [pltpu.VMEM((tile, total), F32)]
    if mode == "first":
        out_specs = [pl.BlockSpec((tile, total), lambda i, place: (i, 0)), pl.BlockSpec((tile, 128), lambda i, place: (i, 0))]
        out_shape = [jax.ShapeDtypeStruct((rows, total), BF16), jax.ShapeDtypeStruct((rows, 128), F32)]
        scratch = []
    elif mode == "rest":
        out_specs = pl.BlockSpec((tile, total + 128), lambda i, place: (i, 0))
        out_shape = jax.ShapeDtypeStruct((rows, total + 128), BF16)
    elif own is None:
        out_specs = pl.BlockSpec((tile, total), lambda i, place: (i, 0))
        out_shape = jax.ShapeDtypeStruct((rows, total), BF16)
    else:
        group, groups, _ = own
        head_size = gates.shape[0] // rows
        out_specs = pl.BlockSpec((tile, total), lambda i, place: (i, place[0] * groups + group))
        out_shape = jax.ShapeDtypeStruct((rows, groups * total * head_size), BF16)
    return pl.pallas_call(
        functools.partial(back_kernel, mode, len(chunks), len(after)),
        grid_spec=pltpu.PrefetchScalarGridSpec(
            num_scalar_prefetch=1, grid=(steps,), in_specs=specs, out_specs=out_specs, scratch_shapes=scratch
        ),
        out_shape=out_shape,
        input_output_aliases=aliases,
        compiler_params=params(),
        name=f"back_{mode}",
        cost_estimate=pl.CostEstimate(
            flops=10**9, bytes_accessed=rows * total * 8 + 3 * STATE * total, transcendentals=rows * total
        ),
    )(place, *operands)


def put_kernel(split, place_ref, *refs):
    o_ref = refs[-1]
    if split:
        first_ref, rest_ref = refs[:2]
        half = first_ref.shape[1]
        scale = (rest_ref[:, half : half + 1].astype(F32) + rest_ref[:, half + 64 : half + 65].astype(F32))
        o_ref[:, :half] = (first_ref[...].astype(F32) * scale).astype(BF16)
        o_ref[:, half:] = rest_ref[:, :half]
    else:
        o_ref[...] = refs[0][...]


def put(result, pieces, source, group, groups, after):
    rows = result.shape[0]
    split = len(pieces) == 2
    width = 2 * pieces[0].shape[1] if split else pieces[0].shape[1]
    tile = 64
    return pl.pallas_call(
        functools.partial(put_kernel, split),
        grid_spec=pltpu.PrefetchScalarGridSpec(
            num_scalar_prefetch=1,
            grid=(rows // tile,),
            in_specs=[pl.BlockSpec((tile, piece.shape[1]), lambda i, place: (i, 0)) for piece in pieces]
            + behind(1 + len(after)),
            out_specs=pl.BlockSpec((tile, width), lambda i, place: (i, place[0] * groups + group)),
        ),
        out_shape=jax.ShapeDtypeStruct(result.shape, BF16),
        input_output_aliases={1 + len(pieces): 0},
        compiler_params=params(),
        name="put",
        cost_estimate=pl.CostEstimate(flops=10**7, bytes_accessed=rows * width * 4, transcendentals=0),
    )(source, *pieces, result, *after)


def shifted(value, pairs, steps):
    return lax.ppermute(
        value,
        "ctx",
        [(2 * q + y, 2 * (q + steps) + y) for q in range(pairs - steps) for y in range(2)],
    )


def swapped(value, pairs):
    return lax.ppermute(value, "ctx", [(2 * q + y, 2 * q + 1 - y) for q in range(pairs) for y in range(2)])


class Line:
    def __init__(self):
        self.last = []

    def run(self, make, *args, **kwargs):
        made = make(*args, after=self.last, **kwargs)
        self.last = [made[-1] if isinstance(made, (list, tuple)) else made]
        return made


class Exchange:
    def __init__(self, line, odd, pairs, sent, kept):
        self.line = line
        self.odd = odd
        self.pairs = pairs
        self.kept = kept
        self.got = swapped(sent, pairs)

    def pair(self):
        self.total, sent = self.line.run(
            join, pair_kernel, "pair", self.odd, [self.kept, self.got], ["kept", "sent"]
        )
        self.before = shifted(sent, self.pairs, 1)
        self.reach = 1

    def double(self):
        (sent,) = self.line.run(join, inclusive_kernel, "inclusive", None, [self.total, self.before], ["sent"])
        self.far = shifted(sent, self.pairs, self.reach + 1)
        self.reach = 2 * self.reach + 1

    def extend(self):
        while self.reach < self.pairs - 1:
            (self.before,) = self.line.run(join, extend_kernel, "extend", None, [self.before, self.far], ["kept"])
            self.double()

    def finish(self):
        self.extend()
        self.mine, sent = self.line.run(
            join, last_kernel, "last", self.odd, [self.before, self.far, self.kept, self.got], ["state", "state"]
        )
        self.other = swapped(sent, self.pairs)


def shards(
    features, gates, state_io, step_size, log_decay, conv_feat, conv_state, skip_gain, norm_gain
):
    tokens, channels = features.shape
    heads = step_size.shape[0]
    head_dim = channels // heads
    groups = state_io.shape[2] // STATE
    group_width = channels // groups
    width = group_width // 2
    count = conv_feat.shape[0]
    rim = count - 1
    ctx_size = lax.axis_size("ctx")
    head_size = lax.axis_size("head")
    pairs = ctx_size // 2
    rows = tokens // head_size
    me = lax.axis_index("head").astype(jnp.int32)
    odd = (lax.axis_index("ctx").astype(jnp.int32) % 2)[None]

    onward = [(i, i + 1) for i in range(ctx_size - 1)]
    pad = HALO - rim
    halo = jnp.pad(lax.ppermute(features[tokens - rim :], "ctx", onward), ((pad, 0), (0, 0)))
    io_halo = jnp.pad(lax.ppermute(state_io[tokens - rim :], "ctx", onward), ((pad, 0), (0, 0), (0, 0)))
    spread = jnp.asarray(spread_table(heads, head_dim), BF16)
    shifts = jnp.asarray(shift_table(count), BF16)
    halves = jnp.asarray(np.arange(128)[None, :] // head_dim == np.arange(2)[:, None], BF16)
    col, row, loc, dev, ecum, edev = decay_tables(log_decay, step_size)
    skip_row = jnp.repeat(skip_gain, head_dim)[None]
    gain_row = norm_gain[None]

    line = Line()
    chunks = [(c * width, width) for c in range(2 * groups)]
    fronts = {}
    maps = {}
    exchanges = {}
    ys = {}

    def run_front(c):
        g = c // 2
        io = (state_io, io_halo, conv_state) if c % 2 == 0 else None
        in_map = None if c % 2 == 0 else maps[g][0]
        made = line.run(
            front, chunks[c], g, odd, features, halo, conv_feat, dev, edev, spread, shifts, io, in_map
        )
        if c % 2 == 0:
            maps[g] = made[3:]
        fronts[c] = made[0]
        line.last = [made[2]]
        exchanges[c] = Exchange(line, odd, pairs, made[1], made[2])

    def run_spans(c):
        g = c // 2
        ys[c] = line.run(
            spans_of, chunks[c], head_dim, fronts[c], *maps[g], col, row, loc, ecum, spread, skip_row, halves
        )

    def part(c):
        return (chunks[c], ys[c], exchanges[c].mine, exchanges[c].other)

    def place_of(r):
        return jnp.concatenate([(me ^ r)[None], odd])

    partners = list(range(head_size - 1, 1, -1))
    squares = {}
    pieces = {}

    def ship(piece, r):
        return lax.ppermute(piece, "head", [(i, i ^ r) for i in range(head_size)])

    def run_first(g):
        for r in partners:
            piece, squares[g, r] = line.run(
                back, "first", place_of(r), rows, [part(2 * g)], maps[g][1], edev, spread, gates, gain_row, None
            )
            pieces[g, r] = [ship(piece, r)]

    def run_rest(g):
        for r in partners:
            piece = line.run(
                back, "rest", place_of(r), rows, [part(2 * g + 1)], maps[g][1], edev, spread, gates, gain_row,
                squares[g, r],
            )
            pieces[g, r].append(ship(piece, r))

    def run_whole(g, r, own=None):
        return line.run(
            back, "whole", place_of(r), rows, [part(2 * g), part(2 * g + 1)], maps[g][1], edev, spread, gates,
            gain_row, None, own=own,
        )

    result = None

    def run_near(g):
        nonlocal result
        pieces[g, 1] = [ship(run_whole(g, 1), 1)]
        result = run_whole(g, 0, own=(g, groups, result))

    def run_put(g, r):
        nonlocal result
        result = line.run(put, result, pieces[g, r], (me ^ r)[None], g, groups)

    ex = exchanges
    if groups == 2:
        run_front(0)
        run_front(1)
        ex[0].pair()
        run_front(2)
        ex[0].double()
        ex[1].pair()
        run_spans(0)
        ex[0].finish()
        ex[1].double()
        ex[2].pair()
        run_first(0)
        run_spans(1)
        ex[1].finish()
        run_front(3)
        ex[2].double()
        run_rest(0)
        ex[3].pair()
        run_spans(2)
        ex[2].finish()
        ex[3].double()
        run_first(1)
        run_spans(3)
        ex[3].finish()
        run_near(0)
        run_rest(1)
        run_near(1)
    else:
        for c in range(2 * groups):
            run_front(c)
            ex[c].pair()
        for c in range(2 * groups):
            ex[c].double()
            run_spans(c)
        for c in range(2 * groups):
            ex[c].finish()
        for g in range(groups):
            run_first(g)
            run_rest(g)
            run_near(g)
    for g in range(groups):
        run_put(g, 1)
    for g in range(groups):
        for r in partners:
            run_put(g, r)
    return result


def solution(mesh):
    in_specs = (
        P("ctx", "head"),
        P("ctx", "head"),
        P("ctx", None, "head"),
        P("head", "ctx"),
        P("head", "ctx"),
        P(None, "head"),
        P(None, None, "head"),
        P("head"),
        P("head"),
    )
    out_specs = P(("ctx", "head"), None)
    return jax.shard_map(shards, mesh=mesh, in_specs=in_specs, out_specs=out_specs, check_vma=False)
```

```python
import functools

import jax
import jax.numpy as jnp
import numpy as np
from jax import lax
from jax.experimental import pallas as pl
from jax.experimental.pallas import tpu as pltpu
from jax.sharding import PartitionSpec as P

STATE = 256
SPAN = 128
HALO = 16
EPS = 1e-05
F32 = jnp.float32
BF16 = jnp.bfloat16
VMEM_BYTES = 48 * 1024 * 1024
VMEM_SMALL = 8 * 1024 * 1024
COST = pl.CostEstimate(flops=1, bytes_accessed=1, transcendentals=0)
MSG = STATE + 16
KEPT = STATE + 8


def dot(a, b):
    return jnp.dot(a, b, preferred_element_type=F32)


def silu(v):
    half = 0.5 * v
    return half * jnp.tanh(half) + half


def params(limit=VMEM_BYTES):
    return pltpu.CompilerParams(vmem_limit_bytes=limit)


def spread_table(heads, head_dim):
    head = np.arange(2 * heads) % heads
    return (head[:, None] == (np.arange(heads * head_dim) // head_dim)[None, :]).astype(np.float32)


def decay_kernel(log_ref, step_ref, skip_ref, col_ref, row_ref, loc_ref, dev_ref, ecum_ref, edev_ref, skips_ref):
    heads, tokens = log_ref.shape
    spans = tokens // SPAN
    r = lax.broadcasted_iota(jnp.int32, (SPAN, SPAN), 0)
    c = lax.broadcasted_iota(jnp.int32, (SPAN, SPAN), 1)
    upper = (r <= c).astype(F32)
    cums = []
    for k in range(spans):
        cums.append(
            jnp.dot(
                log_ref[:, k * SPAN : (k + 1) * SPAN],
                upper,
                precision=lax.Precision.HIGHEST,
                preferred_element_type=F32,
            )
        )
    totals = [cum[:, SPAN - 1 :] for cum in cums]
    before = [jnp.zeros_like(totals[0])]
    for k in range(spans - 1):
        before.append(before[-1] + totals[k])
    after = [jnp.zeros_like(totals[0])]
    for k in range(spans - 1, 0, -1):
        after.insert(0, after[0] + totals[k])

    def put(ref, k, value):
        high = value.astype(BF16).astype(F32)
        both = jnp.concatenate([high, value - high], axis=0)
        ref[k * SPAN : (k + 1) * SPAN, :] = both.T.astype(BF16)

    skip = skip_ref[...]
    high = skip.astype(BF16).astype(F32)
    parts = jnp.concatenate([high, skip - high], axis=1)
    skips_ref[...] = jnp.broadcast_to(parts, skips_ref.shape).astype(BF16)
    for k in range(spans):
        cum = cums[k]
        step = step_ref[:, k * SPAN : (k + 1) * SPAN]
        col_ref[k * SPAN : (k + 1) * SPAN, :] = jnp.concatenate([cum, cum], axis=0).T
        row_ref[:, k * SPAN : (k + 1) * SPAN] = cum - jnp.log(step)
        to_end = totals[k] - cum
        put(loc_ref, k, jnp.exp(to_end) * step)
        put(dev_ref, k, jnp.exp(to_end + after[k]) * step)
        put(ecum_ref, k, jnp.exp(cum))
        put(edev_ref, k, jnp.exp(cum + before[k]))


def behind(count):
    return [pl.BlockSpec(memory_space=pl.ANY)] * count


def decay_tables(log_decay, step_size, skip_gain):
    heads, tokens = log_decay.shape
    wide = jax.ShapeDtypeStruct((tokens, 2 * heads), BF16)
    return pl.pallas_call(
        decay_kernel,
        out_shape=(
            jax.ShapeDtypeStruct((tokens, 2 * heads), F32),
            jax.ShapeDtypeStruct((heads, tokens), F32),
            wide,
            wide,
            wide,
            wide,
            jax.ShapeDtypeStruct((16, 2 * heads), BF16),
        ),
        compiler_params=params(VMEM_SMALL),
        name="decays",
        cost_estimate=COST,
    )(log_decay, step_size, skip_gain[None])


def conv_rows(read, rows, halo, taps, store):
    count = taps.shape[0]
    for b in range(rows // SPAN):
        own = read(b * SPAN, (b + 1) * SPAN).astype(F32)
        prev = (halo if b == 0 else read(b * SPAN - HALO, b * SPAN)).astype(F32)
        both = jnp.concatenate([prev[HALO - 8 :], own], axis=0)
        total = own * taps[count - 1 : count]
        for k in range(1, count):
            total = total + both[8 - k : 8 - k + SPAN] * taps[count - 1 - k : count - k]
        store(b, silu(total).astype(BF16))


def read_state(ref):
    if ref.dtype == F32:
        return ref[:STATE, :], ref[STATE : STATE + 1, :]
    tail = ref[STATE:MSG, :].astype(F32)
    return ref[:STATE, :].astype(F32), tail[0:1] + tail[8:9]


def write_kept(ref, value, decay):
    ref[:STATE, :] = value
    ref[STATE:KEPT, :] = jnp.broadcast_to(decay, (KEPT - STATE, decay.shape[1]))


def write_sent(ref, value, decay):
    ref[:STATE, :] = value.astype(BF16)
    high = decay.astype(BF16).astype(F32)
    shape = (8, decay.shape[1])
    rows = jnp.concatenate([jnp.broadcast_to(high, shape), jnp.broadcast_to(decay - high, shape)], axis=0)
    ref[STATE:MSG, :] = rows.astype(BF16)


def maps_kernel(order, io_ref, halo_ref, taps_ref, *refs):
    in_map_ref, out_map_ref, turned_ref = refs[order:]

    def put_in(b, value):
        in_map_ref[b * SPAN : (b + 1) * SPAN, :] = value
        turned_ref[:, b * SPAN : (b + 1) * SPAN] = value.T

    def put_out(b, value):
        out_map_ref[b * SPAN : (b + 1) * SPAN, :] = value

    for i, put in ((0, put_in), (1, put_out)):
        conv_rows(
            lambda lo, hi: io_ref[lo:hi, i, :], io_ref.shape[0], halo_ref[:, i, :],
            taps_ref[:, i, :].astype(F32), put,
        )


def maps_of(group, state_io, halo, conv_state, after):
    tokens = state_io.shape[0]
    count = conv_state.shape[0]

    def mine(j):
        return (0, 0, group)

    return pl.pallas_call(
        functools.partial(maps_kernel, len(after)),
        grid=(1,),
        in_specs=[
            pl.BlockSpec((tokens, 2, STATE), mine),
            pl.BlockSpec((HALO, 2, STATE), mine),
            pl.BlockSpec((count, 2, STATE), mine),
            *behind(len(after)),
        ],
        out_specs=[
            pl.BlockSpec((tokens, STATE), lambda j: (0, 0)),
            pl.BlockSpec((tokens, STATE), lambda j: (0, 0)),
            pl.BlockSpec((STATE, tokens), lambda j: (0, 0)),
        ],
        out_shape=[
            jax.ShapeDtypeStruct((tokens, STATE), BF16),
            jax.ShapeDtypeStruct((tokens, STATE), BF16),
            jax.ShapeDtypeStruct((STATE, tokens), BF16),
        ],
        compiler_params=params(),
        name="maps",
        cost_estimate=COST,
    )(state_io, halo, conv_state, *after)


def front_kernel(order, blocks, where_ref, feat_ref, halo_ref, taps_ref, dev_ref, edev_ref, spread_ref, turned_ref, *refs):
    xh_ref, sent_ref, kept_ref, scaled = refs[order:]
    j = pl.program_id(0)
    spread = spread_ref[...]

    def put_feat(b, value):
        rows = slice(b * SPAN, (b + 1) * SPAN)
        xh_ref[rows, :] = value
        scaled[rows, :] = (value.astype(F32) * dot(dev_ref[rows, :], spread)).astype(BF16)

    conv_rows(
        lambda lo, hi: feat_ref[lo:hi, :], feat_ref.shape[0], halo_ref[...], taps_ref[...].astype(F32), put_feat
    )
    state = dot(turned_ref[...], scaled[...])
    decay = dot(edev_ref[...], spread)[15:16]

    @pl.when(j < blocks)
    def _():
        write_sent(sent_ref, state, decay)

    @pl.when(j >= blocks)
    def _():
        write_kept(kept_ref, state, decay)


def front(chunk, where, features, halo, conv_feat, dev, edev, spread, turned, after):
    tokens = features.shape[0]
    start, width = chunk
    half = width // 2
    block = min(512, half)
    blocks = half // block
    base = start // block
    count = conv_feat.shape[0]
    heads2 = dev.shape[1]

    def place(j, where):
        sending = (j < blocks).astype(jnp.int32)
        which = sending * (1 - where[1]) + (1 - sending) * where[1]
        return which * blocks + j - (1 - sending) * blocks

    def cols(j, where):
        return (0, base + place(j, where))

    def same(j, where):
        return (0, 0)

    return pl.pallas_call(
        functools.partial(front_kernel, len(after), blocks),
        grid_spec=pltpu.PrefetchScalarGridSpec(
            num_scalar_prefetch=1,
            grid=(2 * blocks,),
            in_specs=[
                pl.BlockSpec((tokens, block), cols),
                pl.BlockSpec((HALO, block), cols),
                pl.BlockSpec((count, block), cols),
                pl.BlockSpec((tokens, heads2), same),
                pl.BlockSpec((16, heads2), lambda j, where: (tokens // 16 - 1, 0)),
                pl.BlockSpec((heads2, block), cols),
                pl.BlockSpec((STATE, tokens), same),
                *behind(len(after)),
            ],
            out_specs=[
                pl.BlockSpec((tokens, block), lambda j, where: (0, place(j, where))),
                pl.BlockSpec((MSG, block), lambda j, where: (0, jnp.minimum(j, blocks - 1))),
                pl.BlockSpec((KEPT, block), lambda j, where: (0, jnp.maximum(j - blocks, 0))),
            ],
            scratch_shapes=[pltpu.VMEM((tokens, block), BF16)],
        ),
        out_shape=[
            jax.ShapeDtypeStruct((tokens, width), BF16),
            jax.ShapeDtypeStruct((MSG, half), BF16),
            jax.ShapeDtypeStruct((KEPT, half), F32),
        ],
        compiler_params=params(),
        name="front",
        cost_estimate=COST,
    )(where, features, halo, conv_feat, dev, edev, spread, turned, *after)


def span_kernel(
    first_head, order, xh_ref, in_ref, out_ref, col_ref, row_ref, loc_ref, ecum_ref, spread_ref, skips_ref, halves_ref,
    *refs,
):
    y_ref, state = refs[order:]
    width = xh_ref.shape[1]
    head_dim = width // row_ref.shape[0]

    @pl.when(pl.program_id(0) == 0)
    def _():
        state[...] = jnp.zeros_like(state)

    t = lax.broadcasted_iota(jnp.int32, (SPAN, SPAN), 0)
    s = lax.broadcasted_iota(jnp.int32, (SPAN, SPAN), 1)
    first = halves_ref[0:1, :]
    second = halves_ref[1:2, :]
    block = 256
    for k in range(xh_ref.shape[0] // SPAN):
        rows = slice(k * SPAN, (k + 1) * SPAN)
        in_map = in_ref[rows, :]
        out_map = out_ref[rows, :]
        scores = lax.dot_general(out_map, in_map, (((1,), (1,)), ((), ())), preferred_element_type=F32)
        scores = jnp.where(s <= t, scores, 0.0)
        in_turned = in_map.T
        tables = jnp.concatenate([loc_ref[rows, :], ecum_ref[rows, :], skips_ref[...]], axis=0)
        for q in range(width // block):
            cols = slice(q * block, (q + 1) * block)
            feats = xh_ref[rows, cols]
            feats32 = feats.astype(F32)
            wide = dot(tables, spread_ref[:, cols])
            scaled = (feats32 * wide[:SPAN]).astype(BF16)
            ecum = wide[SPAN : 2 * SPAN]
            skip = wide[2 * SPAN : 2 * SPAN + 1]
            pairs = []
            for p in range(block // 128):
                weights = []
                for i in range(2):
                    h = (q * block + p * 128) // head_dim + i
                    gap = col_ref[rows, first_head + h : first_head + h + 1] - row_ref[h : h + 1, rows]
                    weights.append((scores * jnp.exp(jnp.minimum(gap, 0.0))).astype(BF16))
                pair = feats[:, p * 128 : (p + 1) * 128]
                stacked = jnp.concatenate([pair * first, pair * second], axis=0)
                pairs.append(dot(jnp.concatenate(weights, axis=1), stacked))
            diag = jnp.concatenate(pairs, axis=1)
            held = state[:, cols]
            carried = dot(out_map, held.astype(BF16)) * ecum
            y_ref[rows, cols] = diag + carried + skip * feats32
            state[:, cols] = ecum[SPAN - 1 :] * held + dot(in_turned, scaled)


def spans_of(chunk, head_dim, xh, in_map, out_map, col, row, loc, ecum, spread, skips, halves, after):
    tokens, width = xh.shape
    index = chunk[0] // width
    some = width // head_dim
    heads2 = loc.shape[1]
    tile = 2 * SPAN
    return pl.pallas_call(
        functools.partial(span_kernel, index * some, len(after)),
        grid=(tokens // tile,),
        in_specs=[
            pl.BlockSpec((tile, width), lambda k: (k, 0)),
            pl.BlockSpec((tile, STATE), lambda k: (k, 0)),
            pl.BlockSpec((tile, STATE), lambda k: (k, 0)),
            pl.BlockSpec((tile, heads2), lambda k: (k, 0)),
            pl.BlockSpec((some, tile), lambda k: (index, k)),
            pl.BlockSpec((tile, heads2), lambda k: (k, 0)),
            pl.BlockSpec((tile, heads2), lambda k: (k, 0)),
            pl.BlockSpec((heads2, width), lambda k: (0, index)),
            pl.BlockSpec(skips.shape, lambda k: (0, 0)),
            pl.BlockSpec(halves.shape, lambda k: (0, 0)),
            *behind(len(after)),
        ],
        out_specs=pl.BlockSpec((tile, width), lambda k: (k, 0)),
        out_shape=jax.ShapeDtypeStruct((tokens, width), F32),
        scratch_shapes=[pltpu.VMEM((STATE, width), F32)],
        compiler_params=params(),
        name="spans",
        cost_estimate=COST,
    )(xh, in_map, out_map, col, row, loc, ecum, spread, skips, halves, *after)


def pair_kernel(where_ref, kept_ref, got_ref, *refs):
    total_ref, sent_ref = refs[-2:]
    kept, kept_decay = read_state(kept_ref)
    got, got_decay = read_state(got_ref)

    def put(first, second, decay):
        total = decay * first + second
        write_kept(total_ref, total, kept_decay * got_decay)
        write_sent(sent_ref, total, kept_decay * got_decay)

    @pl.when(where_ref[1] == 0)
    def _():
        put(kept, got, got_decay)

    @pl.when(where_ref[1] == 1)
    def _():
        put(got, kept, kept_decay)


def inclusive_kernel(total_ref, before_ref, *refs):
    sent_ref = refs[-1]
    total, decay = read_state(total_ref)
    before, before_decay = read_state(before_ref)
    write_sent(sent_ref, total + decay * before, decay * before_decay)


def extend_kernel(before_ref, far_ref, *refs):
    before, decay = read_state(before_ref)
    far, far_decay = read_state(far_ref)
    write_kept(refs[-1], before + decay * far, decay * far_decay)


def last_kernel(where_ref, before_ref, far_ref, kept_ref, got_ref, *refs):
    mine_ref, sent_ref = refs[-2:]
    before, before_decay = read_state(before_ref)
    far, _ = read_state(far_ref)
    carried = before + before_decay * far

    @pl.when(where_ref[1] == 0)
    def _():
        kept, decay = read_state(kept_ref)
        mine_ref[...] = carried.astype(BF16)
        sent_ref[...] = (decay * carried + kept).astype(BF16)

    @pl.when(where_ref[1] == 1)
    def _():
        got, decay = read_state(got_ref)
        mine_ref[...] = (decay * carried + got).astype(BF16)
        sent_ref[...] = carried.astype(BF16)


def join(kernel, name, where, operands, outs, after):
    width = operands[0].shape[1]
    shapes = {
        "kept": jax.ShapeDtypeStruct((KEPT, width), F32),
        "sent": jax.ShapeDtypeStruct((MSG, width), BF16),
        "state": jax.ShapeDtypeStruct((STATE, width), BF16),
    }
    scalars = [] if where is None else [where]
    return pl.pallas_call(
        kernel,
        in_specs=[pl.BlockSpec(memory_space=pltpu.SMEM)] * len(scalars)
        + [pl.BlockSpec(memory_space=pltpu.VMEM)] * len(operands)
        + behind(len(after)),
        out_specs=[pl.BlockSpec(memory_space=pltpu.VMEM)] * len(outs),
        out_shape=[shapes[out] for out in outs],
        compiler_params=params(VMEM_SMALL),
        name=name,
        cost_estimate=COST,
    )(*scalars, *operands, *after)


def back_kernel(mode, count, partners, order, where_ref, out_ref, edev_ref, *refs):
    chunks = [refs[6 * i : 6 * i + 6] for i in range(count)]
    refs = refs[6 * count :]
    if mode == "rest":
        squares_ref, *refs = refs
    refs = refs[order:]
    o_refs = refs[:partners]
    if mode == "first":
        squares_ref = refs[partners]
    gated = refs[-1]
    out_map = out_ref[...]
    edev = edev_ref[...]
    rows = out_map.shape[0]
    block = 256
    steps = pl.num_programs(0) // partners
    odd = where_ref[1] == 1
    squares = squares_ref[...] if mode == "rest" else jnp.zeros((rows, 128), F32)
    at = 0
    for y_ref, mine_ref, other_ref, spread_ref, gate_ref, gain_ref in chunks:
        half = mine_ref.shape[1]
        for q in range(2 * half // block):
            cols = slice(q * block, (q + 1) * block)
            inner = slice(q * block % half, q * block % half + block)
            mine = mine_ref[:, inner]
            other = other_ref[:, inner]
            state = jnp.where(odd, other, mine) if q * block < half else jnp.where(odd, mine, other)
            carried = dot(out_map, state) * dot(edev, spread_ref[:, cols])
            value = (y_ref[:, cols] + carried) * silu(gate_ref[:, cols].astype(F32))
            square = value * value
            squares = squares + square[:, :128] + square[:, 128:]
            gated[:, at : at + block] = value * gain_ref[:, cols]
            at += block
    if mode == "first":
        squares_ref[...] = squares
    else:
        width = at if mode == "whole" else 2 * at
        mean = jnp.sum(squares, axis=1, keepdims=True) * (1.0 / width)
        scale = lax.rsqrt(mean + EPS)
    for p in range(partners):

        @pl.when(pl.program_id(0) // steps == p)
        def _(o_ref=o_refs[p]):
            for q in range(at // block):
                cols = slice(q * block, (q + 1) * block)
                value = gated[:, cols] if mode == "first" else gated[:, cols] * scale
                o_ref[:, cols] = value.astype(BF16)
            if mode == "rest":
                high = scale.astype(BF16).astype(F32)
                lane = lax.broadcasted_iota(jnp.int32, (rows, 128), 1)
                o_ref[:, at:] = jnp.where(lane < 64, high, scale - high).astype(BF16)


def back(mode, some, where, rows, chunks, out_map, edev, spread, gates, gain_row, squares, after, own=None):
    heads2 = edev.shape[1]
    tile = 128
    steps = rows // tile
    partners = len(some)

    def at(i, where):
        turn = some[0]
        for p in range(1, partners):
            turn = jnp.where(i >= p * steps, some[p], turn)
        return ((where[0] ^ turn) * steps + i % steps, 0)

    specs = [pl.BlockSpec((tile, STATE), at), pl.BlockSpec((tile, heads2), at)]
    operands = [out_map, edev]
    total = 0
    for (start, width), y, mine, other in chunks:
        index = start // width
        half = width // 2
        total += width
        specs += [
            pl.BlockSpec((tile, width), at),
            pl.BlockSpec((STATE, half), lambda i, where: (0, 0)),
            pl.BlockSpec((STATE, half), lambda i, where: (0, 0)),
            pl.BlockSpec((heads2, width), lambda i, where, index=index: (0, index)),
            pl.BlockSpec((tile, width), lambda i, where, index=index: (at(i, where)[0], index)),
            pl.BlockSpec((1, width), lambda i, where, index=index: (0, index)),
        ]
        operands += [y, mine, other, spread, gates, gain_row]
    if mode == "rest":
        specs.append(pl.BlockSpec((tile, 128), lambda i, where: (i, 0)))
        operands.append(squares)
    aliases = {}
    if own is not None and own[2] is not None:
        after = [own[2], *after]
        aliases = {1 + len(operands): partners - 1}
    specs += behind(len(after))
    operands += after
    sent = total + 128 if mode == "rest" else total

    def part_of(p):
        return lambda i, where: (jnp.clip(i - p * steps, 0, steps - 1), 0)

    out_specs = [pl.BlockSpec((tile, sent), part_of(p)) for p in range(partners)]
    out_shape = [jax.ShapeDtypeStruct((rows, sent), BF16)] * partners
    if own is not None:
        group, groups, _ = own
        out_specs[-1] = pl.BlockSpec(
            (tile, total),
            lambda i, where: (jnp.clip(i - (partners - 1) * steps, 0, steps - 1), (where[0] ^ some[-1]) * groups + group),
        )
        out_shape[-1] = jax.ShapeDtypeStruct((rows, groups * total * (gates.shape[0] // rows)), BF16)
    if mode == "first":
        out_specs.append(pl.BlockSpec((tile, 128), lambda i, where: (i, 0)))
        out_shape.append(jax.ShapeDtypeStruct((partners * rows, 128), F32))
    return pl.pallas_call(
        functools.partial(back_kernel, mode, len(chunks), partners, len(after)),
        grid_spec=pltpu.PrefetchScalarGridSpec(
            num_scalar_prefetch=1,
            grid=(partners * steps,),
            in_specs=specs,
            out_specs=out_specs,
            scratch_shapes=[pltpu.VMEM((tile, total), F32)],
        ),
        out_shape=out_shape,
        input_output_aliases=aliases,
        compiler_params=params(),
        name=f"back_{mode}",
        cost_estimate=COST,
    )(where, *operands)


def shifted(value, pairs, steps):
    return lax.ppermute(
        value,
        "ctx",
        [(2 * q + y, 2 * (q + steps) + y) for q in range(pairs - steps) for y in range(2)],
    )


def swapped(value, pairs):
    return lax.ppermute(value, "ctx", [(2 * q + y, 2 * q + 1 - y) for q in range(pairs) for y in range(2)])


class Line:
    def __init__(self):
        self.last = []

    def run(self, make, *args, **kwargs):
        made = make(*args, after=self.last, **kwargs)
        self.last = [made[0] if isinstance(made, (list, tuple)) else made]
        return made


class Exchange:
    def __init__(self, line, where, pairs, sent, kept):
        self.line = line
        self.where = where
        self.pairs = pairs
        self.kept = kept
        self.got = swapped(sent, pairs)

    def pair(self):
        self.total, sent = self.line.run(
            join, pair_kernel, "pair", self.where, [self.kept, self.got], ["kept", "sent"]
        )
        self.before = shifted(sent, self.pairs, 1)
        self.reach = 1

    def double(self):
        (sent,) = self.line.run(join, inclusive_kernel, "inclusive", None, [self.total, self.before], ["sent"])
        self.far = shifted(sent, self.pairs, self.reach + 1)
        self.reach = 2 * self.reach + 1

    def extend(self):
        while self.reach < self.pairs - 1:
            (self.before,) = self.line.run(join, extend_kernel, "extend", None, [self.before, self.far], ["kept"])
            self.double()

    def finish(self):
        self.extend()
        self.mine, sent = self.line.run(
            join, last_kernel, "last", self.where, [self.before, self.far, self.kept, self.got], ["state", "state"]
        )
        self.other = swapped(sent, self.pairs)


def shards(
    features, gates, state_io, step_size, log_decay, conv_feat, conv_state, skip_gain, norm_gain
):
    tokens, channels = features.shape
    heads = step_size.shape[0]
    head_dim = channels // heads
    groups = state_io.shape[2] // STATE
    group_width = channels // groups
    width = group_width // 2
    count = conv_feat.shape[0]
    rim = count - 1
    ctx_size = lax.axis_size("ctx")
    head_size = lax.axis_size("head")
    pairs = ctx_size // 2
    rows = tokens // head_size
    me = lax.axis_index("head").astype(jnp.int32)
    where = jnp.stack([me, lax.axis_index("ctx").astype(jnp.int32) % 2])

    onward = [(i, i + 1) for i in range(ctx_size - 1)]
    pad = HALO - rim
    halo = jnp.pad(lax.ppermute(features[tokens - rim :], "ctx", onward), ((pad, 0), (0, 0)))
    io_halo = jnp.pad(lax.ppermute(state_io[tokens - rim :], "ctx", onward), ((pad, 0), (0, 0), (0, 0)))
    spread = jnp.asarray(spread_table(heads, head_dim), BF16)
    halves = jnp.asarray(np.arange(128)[None, :] // head_dim == np.arange(2)[:, None], BF16)
    col, row, loc, dev, ecum, edev, skips = decay_tables(log_decay, step_size, skip_gain)
    gain_row = norm_gain[None]

    line = Line()
    chunks = [(c * width, width) for c in range(2 * groups)]
    fronts = {}
    maps = {}
    exchanges = {}
    ys = {}

    def run_maps(g):
        maps[g] = line.run(maps_of, g, state_io, io_halo, conv_state)

    def run_front(c):
        made = line.run(
            front, chunks[c], where, features, halo, conv_feat, dev, edev, spread, maps[c // 2][2]
        )
        fronts[c] = made[0]
        exchanges[c] = Exchange(line, where, pairs, made[1], made[2])

    def run_spans(c):
        g = c // 2
        ys[c] = line.run(
            spans_of, chunks[c], head_dim, fronts[c], *maps[g][:2], col, row, loc, ecum, spread, skips, halves
        )

    def part(c):
        return (chunks[c], ys[c], exchanges[c].mine, exchanges[c].other)

    partners = list(range(head_size - 1, 1, -1))
    squares = {}
    pieces = {}

    def ship(piece, r):
        return lax.ppermute(piece, "head", [(i, i ^ r) for i in range(head_size)])

    def run_back(mode, some, g, parts, squares, own=None):
        return line.run(
            back, mode, some, where, rows, [part(c) for c in parts], maps[g][1], edev, spread, gates, gain_row,
            squares, own=own,
        )

    def arrived(g, index):
        line.last += [pieces[g, r][index] for r in partners]

    def run_first(g, apart=False):
        squares[g] = []
        for some in [[r] for r in partners] if apart else [partners]:
            *made, square = run_back("first", some, g, [2 * g], None)
            squares[g].append((some, square))
            for r, piece in zip(some, made):
                pieces[g, r] = [ship(piece, r)]

    def run_rest(g):
        for some, square in squares[g]:
            made = run_back("rest", some, g, [2 * g + 1], square)
            for r, piece in zip(some, made):
                pieces[g, r].append(ship(piece, r))

    result = None

    def run_near(g):
        nonlocal result
        made, result = run_back("whole", [1, 0], g, [2 * g, 2 * g + 1], None, own=(g, groups, result))
        pieces[g, 1] = [ship(made, 1)]

    def run_put(g, r):
        nonlocal result
        start = (me ^ r) * channels + g * group_width
        zero = jnp.int32(0)
        if len(pieces[g, r]) == 2:
            first, rest = pieces[g, r]
            scale = rest[:, width : width + 1].astype(F32) + rest[:, width + 64 : width + 65].astype(F32)
            first = (first.astype(F32) * scale).astype(BF16)
            result = lax.dynamic_update_slice(result, first, (zero, start))
            result = lax.dynamic_update_slice(result, rest[:, :width], (zero, start + width))
        else:
            result = lax.dynamic_update_slice(result, pieces[g, r][0], (zero, start))

    ex = exchanges
    if groups == 2:
        run_maps(0)
        run_front(0)
        run_front(1)
        ex[0].pair()
        run_maps(1)
        ex[0].double()
        ex[1].pair()
        run_spans(0)
        ex[0].finish()
        ex[1].double()
        run_first(0, apart=True)
        run_front(2)
        run_spans(1)
        ex[1].finish()
        ex[2].pair()
        run_front(3)
        arrived(0, 0)
        run_rest(0)
        ex[2].double()
        ex[3].pair()
        run_spans(2)
        ex[2].finish()
        ex[3].double()
        arrived(0, 1)
        run_first(1)
        run_spans(3)
        ex[3].finish()
        run_near(0)
        arrived(1, 0)
        run_rest(1)
        run_near(1)
    else:
        for c in range(2 * groups):
            if c % 2 == 0:
                run_maps(c // 2)
            run_front(c)
            ex[c].pair()
        for c in range(2 * groups):
            ex[c].double()
            run_spans(c)
        for c in range(2 * groups):
            ex[c].finish()
        for g in range(groups):
            run_first(g)
            run_rest(g)
            run_near(g)
    for g in range(groups):
        run_put(g, 1)
    for g in range(groups):
        for r in partners:
            run_put(g, r)
    return result


def solution(mesh):
    in_specs = (
        P("ctx", "head"),
        P("ctx", "head"),
        P("ctx", None, "head"),
        P("head", "ctx"),
        P("head", "ctx"),
        P(None, "head"),
        P(None, None, "head"),
        P("head"),
        P("head"),
    )
    out_specs = P(("ctx", "head"), None)
    return jax.shard_map(shards, mesh=mesh, in_specs=in_specs, out_specs=out_specs, check_vma=False)
```

```python
import functools

import jax
import jax.numpy as jnp
import numpy as np
from jax import lax
from jax.experimental import pallas as pl
from jax.experimental.pallas import tpu as pltpu
from jax.sharding import PartitionSpec as P

STATE = 256
SPAN = 128
HALO = 16
EPS = 1e-05
F32 = jnp.float32
BF16 = jnp.bfloat16
VMEM_BYTES = 40 * 1024 * 1024
VMEM_SMALL = 8 * 1024 * 1024
COST_SCALE = 10**9
MSG = STATE + 16
KEPT = STATE + 8


def dot(a, b):
    return jnp.dot(a, b, preferred_element_type=F32)


def silu(v):
    half = 0.5 * v
    return half * jnp.tanh(half) + half


def cost(micros):
    return pl.CostEstimate(flops=int(micros * COST_SCALE), bytes_accessed=1, transcendentals=0)


def params(limit=VMEM_BYTES):
    return pltpu.CompilerParams(vmem_limit_bytes=limit)


def spread_table(heads, head_dim):
    head = np.arange(2 * heads) % heads
    return (head[:, None] == (np.arange(heads * head_dim) // head_dim)[None, :]).astype(np.float32)


def decay_kernel(log_ref, step_ref, skip_ref, col_ref, row_ref, loc_ref, dev_ref, ecum_ref, edev_ref, skips_ref):
    heads, tokens = log_ref.shape
    spans = tokens // SPAN
    r = lax.broadcasted_iota(jnp.int32, (SPAN, SPAN), 0)
    c = lax.broadcasted_iota(jnp.int32, (SPAN, SPAN), 1)
    upper = (r <= c).astype(F32)
    cums = []
    for k in range(spans):
        cums.append(
            jnp.dot(
                log_ref[:, k * SPAN : (k + 1) * SPAN],
                upper,
                precision=lax.Precision.HIGHEST,
                preferred_element_type=F32,
            )
        )
    totals = [cum[:, SPAN - 1 :] for cum in cums]
    before = [jnp.zeros_like(totals[0])]
    for k in range(spans - 1):
        before.append(before[-1] + totals[k])
    after = [jnp.zeros_like(totals[0])]
    for k in range(spans - 1, 0, -1):
        after.insert(0, after[0] + totals[k])

    def put(ref, k, value):
        high = value.astype(BF16).astype(F32)
        both = jnp.concatenate([high, value - high], axis=0)
        ref[k * SPAN : (k + 1) * SPAN, :] = both.T.astype(BF16)

    skip = skip_ref[...]
    high = skip.astype(BF16).astype(F32)
    parts = jnp.concatenate([high, skip - high], axis=1)
    skips_ref[...] = jnp.broadcast_to(parts, skips_ref.shape).astype(BF16)
    for k in range(spans):
        cum = cums[k]
        step = step_ref[:, k * SPAN : (k + 1) * SPAN]
        col_ref[k * SPAN : (k + 1) * SPAN, :] = jnp.concatenate([cum, cum], axis=0).T
        row_ref[:, k * SPAN : (k + 1) * SPAN] = cum - jnp.log(step)
        to_end = totals[k] - cum
        put(loc_ref, k, jnp.exp(to_end) * step)
        put(dev_ref, k, jnp.exp(to_end + after[k]) * step)
        put(ecum_ref, k, jnp.exp(cum))
        put(edev_ref, k, jnp.exp(cum + before[k]))


def behind(count):
    return [pl.BlockSpec(memory_space=pl.ANY)] * count


def decay_tables(log_decay, step_size, skip_gain):
    heads, tokens = log_decay.shape
    wide = jax.ShapeDtypeStruct((tokens, 2 * heads), BF16)
    return pl.pallas_call(
        decay_kernel,
        out_shape=(
            jax.ShapeDtypeStruct((tokens, 2 * heads), F32),
            jax.ShapeDtypeStruct((heads, tokens), F32),
            wide,
            wide,
            wide,
            wide,
            jax.ShapeDtypeStruct((16, 2 * heads), BF16),
        ),
        compiler_params=params(),
        name="decays",
        cost_estimate=cost(1.5),
    )(log_decay, step_size, skip_gain[None])


def conv_rows(read, rows, halo, taps, store):
    count = taps.shape[0]
    for b in range(rows // SPAN):
        own = read(b * SPAN, (b + 1) * SPAN).astype(F32)
        prev = (halo if b == 0 else read(b * SPAN - HALO, b * SPAN)).astype(F32)
        both = jnp.concatenate([prev[HALO - 8 :], own], axis=0)
        total = own * taps[count - 1 : count]
        for k in range(1, count):
            total = total + both[8 - k : 8 - k + SPAN] * taps[count - 1 - k : count - k]
        store(b, silu(total).astype(BF16))


def read_state(ref):
    if ref.dtype == F32:
        return ref[:STATE, :], ref[STATE : STATE + 1, :]
    tail = ref[STATE:MSG, :].astype(F32)
    return ref[:STATE, :].astype(F32), tail[0:1] + tail[8:9]


def write_kept(ref, value, decay):
    ref[:STATE, :] = value
    ref[STATE:KEPT, :] = jnp.broadcast_to(decay, (KEPT - STATE, decay.shape[1]))


def write_sent(ref, value, decay):
    ref[:STATE, :] = value.astype(BF16)
    high = decay.astype(BF16).astype(F32)
    shape = (8, decay.shape[1])
    rows = jnp.concatenate([jnp.broadcast_to(high, shape), jnp.broadcast_to(decay - high, shape)], axis=0)
    ref[STATE:MSG, :] = rows.astype(BF16)


def maps_kernel(order, io_ref, halo_ref, taps_ref, *refs):
    in_map_ref, out_map_ref, turned_ref = refs[order:]

    def put_in(b, value):
        in_map_ref[b * SPAN : (b + 1) * SPAN, :] = value
        turned_ref[:, b * SPAN : (b + 1) * SPAN] = value.T

    def put_out(b, value):
        out_map_ref[b * SPAN : (b + 1) * SPAN, :] = value

    for i, put in ((0, put_in), (1, put_out)):
        conv_rows(
            lambda lo, hi: io_ref[lo:hi, i, :], io_ref.shape[0], halo_ref[:, i, :],
            taps_ref[:, i, :].astype(F32), put,
        )


def maps_of(group, state_io, halo, conv_state, after):
    tokens = state_io.shape[0]
    count = conv_state.shape[0]

    def mine(j):
        return (0, 0, group)

    return pl.pallas_call(
        functools.partial(maps_kernel, len(after)),
        grid=(1,),
        in_specs=[
            pl.BlockSpec((tokens, 2, STATE), mine),
            pl.BlockSpec((HALO, 2, STATE), mine),
            pl.BlockSpec((count, 2, STATE), mine),
            *behind(len(after)),
        ],
        out_specs=[
            pl.BlockSpec((tokens, STATE), lambda j: (0, 0)),
            pl.BlockSpec((tokens, STATE), lambda j: (0, 0)),
            pl.BlockSpec((STATE, tokens), lambda j: (0, 0)),
        ],
        out_shape=[
            jax.ShapeDtypeStruct((tokens, STATE), BF16),
            jax.ShapeDtypeStruct((tokens, STATE), BF16),
            jax.ShapeDtypeStruct((STATE, tokens), BF16),
        ],
        compiler_params=params(),
        name="maps",
        cost_estimate=cost(3),
    )(state_io, halo, conv_state, *after)


def front_kernel(order, blocks, where_ref, feat_ref, halo_ref, taps_ref, dev_ref, edev_ref, spread_ref, turned_ref, *refs):
    xh_ref, sent_ref, kept_ref, scaled = refs[order:]
    j = pl.program_id(0)
    spread = spread_ref[...]

    def put_feat(b, value):
        rows = slice(b * SPAN, (b + 1) * SPAN)
        xh_ref[rows, :] = value
        scaled[rows, :] = (value.astype(F32) * dot(dev_ref[rows, :], spread)).astype(BF16)

    conv_rows(
        lambda lo, hi: feat_ref[lo:hi, :], feat_ref.shape[0], halo_ref[...], taps_ref[...].astype(F32), put_feat
    )
    state = dot(turned_ref[...], scaled[...])
    decay = dot(edev_ref[...], spread)[15:16]

    @pl.when(j < blocks)
    def _():
        write_sent(sent_ref, state, decay)

    @pl.when(j >= blocks)
    def _():
        write_kept(kept_ref, state, decay)


def front(chunk, where, features, halo, conv_feat, dev, edev, spread, turned, after):
    tokens = features.shape[0]
    start, width = chunk
    half = width // 2
    block = min(512, half)
    blocks = half // block
    base = start // block
    count = conv_feat.shape[0]
    heads2 = dev.shape[1]

    def place(j, where):
        sending = (j < blocks).astype(jnp.int32)
        which = sending * (1 - where[1]) + (1 - sending) * where[1]
        return which * blocks + j - (1 - sending) * blocks

    def cols(j, where):
        return (0, base + place(j, where))

    def same(j, where):
        return (0, 0)

    return pl.pallas_call(
        functools.partial(front_kernel, len(after), blocks),
        grid_spec=pltpu.PrefetchScalarGridSpec(
            num_scalar_prefetch=1,
            grid=(2 * blocks,),
            in_specs=[
                pl.BlockSpec((tokens, block), cols),
                pl.BlockSpec((HALO, block), cols),
                pl.BlockSpec((count, block), cols),
                pl.BlockSpec((tokens, heads2), same),
                pl.BlockSpec((16, heads2), lambda j, where: (tokens // 16 - 1, 0)),
                pl.BlockSpec((heads2, block), cols),
                pl.BlockSpec((STATE, tokens), same),
                *behind(len(after)),
            ],
            out_specs=[
                pl.BlockSpec((tokens, block), lambda j, where: (0, place(j, where))),
                pl.BlockSpec((MSG, block), lambda j, where: (0, jnp.minimum(j, blocks - 1))),
                pl.BlockSpec((KEPT, block), lambda j, where: (0, jnp.maximum(j - blocks, 0))),
            ],
            scratch_shapes=[pltpu.VMEM((tokens, block), BF16)],
        ),
        out_shape=[
            jax.ShapeDtypeStruct((tokens, width), BF16),
            jax.ShapeDtypeStruct((MSG, half), BF16),
            jax.ShapeDtypeStruct((KEPT, half), F32),
        ],
        compiler_params=params(),
        name="front",
        cost_estimate=cost(3),
    )(where, features, halo, conv_feat, dev, edev, spread, turned, *after)


def span_kernel(
    first_head, order, xh_ref, in_ref, out_ref, col_ref, row_ref, loc_ref, ecum_ref, spread_ref, skips_ref, halves_ref,
    *refs,
):
    y_ref, state = refs[order:]
    width = xh_ref.shape[1]
    head_dim = width // row_ref.shape[0]

    @pl.when(pl.program_id(0) == 0)
    def _():
        state[...] = jnp.zeros_like(state)

    t = lax.broadcasted_iota(jnp.int32, (SPAN, SPAN), 0)
    s = lax.broadcasted_iota(jnp.int32, (SPAN, SPAN), 1)
    first = halves_ref[0:1, :]
    second = halves_ref[1:2, :]
    block = 256
    for k in range(xh_ref.shape[0] // SPAN):
        rows = slice(k * SPAN, (k + 1) * SPAN)
        in_map = in_ref[rows, :]
        out_map = out_ref[rows, :]
        scores = lax.dot_general(out_map, in_map, (((1,), (1,)), ((), ())), preferred_element_type=F32)
        scores = jnp.where(s <= t, scores, 0.0)
        in_turned = in_map.T
        tables = jnp.concatenate([loc_ref[rows, :], ecum_ref[rows, :], skips_ref[...]], axis=0)
        for q in range(width // block):
            cols = slice(q * block, (q + 1) * block)
            feats = xh_ref[rows, cols]
            feats32 = feats.astype(F32)
            wide = dot(tables, spread_ref[:, cols])
            scaled = (feats32 * wide[:SPAN]).astype(BF16)
            ecum = wide[SPAN : 2 * SPAN]
            skip = wide[2 * SPAN : 2 * SPAN + 1]
            pairs = []
            for p in range(block // 128):
                weights = []
                for i in range(2):
                    h = (q * block + p * 128) // head_dim + i
                    gap = col_ref[rows, first_head + h : first_head + h + 1] - row_ref[h : h + 1, rows]
                    weights.append((scores * jnp.exp(jnp.minimum(gap, 0.0))).astype(BF16))
                pair = feats[:, p * 128 : (p + 1) * 128]
                stacked = jnp.concatenate([pair * first, pair * second], axis=0)
                pairs.append(dot(jnp.concatenate(weights, axis=1), stacked))
            diag = jnp.concatenate(pairs, axis=1)
            held = state[:, cols]
            carried = dot(out_map, held.astype(BF16)) * ecum
            y_ref[rows, cols] = diag + carried + skip * feats32
            state[:, cols] = ecum[SPAN - 1 :] * held + dot(in_turned, scaled)


def spans_of(chunk, head_dim, xh, in_map, out_map, col, row, loc, ecum, spread, skips, halves, after):
    tokens, width = xh.shape
    index = chunk[0] // width
    some = width // head_dim
    heads2 = loc.shape[1]
    tile = 2 * SPAN
    return pl.pallas_call(
        functools.partial(span_kernel, index * some, len(after)),
        grid=(tokens // tile,),
        in_specs=[
            pl.BlockSpec((tile, width), lambda k: (k, 0)),
            pl.BlockSpec((tile, STATE), lambda k: (k, 0)),
            pl.BlockSpec((tile, STATE), lambda k: (k, 0)),
            pl.BlockSpec((tile, heads2), lambda k: (k, 0)),
            pl.BlockSpec((some, tile), lambda k: (index, k)),
            pl.BlockSpec((tile, heads2), lambda k: (k, 0)),
            pl.BlockSpec((tile, heads2), lambda k: (k, 0)),
            pl.BlockSpec((heads2, width), lambda k: (0, index)),
            pl.BlockSpec(skips.shape, lambda k: (0, 0)),
            pl.BlockSpec(halves.shape, lambda k: (0, 0)),
            *behind(len(after)),
        ],
        out_specs=pl.BlockSpec((tile, width), lambda k: (k, 0)),
        out_shape=jax.ShapeDtypeStruct((tokens, width), F32),
        scratch_shapes=[pltpu.VMEM((STATE, width), F32)],
        compiler_params=params(),
        name="spans",
        cost_estimate=cost(200),
    )(xh, in_map, out_map, col, row, loc, ecum, spread, skips, halves, *after)


def pair_kernel(where_ref, kept_ref, got_ref, *refs):
    total_ref, sent_ref = refs[-2:]
    kept, kept_decay = read_state(kept_ref)
    got, got_decay = read_state(got_ref)

    def put(first, second, decay):
        total = decay * first + second
        write_kept(total_ref, total, kept_decay * got_decay)
        write_sent(sent_ref, total, kept_decay * got_decay)

    @pl.when(where_ref[1] == 0)
    def _():
        put(kept, got, got_decay)

    @pl.when(where_ref[1] == 1)
    def _():
        put(got, kept, kept_decay)


def inclusive_kernel(total_ref, before_ref, *refs):
    sent_ref = refs[-1]
    total, decay = read_state(total_ref)
    before, before_decay = read_state(before_ref)
    write_sent(sent_ref, total + decay * before, decay * before_decay)


def extend_kernel(before_ref, far_ref, *refs):
    before, decay = read_state(before_ref)
    far, far_decay = read_state(far_ref)
    write_kept(refs[-1], before + decay * far, decay * far_decay)


def last_kernel(where_ref, before_ref, far_ref, kept_ref, got_ref, *refs):
    mine_ref, sent_ref = refs[-2:]
    before, before_decay = read_state(before_ref)
    far, _ = read_state(far_ref)
    carried = before + before_decay * far

    @pl.when(where_ref[1] == 0)
    def _():
        kept, decay = read_state(kept_ref)
        mine_ref[...] = carried.astype(BF16)
        sent_ref[...] = (decay * carried + kept).astype(BF16)

    @pl.when(where_ref[1] == 1)
    def _():
        got, decay = read_state(got_ref)
        mine_ref[...] = (decay * carried + got).astype(BF16)
        sent_ref[...] = carried.astype(BF16)


def join(kernel, name, where, operands, outs, after):
    width = operands[0].shape[1]
    shapes = {
        "kept": jax.ShapeDtypeStruct((KEPT, width), F32),
        "sent": jax.ShapeDtypeStruct((MSG, width), BF16),
        "state": jax.ShapeDtypeStruct((STATE, width), BF16),
    }
    scalars = [] if where is None else [where]
    return pl.pallas_call(
        kernel,
        in_specs=[pl.BlockSpec(memory_space=pltpu.SMEM)] * len(scalars)
        + [pl.BlockSpec(memory_space=pltpu.VMEM)] * len(operands)
        + behind(len(after)),
        out_specs=[pl.BlockSpec(memory_space=pltpu.VMEM)] * len(outs),
        out_shape=[shapes[out] for out in outs],
        compiler_params=params(VMEM_SMALL),
        name=name,
        cost_estimate=cost(0.7),
    )(*scalars, *operands, *after)


def back_kernel(mode, count, partners, order, where_ref, out_ref, edev_ref, *refs):
    chunks = [refs[6 * i : 6 * i + 6] for i in range(count)]
    refs = refs[6 * count :]
    if mode == "rest":
        squares_ref, *refs = refs
    refs = refs[order:]
    o_refs = refs[:partners]
    if mode == "first":
        squares_ref = refs[partners]
    gated = refs[-1]
    out_map = out_ref[...]
    edev = edev_ref[...]
    rows = out_map.shape[0]
    block = 256
    steps = pl.num_programs(0) // partners
    odd = where_ref[1] == 1
    squares = squares_ref[...] if mode == "rest" else jnp.zeros((rows, 128), F32)
    at = 0
    for y_ref, mine_ref, other_ref, spread_ref, gate_ref, gain_ref in chunks:
        half = mine_ref.shape[1]
        for q in range(2 * half // block):
            cols = slice(q * block, (q + 1) * block)
            inner = slice(q * block % half, q * block % half + block)
            mine = mine_ref[:, inner]
            other = other_ref[:, inner]
            state = jnp.where(odd, other, mine) if q * block < half else jnp.where(odd, mine, other)
            carried = dot(out_map, state) * dot(edev, spread_ref[:, cols])
            value = (y_ref[:, cols] + carried) * silu(gate_ref[:, cols].astype(F32))
            square = value * value
            squares = squares + square[:, :128] + square[:, 128:]
            gated[:, at : at + block] = value * gain_ref[:, cols]
            at += block
    if mode == "first":
        squares_ref[...] = squares
    else:
        width = at if mode == "whole" else 2 * at
        mean = jnp.sum(squares, axis=1, keepdims=True) * (1.0 / width)
        scale = lax.rsqrt(mean + EPS)
    for p in range(partners):

        @pl.when(pl.program_id(0) // steps == p)
        def _(o_ref=o_refs[p]):
            if mode == "rest":
                step = pl.program_id(0) - p * steps
                start = pl.multiple_of(step * rows, rows)
                high = scale.astype(BF16).astype(F32)
                parts = [jnp.broadcast_to(part, (rows, 128)).T[:8] for part in (high, scale - high)]
                o_ref[steps * rows :, pl.ds(start, rows)] = jnp.concatenate(parts, axis=0).astype(BF16)
            for q in range(at // block):
                cols = slice(q * block, (q + 1) * block)
                value = gated[:, cols] if mode == "first" else gated[:, cols] * scale
                if mode == "rest":
                    o_ref[pl.ds(start, rows), cols] = value.astype(BF16)
                else:
                    o_ref[:, cols] = value.astype(BF16)


def back(mode, some, where, rows, chunks, out_map, edev, spread, gates, gain_row, squares, after, own=None):
    heads2 = edev.shape[1]
    tile = 128
    steps = rows // tile
    partners = len(some)

    def at(i, where):
        turn = some[0]
        for p in range(1, partners):
            turn = jnp.where(i >= p * steps, some[p], turn)
        return ((where[0] ^ turn) * steps + i % steps, 0)

    specs = [pl.BlockSpec((tile, STATE), at), pl.BlockSpec((tile, heads2), at)]
    operands = [out_map, edev]
    total = 0
    for (start, width), y, mine, other in chunks:
        index = start // width
        half = width // 2
        total += width
        specs += [
            pl.BlockSpec((tile, width), at),
            pl.BlockSpec((STATE, half), lambda i, where: (0, 0)),
            pl.BlockSpec((STATE, half), lambda i, where: (0, 0)),
            pl.BlockSpec((heads2, width), lambda i, where, index=index: (0, index)),
            pl.BlockSpec((tile, width), lambda i, where, index=index: (at(i, where)[0], index)),
            pl.BlockSpec((1, width), lambda i, where, index=index: (0, index)),
        ]
        operands += [y, mine, other, spread, gates, gain_row]
    if mode == "rest":
        specs.append(pl.BlockSpec((tile, 128), lambda i, where: (i, 0)))
        operands.append(squares)
    aliases = {}
    if own is not None and own[2] is not None:
        after = [own[2], *after]
        aliases = {1 + len(operands): partners - 1}
    specs += behind(len(after))
    operands += after
    sent = rows + 16 if mode == "rest" else rows
    part = sent if mode == "rest" else tile

    def part_of(p):
        if mode == "rest":
            return lambda i, where: (0, 0)
        return lambda i, where: (jnp.clip(i - p * steps, 0, steps - 1), 0)

    out_specs = [pl.BlockSpec((part, total), part_of(p)) for p in range(partners)]
    out_shape = [jax.ShapeDtypeStruct((sent, total), BF16)] * partners
    if own is not None:
        group, groups, _ = own
        out_specs[-1] = pl.BlockSpec(
            (tile, total),
            lambda i, where: (jnp.clip(i - (partners - 1) * steps, 0, steps - 1), (where[0] ^ some[-1]) * groups + group),
        )
        out_shape[-1] = jax.ShapeDtypeStruct((rows, groups * total * (gates.shape[0] // rows)), BF16)
    if mode == "first":
        out_specs.append(pl.BlockSpec((tile, 128), lambda i, where: (i, 0)))
        out_shape.append(jax.ShapeDtypeStruct((partners * rows, 128), F32))
    return pl.pallas_call(
        functools.partial(back_kernel, mode, len(chunks), partners, len(after)),
        grid_spec=pltpu.PrefetchScalarGridSpec(
            num_scalar_prefetch=1,
            grid=(partners * steps,),
            in_specs=specs,
            out_specs=out_specs,
            scratch_shapes=[pltpu.VMEM((tile, total), F32)],
        ),
        out_shape=out_shape,
        input_output_aliases=aliases,
        compiler_params=params(),
        name=f"back_{mode}",
        cost_estimate=cost(1),
    )(where, *operands)


def shifted(value, pairs, steps):
    return lax.ppermute(
        value,
        "ctx",
        [(2 * q + y, 2 * (q + steps) + y) for q in range(pairs - steps) for y in range(2)],
    )


def swapped(value, pairs):
    return lax.ppermute(value, "ctx", [(2 * q + y, 2 * q + 1 - y) for q in range(pairs) for y in range(2)])


class Line:
    def __init__(self):
        self.last = []

    def run(self, make, *args, **kwargs):
        made = make(*args, after=self.last, **kwargs)
        self.last = [made[0] if isinstance(made, (list, tuple)) else made]
        return made


class Exchange:
    def __init__(self, line, where, pairs, sent, kept):
        self.line = line
        self.where = where
        self.pairs = pairs
        self.kept = kept
        self.got = swapped(sent, pairs)

    def pair(self):
        self.total, sent = self.line.run(
            join, pair_kernel, "pair", self.where, [self.kept, self.got], ["kept", "sent"]
        )
        self.before = shifted(sent, self.pairs, 1)
        self.reach = 1

    def double(self):
        (sent,) = self.line.run(join, inclusive_kernel, "inclusive", None, [self.total, self.before], ["sent"])
        self.far = shifted(sent, self.pairs, self.reach + 1)
        self.reach = 2 * self.reach + 1

    def extend(self):
        while self.reach < self.pairs - 1:
            (self.before,) = self.line.run(join, extend_kernel, "extend", None, [self.before, self.far], ["kept"])
            self.double()

    def finish(self):
        self.extend()
        self.mine, sent = self.line.run(
            join, last_kernel, "last", self.where, [self.before, self.far, self.kept, self.got], ["state", "state"]
        )
        self.other = swapped(sent, self.pairs)


def shards(
    features, gates, state_io, step_size, log_decay, conv_feat, conv_state, skip_gain, norm_gain
):
    tokens, channels = features.shape
    heads = step_size.shape[0]
    head_dim = channels // heads
    groups = state_io.shape[2] // STATE
    group_width = channels // groups
    width = group_width // 2
    count = conv_feat.shape[0]
    rim = count - 1
    ctx_size = lax.axis_size("ctx")
    head_size = lax.axis_size("head")
    pairs = ctx_size // 2
    rows = tokens // head_size
    me = lax.axis_index("head").astype(jnp.int32)
    where = jnp.stack([me, lax.axis_index("ctx").astype(jnp.int32) % 2])

    onward = [(i, i + 1) for i in range(ctx_size - 1)]
    pad = HALO - rim
    halo = jnp.pad(lax.ppermute(features[tokens - rim :], "ctx", onward), ((pad, 0), (0, 0)))
    io_halo = jnp.pad(lax.ppermute(state_io[tokens - rim :], "ctx", onward), ((pad, 0), (0, 0), (0, 0)))
    spread = jnp.asarray(spread_table(heads, head_dim), BF16)
    halves = jnp.asarray(np.arange(128)[None, :] // head_dim == np.arange(2)[:, None], BF16)
    col, row, loc, dev, ecum, edev, skips = decay_tables(log_decay, step_size, skip_gain)
    gain_row = norm_gain[None]

    line = Line()
    chunks = [(c * width, width) for c in range(2 * groups)]
    fronts = {}
    maps = {}
    exchanges = {}
    ys = {}

    def run_maps(g):
        maps[g] = line.run(maps_of, g, state_io, io_halo, conv_state)

    def run_front(c):
        made = line.run(
            front, chunks[c], where, features, halo, conv_feat, dev, edev, spread, maps[c // 2][2]
        )
        fronts[c] = made[0]
        exchanges[c] = Exchange(line, where, pairs, made[1], made[2])

    def run_spans(c):
        g = c // 2
        ys[c] = line.run(
            spans_of, chunks[c], head_dim, fronts[c], *maps[g][:2], col, row, loc, ecum, spread, skips, halves
        )

    def part(c):
        return (chunks[c], ys[c], exchanges[c].mine, exchanges[c].other)

    partners = list(range(head_size - 1, 1, -1))
    squares = {}
    pieces = {}

    def ship(piece, r):
        return lax.ppermute(piece, "head", [(i, i ^ r) for i in range(head_size)])

    def run_back(mode, some, g, parts, squares, own=None):
        return line.run(
            back, mode, some, where, rows, [part(c) for c in parts], maps[g][1], edev, spread, gates, gain_row,
            squares, own=own,
        )

    def arrived(g, index):
        line.last += [pieces[g, r][index] for r in partners]

    def run_first(g, apart=False):
        squares[g] = []
        for some in [[r] for r in partners] if apart else [partners]:
            *made, square = run_back("first", some, g, [2 * g], None)
            squares[g].append((some, square))
            for r, piece in zip(some, made):
                pieces[g, r] = [ship(piece, r)]

    def run_rest(g):
        for some, square in squares[g]:
            made = run_back("rest", some, g, [2 * g + 1], square)
            for r, piece in zip(some, made):
                pieces[g, r].append(ship(piece, r))

    result = None

    def run_near(g):
        nonlocal result
        made, result = run_back("whole", [1, 0], g, [2 * g, 2 * g + 1], None, own=(g, groups, result))
        pieces[g, 1] = [ship(made, 1)]

    def run_put(g, r):
        nonlocal result
        start = (me ^ r) * channels + g * group_width
        zero = jnp.int32(0)
        if len(pieces[g, r]) == 2:
            first, rest = pieces[g, r]
            scale = rest[rows, :rows].astype(F32) + rest[rows + 8, :rows].astype(F32)
            first = (first.astype(F32) * scale[:, None]).astype(BF16)
            result = lax.dynamic_update_slice(result, first, (zero, start))
            result = lax.dynamic_update_slice(result, rest[:rows], (zero, start + width))
        else:
            result = lax.dynamic_update_slice(result, pieces[g, r][0], (zero, start))

    ex = exchanges
    if groups == 2:
        run_maps(0)
        run_front(0)
        run_front(1)
        ex[0].pair()
        run_maps(1)
        ex[0].double()
        ex[1].pair()
        run_front(2)
        run_spans(0)
        ex[0].finish()
        ex[1].double()
        ex[2].pair()
        run_first(0, apart=True)
        run_spans(1)
        ex[1].finish()
        ex[2].double()
        run_front(3)
        arrived(0, 0)
        run_rest(0)
        ex[3].pair()
        run_spans(2)
        ex[2].finish()
        ex[3].double()
        run_spans(3)
        arrived(0, 1)
        run_first(1)
        ex[3].finish()
        arrived(1, 0)
        run_rest(1)
        run_near(0)
        run_near(1)
    else:
        for c in range(2 * groups):
            if c % 2 == 0:
                run_maps(c // 2)
            run_front(c)
            ex[c].pair()
        for c in range(2 * groups):
            ex[c].double()
            run_spans(c)
        for c in range(2 * groups):
            ex[c].finish()
        for g in range(groups):
            run_first(g)
            run_rest(g)
            run_near(g)
    for g in range(groups):
        for r in [1, *partners]:
            run_put(g, r)
    return result


def solution(mesh):
    in_specs = (
        P("ctx", "head"),
        P("ctx", "head"),
        P("ctx", None, "head"),
        P("head", "ctx"),
        P("head", "ctx"),
        P(None, "head"),
        P(None, None, "head"),
        P("head"),
        P("head"),
    )
    out_specs = P(("ctx", "head"), None)
    return jax.shard_map(shards, mesh=mesh, in_specs=in_specs, out_specs=out_specs, check_vma=False)
```

```python
import functools

import jax
import jax.numpy as jnp
import numpy as np
from jax import lax
from jax.experimental import pallas as pl
from jax.experimental.pallas import tpu as pltpu
from jax.sharding import PartitionSpec as P

STATE = 256
SPAN = 128
HALO = 16
EPS = 1e-05
F32 = jnp.float32
BF16 = jnp.bfloat16
VMEM_BYTES = 63 * 1024 * 1024
COST_SCALE = 10**9
MSG = STATE + 16
KEPT = STATE + 8


def dot(a, b):
    return jnp.dot(a, b, preferred_element_type=F32)


def silu(v):
    half = 0.5 * v
    return half * jnp.tanh(half) + half


def cost(micros):
    return pl.CostEstimate(flops=int(micros * COST_SCALE), bytes_accessed=1, transcendentals=0)


def params(limit=VMEM_BYTES):
    return pltpu.CompilerParams(vmem_limit_bytes=limit)


def spread_table(heads, head_dim):
    head = np.arange(2 * heads) % heads
    return (head[:, None] == (np.arange(heads * head_dim) // head_dim)[None, :]).astype(np.float32)


def decay_kernel(log_ref, step_ref, skip_ref, col_ref, row_ref, loc_ref, dev_ref, ecum_ref, edev_ref, skips_ref):
    heads, tokens = log_ref.shape
    spans = tokens // SPAN
    r = lax.broadcasted_iota(jnp.int32, (SPAN, SPAN), 0)
    c = lax.broadcasted_iota(jnp.int32, (SPAN, SPAN), 1)
    upper = (r <= c).astype(F32)
    cums = []
    for k in range(spans):
        cums.append(
            jnp.dot(
                log_ref[:, k * SPAN : (k + 1) * SPAN],
                upper,
                precision=lax.Precision.HIGHEST,
                preferred_element_type=F32,
            )
        )
    totals = [cum[:, SPAN - 1 :] for cum in cums]
    before = [jnp.zeros_like(totals[0])]
    for k in range(spans - 1):
        before.append(before[-1] + totals[k])
    after = [jnp.zeros_like(totals[0])]
    for k in range(spans - 1, 0, -1):
        after.insert(0, after[0] + totals[k])

    def put(ref, k, value):
        high = value.astype(BF16).astype(F32)
        both = jnp.concatenate([high, value - high], axis=0)
        ref[k * SPAN : (k + 1) * SPAN, :] = both.T.astype(BF16)

    skip = skip_ref[...]
    high = skip.astype(BF16).astype(F32)
    parts = jnp.concatenate([high, skip - high], axis=1)
    skips_ref[...] = jnp.broadcast_to(parts, skips_ref.shape).astype(BF16)
    for k in range(spans):
        cum = cums[k]
        step = step_ref[:, k * SPAN : (k + 1) * SPAN]
        col_ref[k * SPAN : (k + 1) * SPAN, :] = jnp.concatenate([cum, cum], axis=0).T
        row_ref[:, k * SPAN : (k + 1) * SPAN] = cum - jnp.log(step)
        to_end = totals[k] - cum
        put(loc_ref, k, jnp.exp(to_end) * step)
        put(dev_ref, k, jnp.exp(to_end + after[k]) * step)
        put(ecum_ref, k, jnp.exp(cum))
        put(edev_ref, k, jnp.exp(cum + before[k]))


def behind(count):
    return [pl.BlockSpec(memory_space=pl.ANY)] * count


def decay_tables(log_decay, step_size, skip_gain):
    heads, tokens = log_decay.shape
    wide = jax.ShapeDtypeStruct((tokens, 2 * heads), BF16)
    return pl.pallas_call(
        decay_kernel,
        out_shape=(
            jax.ShapeDtypeStruct((tokens, 2 * heads), F32),
            jax.ShapeDtypeStruct((heads, tokens), F32),
            wide,
            wide,
            wide,
            wide,
            jax.ShapeDtypeStruct((16, 2 * heads), BF16),
        ),
        compiler_params=params(),
        name="decays",
        cost_estimate=cost(1.5),
    )(log_decay, step_size, skip_gain[None])


def conv_rows(read, rows, halo, taps, store):
    count = taps.shape[0]
    for b in range(rows // SPAN):
        own = read(b * SPAN, (b + 1) * SPAN).astype(F32)
        prev = (halo if b == 0 else read(b * SPAN - HALO, b * SPAN)).astype(F32)
        both = jnp.concatenate([prev[HALO - 8 :], own], axis=0)
        total = own * taps[count - 1 : count]
        for k in range(1, count):
            total = total + both[8 - k : 8 - k + SPAN] * taps[count - 1 - k : count - k]
        store(b, silu(total).astype(BF16))


def read_state(ref):
    if ref.dtype == F32:
        return ref[:STATE, :], ref[STATE : STATE + 1, :]
    tail = ref[STATE:MSG, :].astype(F32)
    return ref[:STATE, :].astype(F32), tail[0:1] + tail[8:9]


def write_kept(ref, value, decay):
    ref[:STATE, :] = value
    ref[STATE:KEPT, :] = jnp.broadcast_to(decay, (KEPT - STATE, decay.shape[1]))


def write_sent(ref, value, decay):
    ref[:STATE, :] = value.astype(BF16)
    high = decay.astype(BF16).astype(F32)
    shape = (8, decay.shape[1])
    rows = jnp.concatenate([jnp.broadcast_to(high, shape), jnp.broadcast_to(decay - high, shape)], axis=0)
    ref[STATE:MSG, :] = rows.astype(BF16)


def maps_kernel(order, io_ref, halo_ref, taps_ref, *refs):
    in_map_ref, out_map_ref, turned_ref = refs[order:]

    def put_in(b, value):
        in_map_ref[b * SPAN : (b + 1) * SPAN, :] = value
        turned_ref[:, b * SPAN : (b + 1) * SPAN] = value.T

    def put_out(b, value):
        out_map_ref[b * SPAN : (b + 1) * SPAN, :] = value

    for i, put in ((0, put_in), (1, put_out)):
        conv_rows(
            lambda lo, hi: io_ref[lo:hi, i, :], io_ref.shape[0], halo_ref[:, i, :],
            taps_ref[:, i, :].astype(F32), put,
        )


def maps_of(group, state_io, halo, conv_state, after):
    tokens = state_io.shape[0]
    count = conv_state.shape[0]

    def mine(j):
        return (0, 0, group)

    return pl.pallas_call(
        functools.partial(maps_kernel, len(after)),
        grid=(1,),
        in_specs=[
            pl.BlockSpec((tokens, 2, STATE), mine),
            pl.BlockSpec((HALO, 2, STATE), mine),
            pl.BlockSpec((count, 2, STATE), mine),
            *behind(len(after)),
        ],
        out_specs=[
            pl.BlockSpec((tokens, STATE), lambda j: (0, 0)),
            pl.BlockSpec((tokens, STATE), lambda j: (0, 0)),
            pl.BlockSpec((STATE, tokens), lambda j: (0, 0)),
        ],
        out_shape=[
            jax.ShapeDtypeStruct((tokens, STATE), BF16),
            jax.ShapeDtypeStruct((tokens, STATE), BF16),
            jax.ShapeDtypeStruct((STATE, tokens), BF16),
        ],
        compiler_params=params(),
        name="maps",
        cost_estimate=cost(3),
    )(state_io, halo, conv_state, *after)


def front_kernel(order, blocks, where_ref, feat_ref, halo_ref, taps_ref, dev_ref, edev_ref, spread_ref, turned_ref, *refs):
    xh_ref, sent_ref, kept_ref, scaled = refs[order:]
    j = pl.program_id(0)
    spread = spread_ref[...]

    def put_feat(b, value):
        rows = slice(b * SPAN, (b + 1) * SPAN)
        xh_ref[rows, :] = value
        scaled[rows, :] = (value.astype(F32) * dot(dev_ref[rows, :], spread)).astype(BF16)

    conv_rows(
        lambda lo, hi: feat_ref[lo:hi, :], feat_ref.shape[0], halo_ref[...], taps_ref[...].astype(F32), put_feat
    )
    state = dot(turned_ref[...], scaled[...])
    decay = dot(edev_ref[...], spread)[15:16]

    @pl.when(j < blocks)
    def _():
        write_sent(sent_ref, state, decay)

    @pl.when(j >= blocks)
    def _():
        write_kept(kept_ref, state, decay)


def front(chunk, where, features, halo, conv_feat, dev, edev, spread, turned, after):
    tokens = features.shape[0]
    start, width = chunk
    half = width // 2
    block = min(512, half)
    blocks = half // block
    base = start // block
    count = conv_feat.shape[0]
    heads2 = dev.shape[1]

    def place(j, where):
        sending = (j < blocks).astype(jnp.int32)
        which = sending * (1 - where[1]) + (1 - sending) * where[1]
        return which * blocks + j - (1 - sending) * blocks

    def cols(j, where):
        return (0, base + place(j, where))

    def same(j, where):
        return (0, 0)

    return pl.pallas_call(
        functools.partial(front_kernel, len(after), blocks),
        grid_spec=pltpu.PrefetchScalarGridSpec(
            num_scalar_prefetch=1,
            grid=(2 * blocks,),
            in_specs=[
                pl.BlockSpec((tokens, block), cols),
                pl.BlockSpec((HALO, block), cols),
                pl.BlockSpec((count, block), cols),
                pl.BlockSpec((tokens, heads2), same),
                pl.BlockSpec((16, heads2), lambda j, where: (tokens // 16 - 1, 0)),
                pl.BlockSpec((heads2, block), cols),
                pl.BlockSpec((STATE, tokens), same),
                *behind(len(after)),
            ],
            out_specs=[
                pl.BlockSpec((tokens, block), lambda j, where: (0, place(j, where))),
                pl.BlockSpec((MSG, block), lambda j, where: (0, jnp.minimum(j, blocks - 1))),
                pl.BlockSpec((KEPT, block), lambda j, where: (0, jnp.maximum(j - blocks, 0))),
            ],
            scratch_shapes=[pltpu.VMEM((tokens, block), BF16)],
        ),
        out_shape=[
            jax.ShapeDtypeStruct((tokens, width), BF16),
            jax.ShapeDtypeStruct((MSG, half), BF16),
            jax.ShapeDtypeStruct((KEPT, half), F32),
        ],
        compiler_params=params(),
        name="front",
        cost_estimate=cost(3),
    )(where, features, halo, conv_feat, dev, edev, spread, turned, *after)


def span_kernel(
    first_head, order, xh_ref, in_ref, out_ref, col_ref, row_ref, loc_ref, ecum_ref, spread_ref, skips_ref, halves_ref,
    *refs,
):
    y_ref, state = refs[order:]
    width = xh_ref.shape[1]
    head_dim = width // row_ref.shape[0]

    @pl.when(pl.program_id(0) == 0)
    def _():
        state[...] = jnp.zeros_like(state)

    t = lax.broadcasted_iota(jnp.int32, (SPAN, SPAN), 0)
    s = lax.broadcasted_iota(jnp.int32, (SPAN, SPAN), 1)
    first = halves_ref[0:1, :]
    second = halves_ref[1:2, :]
    block = 256
    for k in range(xh_ref.shape[0] // SPAN):
        rows = slice(k * SPAN, (k + 1) * SPAN)
        in_map = in_ref[rows, :]
        out_map = out_ref[rows, :]
        scores = lax.dot_general(out_map, in_map, (((1,), (1,)), ((), ())), preferred_element_type=F32)
        scores = jnp.where(s <= t, scores, 0.0)
        in_turned = in_map.T
        tables = jnp.concatenate([loc_ref[rows, :], ecum_ref[rows, :], skips_ref[...]], axis=0)
        for q in range(width // block):
            cols = slice(q * block, (q + 1) * block)
            feats = xh_ref[rows, cols]
            feats32 = feats.astype(F32)
            wide = dot(tables, spread_ref[:, cols])
            scaled = (feats32 * wide[:SPAN]).astype(BF16)
            ecum = wide[SPAN : 2 * SPAN]
            skip = wide[2 * SPAN : 2 * SPAN + 1]
            pairs = []
            for p in range(block // 128):
                weights = []
                for i in range(2):
                    h = (q * block + p * 128) // head_dim + i
                    gap = col_ref[rows, first_head + h : first_head + h + 1] - row_ref[h : h + 1, rows]
                    weights.append((scores * jnp.exp(jnp.minimum(gap, 0.0))).astype(BF16))
                pair = feats[:, p * 128 : (p + 1) * 128]
                stacked = jnp.concatenate([pair * first, pair * second], axis=0)
                pairs.append(dot(jnp.concatenate(weights, axis=1), stacked))
            diag = jnp.concatenate(pairs, axis=1)
            held = state[:, cols]
            carried = dot(out_map, held.astype(BF16)) * ecum
            y_ref[rows, cols] = diag + carried + skip * feats32
            state[:, cols] = ecum[SPAN - 1 :] * held + dot(in_turned, scaled)


def spans_of(chunk, head_dim, xh, in_map, out_map, col, row, loc, ecum, spread, skips, halves, after):
    tokens, width = xh.shape
    index = chunk[0] // width
    some = width // head_dim
    heads2 = loc.shape[1]
    tile = 2 * SPAN
    return pl.pallas_call(
        functools.partial(span_kernel, index * some, len(after)),
        grid=(tokens // tile,),
        in_specs=[
            pl.BlockSpec((tile, width), lambda k: (k, 0)),
            pl.BlockSpec((tile, STATE), lambda k: (k, 0)),
            pl.BlockSpec((tile, STATE), lambda k: (k, 0)),
            pl.BlockSpec((tile, heads2), lambda k: (k, 0)),
            pl.BlockSpec((some, tile), lambda k: (index, k)),
            pl.BlockSpec((tile, heads2), lambda k: (k, 0)),
            pl.BlockSpec((tile, heads2), lambda k: (k, 0)),
            pl.BlockSpec((heads2, width), lambda k: (0, index)),
            pl.BlockSpec(skips.shape, lambda k: (0, 0)),
            pl.BlockSpec(halves.shape, lambda k: (0, 0)),
            *behind(len(after)),
        ],
        out_specs=pl.BlockSpec((tile, width), lambda k: (k, 0)),
        out_shape=jax.ShapeDtypeStruct((tokens, width), F32),
        scratch_shapes=[pltpu.VMEM((STATE, width), F32)],
        compiler_params=params(),
        name="spans",
        cost_estimate=cost(200),
    )(xh, in_map, out_map, col, row, loc, ecum, spread, skips, halves, *after)


def pair_kernel(where_ref, kept_ref, got_ref, *refs):
    total_ref, sent_ref = refs[-2:]
    kept, kept_decay = read_state(kept_ref)
    got, got_decay = read_state(got_ref)

    def put(first, second, decay):
        total = decay * first + second
        write_kept(total_ref, total, kept_decay * got_decay)
        write_sent(sent_ref, total, kept_decay * got_decay)

    @pl.when(where_ref[1] == 0)
    def _():
        put(kept, got, got_decay)

    @pl.when(where_ref[1] == 1)
    def _():
        put(got, kept, kept_decay)


def inclusive_kernel(total_ref, before_ref, *refs):
    sent_ref = refs[-1]
    total, decay = read_state(total_ref)
    before, before_decay = read_state(before_ref)
    write_sent(sent_ref, total + decay * before, decay * before_decay)


def extend_kernel(before_ref, far_ref, *refs):
    before, decay = read_state(before_ref)
    far, far_decay = read_state(far_ref)
    write_kept(refs[-1], before + decay * far, decay * far_decay)


def last_kernel(where_ref, before_ref, far_ref, kept_ref, got_ref, *refs):
    mine_ref, sent_ref = refs[-2:]
    before, before_decay = read_state(before_ref)
    far, _ = read_state(far_ref)
    carried = before + before_decay * far

    @pl.when(where_ref[1] == 0)
    def _():
        kept, decay = read_state(kept_ref)
        mine_ref[...] = carried.astype(BF16)
        sent_ref[...] = (decay * carried + kept).astype(BF16)

    @pl.when(where_ref[1] == 1)
    def _():
        got, decay = read_state(got_ref)
        mine_ref[...] = (decay * carried + got).astype(BF16)
        sent_ref[...] = carried.astype(BF16)


def join(kernel, name, where, operands, outs, after):
    width = operands[0].shape[1]
    block = min(256, width)
    shapes = {
        "kept": jax.ShapeDtypeStruct((KEPT, width), F32),
        "sent": jax.ShapeDtypeStruct((MSG, width), BF16),
        "state": jax.ShapeDtypeStruct((STATE, width), BF16),
    }
    scalars = [] if where is None else [where]

    def part(rows):
        return pl.BlockSpec((rows, block), lambda j, *_: (0, j))

    return pl.pallas_call(
        kernel,
        grid_spec=pltpu.PrefetchScalarGridSpec(
            num_scalar_prefetch=len(scalars),
            grid=(width // block,),
            in_specs=[part(operand.shape[0]) for operand in operands] + behind(len(after)),
            out_specs=[part(shapes[out].shape[0]) for out in outs],
        ),
        out_shape=[shapes[out] for out in outs],
        compiler_params=params(),
        name=name,
        cost_estimate=cost(0.7),
    )(*scalars, *operands, *after)


def back_kernel(mode, count, partners, order, where_ref, out_ref, edev_ref, *refs):
    chunks = [refs[6 * i : 6 * i + 6] for i in range(count)]
    refs = refs[6 * count :]
    if mode == "rest":
        squares_ref, *refs = refs
    refs = refs[order:]
    o_refs = refs[:partners]
    if mode == "first":
        squares_ref = refs[partners]
    gated = refs[-1]
    out_map = out_ref[...]
    edev = edev_ref[...]
    rows = out_map.shape[0]
    block = 256
    steps = pl.num_programs(0) // partners
    odd = where_ref[1] == 1
    squares = squares_ref[...] if mode == "rest" else jnp.zeros((rows, 128), F32)
    at = 0
    for y_ref, mine_ref, other_ref, spread_ref, gate_ref, gain_ref in chunks:
        half = mine_ref.shape[1]
        for q in range(2 * half // block):
            cols = slice(q * block, (q + 1) * block)
            inner = slice(q * block % half, q * block % half + block)
            mine = mine_ref[:, inner]
            other = other_ref[:, inner]
            state = jnp.where(odd, other, mine) if q * block < half else jnp.where(odd, mine, other)
            carried = dot(out_map, state) * dot(edev, spread_ref[:, cols])
            value = (y_ref[:, cols] + carried) * silu(gate_ref[:, cols].astype(F32))
            square = value * value
            squares = squares + square[:, :128] + square[:, 128:]
            gated[:, at : at + block] = value * gain_ref[:, cols]
            at += block
    if mode == "first":
        squares_ref[...] = squares
    else:
        width = at if mode == "whole" else 2 * at
        mean = jnp.sum(squares, axis=1, keepdims=True) * (1.0 / width)
        scale = lax.rsqrt(mean + EPS)
    for p in range(partners):

        @pl.when(pl.program_id(0) // steps == p)
        def _(o_ref=o_refs[p]):
            if mode == "rest":
                step = pl.program_id(0) - p * steps
                start = pl.multiple_of(step * rows, rows)
                high = scale.astype(BF16).astype(F32)
                parts = [jnp.broadcast_to(part, (rows, 128)).T[:8] for part in (high, scale - high)]
                o_ref[steps * rows :, pl.ds(start, rows)] = jnp.concatenate(parts, axis=0).astype(BF16)
            for q in range(at // block):
                cols = slice(q * block, (q + 1) * block)
                value = gated[:, cols] if mode == "first" else gated[:, cols] * scale
                if mode == "rest":
                    o_ref[pl.ds(start, rows), cols] = value.astype(BF16)
                else:
                    o_ref[:, cols] = value.astype(BF16)


def back(mode, some, where, rows, chunks, out_map, edev, spread, gates, gain_row, squares, after, own=None):
    heads2 = edev.shape[1]
    tile = 128
    steps = rows // tile
    partners = len(some)

    def at(i, where):
        turn = some[0]
        for p in range(1, partners):
            turn = jnp.where(i >= p * steps, some[p], turn)
        return ((where[0] ^ turn) * steps + i % steps, 0)

    specs = [pl.BlockSpec((tile, STATE), at), pl.BlockSpec((tile, heads2), at)]
    operands = [out_map, edev]
    total = 0
    for (start, width), y, mine, other in chunks:
        index = start // width
        half = width // 2
        total += width
        specs += [
            pl.BlockSpec((tile, width), at),
            pl.BlockSpec((STATE, half), lambda i, where: (0, 0)),
            pl.BlockSpec((STATE, half), lambda i, where: (0, 0)),
            pl.BlockSpec((heads2, width), lambda i, where, index=index: (0, index)),
            pl.BlockSpec((tile, width), lambda i, where, index=index: (at(i, where)[0], index)),
            pl.BlockSpec((1, width), lambda i, where, index=index: (0, index)),
        ]
        operands += [y, mine, other, spread, gates, gain_row]
    if mode == "rest":
        specs.append(pl.BlockSpec((tile, 128), lambda i, where: (i, 0)))
        operands.append(squares)
    aliases = {}
    if own is not None and own[2] is not None:
        after = [own[2], *after]
        aliases = {1 + len(operands): partners - 1}
    specs += behind(len(after))
    operands += after
    sent = rows + 16 if mode == "rest" else rows
    part = sent if mode == "rest" else tile

    def part_of(p):
        if mode == "rest":
            return lambda i, where: (0, 0)
        return lambda i, where: (jnp.clip(i - p * steps, 0, steps - 1), 0)

    out_specs = [pl.BlockSpec((part, total), part_of(p)) for p in range(partners)]
    out_shape = [jax.ShapeDtypeStruct((sent, total), BF16)] * partners
    if own is not None:
        group, groups, _ = own
        out_specs[-1] = pl.BlockSpec(
            (tile, total),
            lambda i, where: (jnp.clip(i - (partners - 1) * steps, 0, steps - 1), (where[0] ^ some[-1]) * groups + group),
        )
        out_shape[-1] = jax.ShapeDtypeStruct((rows, groups * total * (gates.shape[0] // rows)), BF16)
    if mode == "first":
        out_specs.append(pl.BlockSpec((tile, 128), lambda i, where: (i, 0)))
        out_shape.append(jax.ShapeDtypeStruct((partners * rows, 128), F32))
    return pl.pallas_call(
        functools.partial(back_kernel, mode, len(chunks), partners, len(after)),
        grid_spec=pltpu.PrefetchScalarGridSpec(
            num_scalar_prefetch=1,
            grid=(partners * steps,),
            in_specs=specs,
            out_specs=out_specs,
            scratch_shapes=[pltpu.VMEM((tile, total), F32)],
        ),
        out_shape=out_shape,
        input_output_aliases=aliases,
        compiler_params=params(),
        name=f"back_{mode}",
        cost_estimate=cost(1),
    )(where, *operands)


def shifted(value, pairs, steps):
    return lax.ppermute(
        value,
        "ctx",
        [(2 * q + y, 2 * (q + steps) + y) for q in range(pairs - steps) for y in range(2)],
    )


def swapped(value, pairs):
    return lax.ppermute(value, "ctx", [(2 * q + y, 2 * q + 1 - y) for q in range(pairs) for y in range(2)])


class Line:
    def __init__(self):
        self.last = []

    def run(self, make, *args, **kwargs):
        made = make(*args, after=self.last, **kwargs)
        self.last = [made[0] if isinstance(made, (list, tuple)) else made]
        return made


class Exchange:
    def __init__(self, line, where, pairs, sent, kept):
        self.line = line
        self.where = where
        self.pairs = pairs
        self.kept = kept
        self.got = swapped(sent, pairs)

    def pair(self):
        self.total, sent = self.line.run(
            join, pair_kernel, "pair", self.where, [self.kept, self.got], ["kept", "sent"]
        )
        self.before = shifted(sent, self.pairs, 1)
        self.reach = 1

    def double(self):
        (sent,) = self.line.run(join, inclusive_kernel, "inclusive", None, [self.total, self.before], ["sent"])
        self.far = shifted(sent, self.pairs, self.reach + 1)
        self.reach = 2 * self.reach + 1

    def extend(self):
        while self.reach < self.pairs - 1:
            (self.before,) = self.line.run(join, extend_kernel, "extend", None, [self.before, self.far], ["kept"])
            self.double()

    def finish(self):
        self.extend()
        self.mine, sent = self.line.run(
            join, last_kernel, "last", self.where, [self.before, self.far, self.kept, self.got], ["state", "state"]
        )
        self.other = swapped(sent, self.pairs)


def shards(
    features, gates, state_io, step_size, log_decay, conv_feat, conv_state, skip_gain, norm_gain
):
    tokens, channels = features.shape
    heads = step_size.shape[0]
    head_dim = channels // heads
    groups = state_io.shape[2] // STATE
    group_width = channels // groups
    width = group_width // 2
    count = conv_feat.shape[0]
    rim = count - 1
    ctx_size = lax.axis_size("ctx")
    head_size = lax.axis_size("head")
    pairs = ctx_size // 2
    rows = tokens // head_size
    me = lax.axis_index("head").astype(jnp.int32)
    where = jnp.stack([me, lax.axis_index("ctx").astype(jnp.int32) % 2])

    onward = [(i, i + 1) for i in range(ctx_size - 1)]
    pad = HALO - rim
    halo = jnp.pad(lax.ppermute(features[tokens - rim :], "ctx", onward), ((pad, 0), (0, 0)))
    io_halo = jnp.pad(lax.ppermute(state_io[tokens - rim :], "ctx", onward), ((pad, 0), (0, 0), (0, 0)))
    spread = jnp.asarray(spread_table(heads, head_dim), BF16)
    halves = jnp.asarray(np.arange(128)[None, :] // head_dim == np.arange(2)[:, None], BF16)
    col, row, loc, dev, ecum, edev, skips = decay_tables(log_decay, step_size, skip_gain)
    gain_row = norm_gain[None]

    line = Line()
    chunks = [(c * width, width) for c in range(2 * groups)]
    fronts = {}
    maps = {}
    exchanges = {}
    ys = {}

    def run_maps(g):
        maps[g] = line.run(maps_of, g, state_io, io_halo, conv_state)

    def run_front(c):
        made = line.run(
            front, chunks[c], where, features, halo, conv_feat, dev, edev, spread, maps[c // 2][2]
        )
        fronts[c] = made[0]
        exchanges[c] = Exchange(line, where, pairs, made[1], made[2])

    def run_spans(c):
        g = c // 2
        ys[c] = line.run(
            spans_of, chunks[c], head_dim, fronts[c], *maps[g][:2], col, row, loc, ecum, spread, skips, halves
        )

    def part(c):
        return (chunks[c], ys[c], exchanges[c].mine, exchanges[c].other)

    partners = list(range(head_size - 1, 1, -1))
    squares = {}
    pieces = {}

    def ship(piece, r):
        return lax.ppermute(piece, "head", [(i, i ^ r) for i in range(head_size)])

    def run_back(mode, some, g, parts, squares, own=None):
        return line.run(
            back, mode, some, where, rows, [part(c) for c in parts], maps[g][1], edev, spread, gates, gain_row,
            squares, own=own,
        )

    def arrived(g, index):
        line.last += [pieces[g, r][index] for r in partners]

    def run_first(g, apart=False):
        squares[g] = []
        for some in [[r] for r in partners] if apart else [partners]:
            *made, square = run_back("first", some, g, [2 * g], None)
            squares[g].append((some, square))
            for r, piece in zip(some, made):
                pieces[g, r] = [ship(piece, r)]

    def run_rest(g):
        for some, square in squares[g]:
            made = run_back("rest", some, g, [2 * g + 1], square)
            for r, piece in zip(some, made):
                pieces[g, r].append(ship(piece, r))

    result = None

    def run_near(g):
        nonlocal result
        made, result = run_back("whole", [1, 0], g, [2 * g, 2 * g + 1], None, own=(g, groups, result))
        pieces[g, 1] = [ship(made, 1)]

    def run_put(g, r):
        nonlocal result
        start = (me ^ r) * channels + g * group_width
        zero = jnp.int32(0)
        if len(pieces[g, r]) == 2:
            first, rest = pieces[g, r]
            scale = rest[rows, :rows].astype(F32) + rest[rows + 8, :rows].astype(F32)
            first = (first.astype(F32) * scale[:, None]).astype(BF16)
            result = lax.dynamic_update_slice(result, first, (zero, start))
            result = lax.dynamic_update_slice(result, rest[:rows], (zero, start + width))
        else:
            result = lax.dynamic_update_slice(result, pieces[g, r][0], (zero, start))

    ex = exchanges
    if groups == 2:
        run_maps(0)
        run_front(0)
        run_front(1)
        ex[0].pair()
        run_maps(1)
        ex[0].double()
        ex[1].pair()
        run_front(2)
        run_spans(0)
        ex[0].finish()
        ex[1].double()
        ex[2].pair()
        run_first(0, apart=True)
        run_spans(1)
        ex[2].double()
        ex[1].finish()
        run_front(3)
        arrived(0, 0)
        run_rest(0)
        ex[3].pair()
        run_spans(2)
        ex[3].double()
        ex[2].finish()
        run_spans(3)
        arrived(0, 1)
        run_first(1)
        ex[3].finish()
        arrived(1, 0)
        run_rest(1)
        run_near(0)
        for r in [*partners, 1]:
            run_put(0, r)
        run_near(1)
    else:
        for c in range(2 * groups):
            if c % 2 == 0:
                run_maps(c // 2)
            run_front(c)
            ex[c].pair()
        for c in range(2 * groups):
            ex[c].double()
            run_spans(c)
        for c in range(2 * groups):
            ex[c].finish()
        for g in range(groups):
            run_first(g)
            run_rest(g)
            run_near(g)
    if groups == 2:
        for r in [partners[0], 1, *partners[1:]]:
            run_put(1, r)
    else:
        for g in range(groups):
            for r in [1, *partners]:
                run_put(g, r)
    return result


def solution(mesh):
    in_specs = (
        P("ctx", "head"),
        P("ctx", "head"),
        P("ctx", None, "head"),
        P("head", "ctx"),
        P("head", "ctx"),
        P(None, "head"),
        P(None, None, "head"),
        P("head"),
        P("head"),
    )
    out_specs = P(("ctx", "head"), None)
    return jax.shard_map(shards, mesh=mesh, in_specs=in_specs, out_specs=out_specs, check_vma=False)
```

```python
import functools

import jax
import jax.numpy as jnp
import numpy as np
from jax import lax
from jax.experimental import pallas as pl
from jax.experimental.pallas import tpu as pltpu
from jax.sharding import PartitionSpec as P

STATE = 256
SPAN = 128
HALO = 16
EPS = 1e-05
F32 = jnp.float32
BF16 = jnp.bfloat16
VMEM_BYTES = 48 * 1024 * 1024
VMEM_SMALL = 8 * 1024 * 1024
COST_SCALE = 10**9
MSG = STATE + 16
KEPT = STATE + 8


def dot(a, b):
    return jnp.dot(a, b, preferred_element_type=F32)


def silu(v):
    half = 0.5 * v
    return half * jnp.tanh(half) + half


def cost(micros):
    return pl.CostEstimate(flops=int(micros * COST_SCALE), bytes_accessed=1, transcendentals=0)


def params(limit=VMEM_BYTES):
    return pltpu.CompilerParams(vmem_limit_bytes=limit)


def spread_table(heads, head_dim):
    head = np.arange(2 * heads) % heads
    return (head[:, None] == (np.arange(heads * head_dim) // head_dim)[None, :]).astype(np.float32)


def decay_kernel(log_ref, step_ref, skip_ref, col_ref, row_ref, loc_ref, dev_ref, ecum_ref, edev_ref, skips_ref):
    heads, tokens = log_ref.shape
    spans = tokens // SPAN
    r = lax.broadcasted_iota(jnp.int32, (SPAN, SPAN), 0)
    c = lax.broadcasted_iota(jnp.int32, (SPAN, SPAN), 1)
    upper = (r <= c).astype(F32)
    cums = []
    for k in range(spans):
        cums.append(
            jnp.dot(
                log_ref[:, k * SPAN : (k + 1) * SPAN],
                upper,
                precision=lax.Precision.HIGHEST,
                preferred_element_type=F32,
            )
        )
    totals = [cum[:, SPAN - 1 :] for cum in cums]
    before = [jnp.zeros_like(totals[0])]
    for k in range(spans - 1):
        before.append(before[-1] + totals[k])
    after = [jnp.zeros_like(totals[0])]
    for k in range(spans - 1, 0, -1):
        after.insert(0, after[0] + totals[k])

    def put(ref, k, value):
        high = value.astype(BF16).astype(F32)
        both = jnp.concatenate([high, value - high], axis=0)
        ref[k * SPAN : (k + 1) * SPAN, :] = both.T.astype(BF16)

    skip = skip_ref[...]
    high = skip.astype(BF16).astype(F32)
    parts = jnp.concatenate([high, skip - high], axis=1)
    skips_ref[...] = jnp.broadcast_to(parts, skips_ref.shape).astype(BF16)
    for k in range(spans):
        cum = cums[k]
        step = step_ref[:, k * SPAN : (k + 1) * SPAN]
        col_ref[k * SPAN : (k + 1) * SPAN, :] = jnp.concatenate([cum, cum], axis=0).T
        row_ref[:, k * SPAN : (k + 1) * SPAN] = cum - jnp.log(step)
        to_end = totals[k] - cum
        put(loc_ref, k, jnp.exp(to_end) * step)
        put(dev_ref, k, jnp.exp(to_end + after[k]) * step)
        put(ecum_ref, k, jnp.exp(cum))
        put(edev_ref, k, jnp.exp(cum + before[k]))


def behind(count):
    return [pl.BlockSpec(memory_space=pl.ANY)] * count


def decay_tables(log_decay, step_size, skip_gain):
    heads, tokens = log_decay.shape
    wide = jax.ShapeDtypeStruct((tokens, 2 * heads), BF16)
    return pl.pallas_call(
        decay_kernel,
        out_shape=(
            jax.ShapeDtypeStruct((tokens, 2 * heads), F32),
            jax.ShapeDtypeStruct((heads, tokens), F32),
            wide,
            wide,
            wide,
            wide,
            jax.ShapeDtypeStruct((16, 2 * heads), BF16),
        ),
        compiler_params=params(),
        name="decays",
        cost_estimate=cost(1.5),
    )(log_decay, step_size, skip_gain[None])


def conv_rows(read, rows, halo, taps, store):
    count, width = taps.shape
    tile = 64
    for b in range(rows // tile):
        for c in range(width // 128):
            cols = slice(c * 128, (c + 1) * 128)
            own = read(b * tile, (b + 1) * tile, cols).astype(F32)
            prev = (halo[:, cols] if b == 0 else read(b * tile - HALO, b * tile, cols)).astype(F32)
            both = jnp.concatenate([prev[HALO - 8 :], own], axis=0)
            total = own * taps[count - 1 : count, cols]
            for k in range(1, count):
                total = total + both[8 - k : 8 - k + tile] * taps[count - 1 - k : count - k, cols]
            store(slice(b * tile, (b + 1) * tile), cols, silu(total))


def read_state(ref):
    if ref.dtype == F32:
        return ref[:STATE, :], ref[STATE : STATE + 1, :]
    tail = ref[STATE:MSG, :].astype(F32)
    return ref[:STATE, :].astype(F32), tail[0:1] + tail[8:9]


def write_kept(ref, value, decay):
    ref[:STATE, :] = value
    ref[STATE:KEPT, :] = jnp.broadcast_to(decay, (KEPT - STATE, decay.shape[1]))


def write_sent(ref, value, decay):
    ref[:STATE, :] = value.astype(BF16)
    high = decay.astype(BF16).astype(F32)
    shape = (8, decay.shape[1])
    rows = jnp.concatenate([jnp.broadcast_to(high, shape), jnp.broadcast_to(decay - high, shape)], axis=0)
    ref[STATE:MSG, :] = rows.astype(BF16)


def maps_kernel(order, io_ref, halo_ref, taps_ref, *refs):
    in_map_ref, out_map_ref, turned_ref = refs[order:]

    def put_in(rows, cols, value):
        in_map_ref[rows, cols] = value.astype(BF16)

    def put_out(rows, cols, value):
        out_map_ref[rows, cols] = value.astype(BF16)

    tokens = io_ref.shape[0]
    for i, put in ((0, put_in), (1, put_out)):
        conv_rows(
            lambda lo, hi, cols: io_ref[lo:hi, i, cols], tokens, halo_ref[:, i, :], taps_ref[:, i, :].astype(F32), put
        )
    for b in range(tokens // SPAN):
        rows = slice(b * SPAN, (b + 1) * SPAN)
        turned_ref[:, rows] = in_map_ref[rows, :].T


def maps_of(group, state_io, halo, conv_state, after):
    tokens = state_io.shape[0]
    count = conv_state.shape[0]

    def mine(j):
        return (0, 0, group)

    return pl.pallas_call(
        functools.partial(maps_kernel, len(after)),
        grid=(1,),
        in_specs=[
            pl.BlockSpec((tokens, 2, STATE), mine),
            pl.BlockSpec((HALO, 2, STATE), mine),
            pl.BlockSpec((count, 2, STATE), mine),
            *behind(len(after)),
        ],
        out_specs=[
            pl.BlockSpec((tokens, STATE), lambda j: (0, 0)),
            pl.BlockSpec((tokens, STATE), lambda j: (0, 0)),
            pl.BlockSpec((STATE, tokens), lambda j: (0, 0)),
        ],
        out_shape=[
            jax.ShapeDtypeStruct((tokens, STATE), BF16),
            jax.ShapeDtypeStruct((tokens, STATE), BF16),
            jax.ShapeDtypeStruct((STATE, tokens), BF16),
        ],
        compiler_params=params(),
        name="maps",
        cost_estimate=cost(3),
    )(state_io, halo, conv_state, *after)


def front_kernel(order, blocks, where_ref, feat_ref, halo_ref, taps_ref, dev_ref, edev_ref, spread_ref, turned_ref, *refs):
    xh_ref, sent_ref, kept_ref, scaled, wide = refs[order:]
    j = pl.program_id(0)
    spread = spread_ref[...]
    wide[...] = dot(dev_ref[...], spread)

    def put_feat(rows, cols, value):
        value = value.astype(BF16)
        xh_ref[rows, cols] = value
        scaled[rows, cols] = (value.astype(F32) * wide[rows, cols]).astype(BF16)

    conv_rows(
        lambda lo, hi, cols: feat_ref[lo:hi, cols], feat_ref.shape[0], halo_ref[...], taps_ref[...].astype(F32), put_feat
    )
    state = dot(turned_ref[...], scaled[...])
    decay = dot(edev_ref[...], spread)[15:16]

    @pl.when(j < blocks)
    def _():
        write_sent(sent_ref, state, decay)

    @pl.when(j >= blocks)
    def _():
        write_kept(kept_ref, state, decay)


def front(chunk, where, features, halo, conv_feat, dev, edev, spread, turned, after):
    tokens = features.shape[0]
    start, width = chunk
    half = width // 2
    block = min(512, half)
    blocks = half // block
    base = start // block
    count = conv_feat.shape[0]
    heads2 = dev.shape[1]

    def place(j, where):
        sending = (j < blocks).astype(jnp.int32)
        which = sending * (1 - where[1]) + (1 - sending) * where[1]
        return which * blocks + j - (1 - sending) * blocks

    def cols(j, where):
        return (0, base + place(j, where))

    def same(j, where):
        return (0, 0)

    return pl.pallas_call(
        functools.partial(front_kernel, len(after), blocks),
        grid_spec=pltpu.PrefetchScalarGridSpec(
            num_scalar_prefetch=1,
            grid=(2 * blocks,),
            in_specs=[
                pl.BlockSpec((tokens, block), cols),
                pl.BlockSpec((HALO, block), cols),
                pl.BlockSpec((count, block), cols),
                pl.BlockSpec((tokens, heads2), same),
                pl.BlockSpec((16, heads2), lambda j, where: (tokens // 16 - 1, 0)),
                pl.BlockSpec((heads2, block), cols),
                pl.BlockSpec((STATE, tokens), same),
                *behind(len(after)),
            ],
            out_specs=[
                pl.BlockSpec((tokens, block), lambda j, where: (0, place(j, where))),
                pl.BlockSpec((MSG, block), lambda j, where: (0, jnp.minimum(j, blocks - 1))),
                pl.BlockSpec((KEPT, block), lambda j, where: (0, jnp.maximum(j - blocks, 0))),
            ],
            scratch_shapes=[pltpu.VMEM((tokens, block), BF16), pltpu.VMEM((tokens, block), F32)],
        ),
        out_shape=[
            jax.ShapeDtypeStruct((tokens, width), BF16),
            jax.ShapeDtypeStruct((MSG, half), BF16),
            jax.ShapeDtypeStruct((KEPT, half), F32),
        ],
        compiler_params=params(),
        name="front",
        cost_estimate=cost(4),
    )(where, features, halo, conv_feat, dev, edev, spread, turned, *after)


def span_kernel(
    first_head, order, xh_ref, in_ref, out_ref, col_ref, row_ref, loc_ref, ecum_ref, spread_ref, skips_ref, halves_ref,
    *refs,
):
    y_ref, state = refs[order:]
    width = xh_ref.shape[1]
    head_dim = width // row_ref.shape[0]

    @pl.when(pl.program_id(0) == 0)
    def _():
        state[...] = jnp.zeros_like(state)

    t = lax.broadcasted_iota(jnp.int32, (SPAN, SPAN), 0)
    s = lax.broadcasted_iota(jnp.int32, (SPAN, SPAN), 1)
    first = halves_ref[0:1, :]
    second = halves_ref[1:2, :]
    block = 256
    for k in range(xh_ref.shape[0] // SPAN):
        rows = slice(k * SPAN, (k + 1) * SPAN)
        in_map = in_ref[rows, :]
        out_map = out_ref[rows, :]
        scores = lax.dot_general(out_map, in_map, (((1,), (1,)), ((), ())), preferred_element_type=F32)
        scores = jnp.where(s <= t, scores, 0.0)
        in_turned = in_map.T
        tables = jnp.concatenate([loc_ref[rows, :], ecum_ref[rows, :], skips_ref[...]], axis=0)
        for q in range(width // block):
            cols = slice(q * block, (q + 1) * block)
            feats = xh_ref[rows, cols]
            feats32 = feats.astype(F32)
            wide = dot(tables, spread_ref[:, cols])
            scaled = (feats32 * wide[:SPAN]).astype(BF16)
            ecum = wide[SPAN : 2 * SPAN]
            skip = wide[2 * SPAN : 2 * SPAN + 1]
            pairs = []
            for p in range(block // 128):
                weights = []
                for i in range(2):
                    h = (q * block + p * 128) // head_dim + i
                    gap = col_ref[rows, first_head + h : first_head + h + 1] - row_ref[h : h + 1, rows]
                    weights.append((scores * jnp.exp(jnp.minimum(gap, 0.0))).astype(BF16))
                pair = feats[:, p * 128 : (p + 1) * 128]
                stacked = jnp.concatenate([pair * first, pair * second], axis=0)
                pairs.append(dot(jnp.concatenate(weights, axis=1), stacked))
            diag = jnp.concatenate(pairs, axis=1)
            held = state[:, cols]
            carried = dot(out_map, held.astype(BF16)) * ecum
            y_ref[rows, cols] = (diag + carried + skip * feats32).astype(BF16)
            state[:, cols] = ecum[SPAN - 1 :] * held + dot(in_turned, scaled)


def spans_of(chunk, head_dim, xh, in_map, out_map, col, row, loc, ecum, spread, skips, halves, after):
    tokens, width = xh.shape
    index = chunk[0] // width
    some = width // head_dim
    heads2 = loc.shape[1]
    tile = 2 * SPAN
    return pl.pallas_call(
        functools.partial(span_kernel, index * some, len(after)),
        grid=(tokens // tile,),
        in_specs=[
            pl.BlockSpec((tile, width), lambda k: (k, 0)),
            pl.BlockSpec((tile, STATE), lambda k: (k, 0)),
            pl.BlockSpec((tile, STATE), lambda k: (k, 0)),
            pl.BlockSpec((tile, heads2), lambda k: (k, 0)),
            pl.BlockSpec((some, tile), lambda k: (index, k)),
            pl.BlockSpec((tile, heads2), lambda k: (k, 0)),
            pl.BlockSpec((tile, heads2), lambda k: (k, 0)),
            pl.BlockSpec((heads2, width), lambda k: (0, index)),
            pl.BlockSpec(skips.shape, lambda k: (0, 0)),
            pl.BlockSpec(halves.shape, lambda k: (0, 0)),
            *behind(len(after)),
        ],
        out_specs=pl.BlockSpec((tile, width), lambda k: (k, 0)),
        out_shape=jax.ShapeDtypeStruct((tokens, width), BF16),
        scratch_shapes=[pltpu.VMEM((STATE, width), F32)],
        compiler_params=params(),
        name="spans",
        cost_estimate=cost(200),
    )(xh, in_map, out_map, col, row, loc, ecum, spread, skips, halves, *after)


def pair_kernel(where_ref, kept_ref, got_ref, *refs):
    total_ref, sent_ref = refs[-2:]
    kept, kept_decay = read_state(kept_ref)
    got, got_decay = read_state(got_ref)

    def put(first, second, decay):
        total = decay * first + second
        write_kept(total_ref, total, kept_decay * got_decay)
        write_sent(sent_ref, total, kept_decay * got_decay)

    @pl.when(where_ref[1] == 0)
    def _():
        put(kept, got, got_decay)

    @pl.when(where_ref[1] == 1)
    def _():
        put(got, kept, kept_decay)


def inclusive_kernel(total_ref, before_ref, *refs):
    sent_ref = refs[-1]
    total, decay = read_state(total_ref)
    before, before_decay = read_state(before_ref)
    write_sent(sent_ref, total + decay * before, decay * before_decay)


def extend_kernel(before_ref, far_ref, *refs):
    before, decay = read_state(before_ref)
    far, far_decay = read_state(far_ref)
    write_kept(refs[-1], before + decay * far, decay * far_decay)


def last_kernel(where_ref, before_ref, far_ref, kept_ref, got_ref, *refs):
    mine_ref, sent_ref = refs[-2:]
    before, before_decay = read_state(before_ref)
    far, _ = read_state(far_ref)
    carried = before + before_decay * far

    @pl.when(where_ref[1] == 0)
    def _():
        kept, decay = read_state(kept_ref)
        mine_ref[...] = carried.astype(BF16)
        sent_ref[...] = (decay * carried + kept).astype(BF16)

    @pl.when(where_ref[1] == 1)
    def _():
        got, decay = read_state(got_ref)
        mine_ref[...] = (decay * carried + got).astype(BF16)
        sent_ref[...] = carried.astype(BF16)


def join(kernel, name, where, operands, outs, after):
    width = operands[0].shape[1]
    shapes = {
        "kept": jax.ShapeDtypeStruct((KEPT, width), F32),
        "sent": jax.ShapeDtypeStruct((MSG, width), BF16),
        "state": jax.ShapeDtypeStruct((STATE, width), BF16),
    }
    scalars = [] if where is None else [where]
    return pl.pallas_call(
        kernel,
        in_specs=[pl.BlockSpec(memory_space=pltpu.SMEM)] * len(scalars)
        + [pl.BlockSpec(memory_space=pltpu.VMEM)] * len(operands)
        + behind(len(after)),
        out_specs=[pl.BlockSpec(memory_space=pltpu.VMEM)] * len(outs),
        out_shape=[shapes[out] for out in outs],
        compiler_params=params(VMEM_SMALL),
        name=name,
        cost_estimate=cost(0.7),
    )(*scalars, *operands, *after)


def back_kernel(mode, count, partners, order, where_ref, out_ref, edev_ref, *refs):
    chunks = [refs[6 * i : 6 * i + 6] for i in range(count)]
    refs = refs[6 * count :]
    if mode == "rest":
        squares_ref, *refs = refs
    refs = refs[order:]
    o_refs = refs[:partners]
    if mode == "first":
        squares_ref = refs[partners]
    gated, sums = refs[-2:]
    out_map = out_ref[...]
    edev = edev_ref[...]
    rows = out_map.shape[0]
    block = 256
    steps = pl.num_programs(0) // partners
    odd = where_ref[1] == 1
    sums[...] = squares_ref[...] if mode == "rest" else jnp.zeros((rows, 128), F32)
    at = 0
    for y_ref, mine_ref, other_ref, spread_ref, gate_ref, gain_ref in chunks:
        half = mine_ref.shape[1]
        for q in range(2 * half // block):
            cols = slice(q * block, (q + 1) * block)
            inner = slice(q * block % half, q * block % half + block)
            mine = mine_ref[:, inner]
            other = other_ref[:, inner]
            state = jnp.where(odd, other, mine) if q * block < half else jnp.where(odd, mine, other)
            gated[:, at : at + block] = dot(out_map, state) * dot(edev, spread_ref[:, cols])
            for c in range(block // 128):
                to = slice(at + c * 128, at + (c + 1) * 128)
                cols = slice(q * block + c * 128, q * block + (c + 1) * 128)
                gain = gain_ref[:, cols]
                for b in range(rows // 64):
                    part = slice(b * 64, (b + 1) * 64)
                    value = (y_ref[part, cols].astype(F32) + gated[part, to]) * silu(gate_ref[part, cols].astype(F32))
                    sums[part, :] = sums[part, :] + value * value
                    gated[part, to] = value * gain
            at += block
    if mode == "first":
        squares_ref[...] = sums[...]
    else:
        width = at if mode == "whole" else 2 * at
        mean = jnp.sum(sums[...], axis=1, keepdims=True) * (1.0 / width)
        scale = lax.rsqrt(mean + EPS)
    for p in range(partners):

        @pl.when(pl.program_id(0) // steps == p)
        def _(o_ref=o_refs[p]):
            if mode == "rest":
                step = pl.program_id(0) - p * steps
                start = pl.multiple_of(step * rows, rows)
                high = scale.astype(BF16).astype(F32)
                parts = [jnp.broadcast_to(part, (rows, 128)).T[:8] for part in (high, scale - high)]
                o_ref[steps * rows :, pl.ds(start, rows)] = jnp.concatenate(parts, axis=0).astype(BF16)
            for q in range(at // block):
                cols = slice(q * block, (q + 1) * block)
                value = gated[:, cols] if mode == "first" else gated[:, cols] * scale
                if mode == "rest":
                    o_ref[pl.ds(start, rows), cols] = value.astype(BF16)
                else:
                    o_ref[:, cols] = value.astype(BF16)


def back(mode, some, where, rows, chunks, out_map, edev, spread, gates, gain_row, squares, after, own=None):
    heads2 = edev.shape[1]
    tile = 128
    steps = rows // tile
    partners = len(some)

    def at(i, where):
        turn = some[0]
        for p in range(1, partners):
            turn = jnp.where(i >= p * steps, some[p], turn)
        return ((where[0] ^ turn) * steps + i % steps, 0)

    specs = [pl.BlockSpec((tile, STATE), at), pl.BlockSpec((tile, heads2), at)]
    operands = [out_map, edev]
    total = 0
    for (start, width), y, mine, other in chunks:
        index = start // width
        half = width // 2
        total += width
        specs += [
            pl.BlockSpec((tile, width), at),
            pl.BlockSpec((STATE, half), lambda i, where: (0, 0)),
            pl.BlockSpec((STATE, half), lambda i, where: (0, 0)),
            pl.BlockSpec((heads2, width), lambda i, where, index=index: (0, index)),
            pl.BlockSpec((tile, width), lambda i, where, index=index: (at(i, where)[0], index)),
            pl.BlockSpec((1, width), lambda i, where, index=index: (0, index)),
        ]
        operands += [y, mine, other, spread, gates, gain_row]
    if mode == "rest":
        specs.append(pl.BlockSpec((tile, 128), lambda i, where: (i, 0)))
        operands.append(squares)
    aliases = {}
    if own is not None and own[2] is not None:
        after = [own[2], *after]
        aliases = {1 + len(operands): partners - 1}
    specs += behind(len(after))
    operands += after
    sent = rows + 16 if mode == "rest" else rows
    part = sent if mode == "rest" else tile

    def part_of(p):
        if mode == "rest":
            return lambda i, where: (0, 0)
        return lambda i, where: (jnp.clip(i - p * steps, 0, steps - 1), 0)

    out_specs = [pl.BlockSpec((part, total), part_of(p)) for p in range(partners)]
    out_shape = [jax.ShapeDtypeStruct((sent, total), BF16)] * partners
    if own is not None:
        group, groups, _ = own
        out_specs[-1] = pl.BlockSpec(
            (tile, total),
            lambda i, where: (jnp.clip(i - (partners - 1) * steps, 0, steps - 1), (where[0] ^ some[-1]) * groups + group),
        )
        out_shape[-1] = jax.ShapeDtypeStruct((rows, groups * total * (gates.shape[0] // rows)), BF16)
    if mode == "first":
        out_specs.append(pl.BlockSpec((tile, 128), lambda i, where: (i, 0)))
        out_shape.append(jax.ShapeDtypeStruct((partners * rows, 128), F32))
    return pl.pallas_call(
        functools.partial(back_kernel, mode, len(chunks), partners, len(after)),
        grid_spec=pltpu.PrefetchScalarGridSpec(
            num_scalar_prefetch=1,
            grid=(partners * steps,),
            in_specs=specs,
            out_specs=out_specs,
            scratch_shapes=[pltpu.VMEM((tile, total), F32), pltpu.VMEM((tile, 128), F32)],
        ),
        out_shape=out_shape,
        input_output_aliases=aliases,
        compiler_params=params(),
        name=f"back_{mode}",
        cost_estimate=cost(1),
    )(where, *operands)


def shifted(value, pairs, steps):
    return lax.ppermute(
        value,
        "ctx",
        [(2 * q + y, 2 * (q + steps) + y) for q in range(pairs - steps) for y in range(2)],
    )


def swapped(value, pairs):
    return lax.ppermute(value, "ctx", [(2 * q + y, 2 * q + 1 - y) for q in range(pairs) for y in range(2)])


class Line:
    def __init__(self):
        self.last = []

    def run(self, make, *args, **kwargs):
        made = make(*args, after=self.last, **kwargs)
        self.last = [made[0] if isinstance(made, (list, tuple)) else made]
        return made


class Exchange:
    def __init__(self, line, where, pairs, sent, kept):
        self.line = line
        self.where = where
        self.pairs = pairs
        self.kept = kept
        self.got = swapped(sent, pairs)

    def pair(self):
        self.total, sent = self.line.run(
            join, pair_kernel, "pair", self.where, [self.kept, self.got], ["kept", "sent"]
        )
        self.before = shifted(sent, self.pairs, 1)
        self.reach = 1

    def double(self):
        (sent,) = self.line.run(join, inclusive_kernel, "inclusive", None, [self.total, self.before], ["sent"])
        self.far = shifted(sent, self.pairs, self.reach + 1)
        self.reach = 2 * self.reach + 1

    def extend(self):
        while self.reach < self.pairs - 1:
            (self.before,) = self.line.run(join, extend_kernel, "extend", None, [self.before, self.far], ["kept"])
            self.double()

    def finish(self):
        self.extend()
        self.mine, sent = self.line.run(
            join, last_kernel, "last", self.where, [self.before, self.far, self.kept, self.got], ["state", "state"]
        )
        self.other = swapped(sent, self.pairs)


def shards(
    features, gates, state_io, step_size, log_decay, conv_feat, conv_state, skip_gain, norm_gain
):
    tokens, channels = features.shape
    heads = step_size.shape[0]
    head_dim = channels // heads
    groups = state_io.shape[2] // STATE
    group_width = channels // groups
    width = group_width // 2
    count = conv_feat.shape[0]
    rim = count - 1
    ctx_size = lax.axis_size("ctx")
    head_size = lax.axis_size("head")
    pairs = ctx_size // 2
    rows = tokens // head_size
    me = lax.axis_index("head").astype(jnp.int32)
    where = jnp.stack([me, lax.axis_index("ctx").astype(jnp.int32) % 2])

    onward = [(i, i + 1) for i in range(ctx_size - 1)]
    pad = HALO - rim
    halo = jnp.pad(lax.ppermute(features[tokens - rim :], "ctx", onward), ((pad, 0), (0, 0)))
    io_halo = jnp.pad(lax.ppermute(state_io[tokens - rim :], "ctx", onward), ((pad, 0), (0, 0), (0, 0)))
    spread = jnp.asarray(spread_table(heads, head_dim), BF16)
    halves = jnp.asarray(np.arange(128)[None, :] // head_dim == np.arange(2)[:, None], BF16)
    col, row, loc, dev, ecum, edev, skips = decay_tables(log_decay, step_size, skip_gain)
    gain_row = norm_gain[None]

    line = Line()
    chunks = [(0, width), (width, width)] + [(g * group_width, group_width) for g in range(1, groups)]
    of_group = [[0, 1]] + [[g + 1] for g in range(1, groups)]
    group_of = [0, 0] + list(range(1, groups))
    fronts = {}
    maps = {}
    exchanges = {}
    ys = {}

    def run_maps(g):
        maps[g] = line.run(maps_of, g, state_io, io_halo, conv_state)

    def run_front(c):
        made = line.run(
            front, chunks[c], where, features, halo, conv_feat, dev, edev, spread, maps[group_of[c]][2]
        )
        fronts[c] = made[0]
        exchanges[c] = Exchange(line, where, pairs, made[1], made[2])

    def run_spans(c):
        g = group_of[c]
        ys[c] = line.run(
            spans_of, chunks[c], head_dim, fronts[c], *maps[g][:2], col, row, loc, ecum, spread, skips, halves
        )

    def part(c):
        return (chunks[c], ys[c], exchanges[c].mine, exchanges[c].other)

    partners = list(range(head_size - 1, 1, -1))
    squares = {}
    pieces = {}

    def ship(piece, r):
        return lax.ppermute(piece, "head", [(i, i ^ r) for i in range(head_size)])

    def run_back(mode, some, g, parts, squares, own=None):
        return line.run(
            back, mode, some, where, rows, [part(c) for c in parts], maps[g][1], edev, spread, gates, gain_row,
            squares, own=own,
        )

    def arrived(g, index):
        line.last += [pieces[g, r][index] for r in partners]

    def run_first(g, apart=False):
        squares[g] = []
        for some in [[r] for r in partners] if apart else [partners]:
            *made, square = run_back("first", some, g, [0], None)
            squares[g].append((some, square))
            for r, piece in zip(some, made):
                pieces[g, r] = [ship(piece, r)]

    def run_rest(g):
        for some, square in squares[g]:
            made = run_back("rest", some, g, [1], square)
            for r, piece in zip(some, made):
                pieces[g, r].append(ship(piece, r))

    result = None

    def run_one(g, r):
        (piece,) = run_back("whole", [r], g, of_group[g], None)
        pieces[g, r] = [ship(piece, r)]

    def run_near(g):
        nonlocal result
        made, result = run_back("whole", [1, 0], g, of_group[g], None, own=(g, groups, result))
        pieces[g, 1] = [ship(made, 1)]

    def run_own(g):
        nonlocal result
        (result,) = run_back("whole", [0], g, of_group[g], None, own=(g, groups, result))

    def run_put(g, r):
        nonlocal result
        start = (me ^ r) * channels + g * group_width
        zero = jnp.int32(0)
        if len(pieces[g, r]) == 2:
            first, rest = pieces[g, r]
            scale = rest[rows, :rows].astype(F32) + rest[rows + 8, :rows].astype(F32)
            first = (first.astype(F32) * scale[:, None]).astype(BF16)
            result = lax.dynamic_update_slice(result, first, (zero, start))
            result = lax.dynamic_update_slice(result, rest[:rows], (zero, start + width))
        else:
            result = lax.dynamic_update_slice(result, pieces[g, r][0], (zero, start))

    ex = exchanges
    later = range(1, groups)
    run_maps(0)
    run_front(0)
    run_front(1)
    ex[0].pair()
    for g in later:
        run_maps(g)
    ex[0].double()
    ex[1].pair()
    for g in later:
        run_front(g + 1)
    run_spans(0)
    ex[0].finish()
    ex[1].double()
    for g in later:
        ex[g + 1].pair()
    run_first(0, apart=True)
    run_spans(1)
    for g in later:
        ex[g + 1].double()
    ex[1].finish()
    arrived(0, 0)
    run_rest(0)
    for g in later:
        run_spans(g + 1)
        ex[g + 1].finish()
    run_near(0)
    arrived(0, 1)
    for g in later:
        run_one(g, partners[0])
        run_one(g, 1)
        for r in partners[1:]:
            run_one(g, r)
    for r in [*partners, 1]:
        run_put(0, r)
    for g in later:
        run_own(g)
        for r in [partners[0], 1, *partners[1:]]:
            run_put(g, r)
    return result


def solution(mesh):
    in_specs = (
        P("ctx", "head"),
        P("ctx", "head"),
        P("ctx", None, "head"),
        P("head", "ctx"),
        P("head", "ctx"),
        P(None, "head"),
        P(None, None, "head"),
        P("head"),
        P("head"),
    )
    out_specs = P(("ctx", "head"), None)
    return jax.shard_map(shards, mesh=mesh, in_specs=in_specs, out_specs=out_specs, check_vma=False)
```

```python
import functools

import jax
import jax.numpy as jnp
import numpy as np
from jax import lax
from jax.experimental import pallas as pl
from jax.experimental.pallas import tpu as pltpu
from jax.sharding import PartitionSpec as P

STATE = 256
SPAN = 128
HALO = 16
EPS = 1e-05
F32 = jnp.float32
BF16 = jnp.bfloat16
VMEM_BYTES = 48 * 1024 * 1024
VMEM_SMALL = 8 * 1024 * 1024
COST_SCALE = 10**9
MSG = STATE + 16
KEPT = STATE + 8


def dot(a, b):
    return jnp.dot(a, b, preferred_element_type=F32)


def silu(v):
    half = 0.5 * v
    return half * jnp.tanh(half) + half


def cost(micros):
    return pl.CostEstimate(flops=int(micros * COST_SCALE), bytes_accessed=1, transcendentals=0)


def params(limit=VMEM_BYTES):
    return pltpu.CompilerParams(vmem_limit_bytes=limit)


def spread_table(heads, head_dim):
    head = np.arange(2 * heads) % heads
    return (head[:, None] == (np.arange(heads * head_dim) // head_dim)[None, :]).astype(np.float32)


def decay_kernel(log_ref, step_ref, skip_ref, col_ref, row_ref, loc_ref, dev_ref, ecum_ref, edev_ref, skips_ref):
    heads, tokens = log_ref.shape
    spans = tokens // SPAN
    r = lax.broadcasted_iota(jnp.int32, (SPAN, SPAN), 0)
    c = lax.broadcasted_iota(jnp.int32, (SPAN, SPAN), 1)
    upper = (r <= c).astype(F32)
    cums = []
    for k in range(spans):
        cums.append(
            jnp.dot(
                log_ref[:, k * SPAN : (k + 1) * SPAN],
                upper,
                precision=lax.Precision.HIGHEST,
                preferred_element_type=F32,
            )
        )
    totals = [cum[:, SPAN - 1 :] for cum in cums]
    before = [jnp.zeros_like(totals[0])]
    for k in range(spans - 1):
        before.append(before[-1] + totals[k])
    after = [jnp.zeros_like(totals[0])]
    for k in range(spans - 1, 0, -1):
        after.insert(0, after[0] + totals[k])

    def put(ref, k, value):
        high = value.astype(BF16).astype(F32)
        both = jnp.concatenate([high, value - high], axis=0)
        ref[k * SPAN : (k + 1) * SPAN, :] = both.T.astype(BF16)

    skip = skip_ref[...]
    high = skip.astype(BF16).astype(F32)
    parts = jnp.concatenate([high, skip - high], axis=1)
    skips_ref[...] = jnp.broadcast_to(parts, skips_ref.shape).astype(BF16)
    for k in range(spans):
        cum = cums[k]
        step = step_ref[:, k * SPAN : (k + 1) * SPAN]
        col_ref[k * SPAN : (k + 1) * SPAN, :] = jnp.concatenate([cum, cum], axis=0).T
        row_ref[:, k * SPAN : (k + 1) * SPAN] = cum - jnp.log(step)
        to_end = totals[k] - cum
        put(loc_ref, k, jnp.exp(to_end) * step)
        put(dev_ref, k, jnp.exp(to_end + after[k]) * step)
        put(ecum_ref, k, jnp.exp(cum))
        put(edev_ref, k, jnp.exp(cum + before[k]))


def behind(count):
    return [pl.BlockSpec(memory_space=pl.ANY)] * count


def decay_tables(log_decay, step_size, skip_gain):
    heads, tokens = log_decay.shape
    wide = jax.ShapeDtypeStruct((tokens, 2 * heads), BF16)
    return pl.pallas_call(
        decay_kernel,
        out_shape=(
            jax.ShapeDtypeStruct((tokens, 2 * heads), F32),
            jax.ShapeDtypeStruct((heads, tokens), F32),
            wide,
            wide,
            wide,
            wide,
            jax.ShapeDtypeStruct((16, 2 * heads), BF16),
        ),
        compiler_params=params(),
        name="decays",
        cost_estimate=cost(1.5),
    )(log_decay, step_size, skip_gain[None])


def conv_rows(read, rows, halo, taps, store):
    count, width = taps.shape
    tile = SPAN
    for b in range(rows // tile):
        for c in range(1):
            cols = slice(0, width)
            own = read(b * tile, (b + 1) * tile, cols).astype(F32)
            prev = (halo[:, cols] if b == 0 else read(b * tile - HALO, b * tile, cols)).astype(F32)
            both = jnp.concatenate([prev[HALO - 8 :], own], axis=0)
            total = own * taps[count - 1 : count, cols]
            for k in range(1, count):
                total = total + both[8 - k : 8 - k + tile] * taps[count - 1 - k : count - k, cols]
            store(slice(b * tile, (b + 1) * tile), cols, silu(total))


def read_state(ref):
    if ref.dtype == F32:
        return ref[:STATE, :], ref[STATE : STATE + 1, :]
    tail = ref[STATE:MSG, :].astype(F32)
    return ref[:STATE, :].astype(F32), tail[0:1] + tail[8:9]


def write_kept(ref, value, decay):
    ref[:STATE, :] = value
    ref[STATE:KEPT, :] = jnp.broadcast_to(decay, (KEPT - STATE, decay.shape[1]))


def write_sent(ref, value, decay):
    ref[:STATE, :] = value.astype(BF16)
    high = decay.astype(BF16).astype(F32)
    shape = (8, decay.shape[1])
    rows = jnp.concatenate([jnp.broadcast_to(high, shape), jnp.broadcast_to(decay - high, shape)], axis=0)
    ref[STATE:MSG, :] = rows.astype(BF16)


def maps_kernel(order, io_ref, halo_ref, taps_ref, *refs):
    in_map_ref, out_map_ref, turned_ref = refs[order:]

    def put_in(rows, cols, value):
        in_map_ref[rows, cols] = value.astype(BF16)

    def put_out(rows, cols, value):
        out_map_ref[rows, cols] = value.astype(BF16)

    tokens = io_ref.shape[0]
    for i, put in ((0, put_in), (1, put_out)):
        conv_rows(
            lambda lo, hi, cols: io_ref[lo:hi, i, cols], tokens, halo_ref[:, i, :], taps_ref[:, i, :].astype(F32), put
        )
    for b in range(tokens // SPAN):
        rows = slice(b * SPAN, (b + 1) * SPAN)
        turned_ref[:, rows] = in_map_ref[rows, :].T


def maps_of(group, state_io, halo, conv_state, after):
    tokens = state_io.shape[0]
    count = conv_state.shape[0]

    def mine(j):
        return (0, 0, group)

    return pl.pallas_call(
        functools.partial(maps_kernel, len(after)),
        grid=(1,),
        in_specs=[
            pl.BlockSpec((tokens, 2, STATE), mine),
            pl.BlockSpec((HALO, 2, STATE), mine),
            pl.BlockSpec((count, 2, STATE), mine),
            *behind(len(after)),
        ],
        out_specs=[
            pl.BlockSpec((tokens, STATE), lambda j: (0, 0)),
            pl.BlockSpec((tokens, STATE), lambda j: (0, 0)),
            pl.BlockSpec((STATE, tokens), lambda j: (0, 0)),
        ],
        out_shape=[
            jax.ShapeDtypeStruct((tokens, STATE), BF16),
            jax.ShapeDtypeStruct((tokens, STATE), BF16),
            jax.ShapeDtypeStruct((STATE, tokens), BF16),
        ],
        compiler_params=params(),
        name="maps",
        cost_estimate=cost(3),
    )(state_io, halo, conv_state, *after)


def front_kernel(order, blocks, where_ref, feat_ref, halo_ref, taps_ref, dev_ref, edev_ref, spread_ref, turned_ref, *refs):
    xh_ref, sent_ref, kept_ref, scaled, wide = refs[order:]
    j = pl.program_id(0)
    spread = spread_ref[...]
    wide[...] = dot(dev_ref[...], spread)

    def put_feat(rows, cols, value):
        value = value.astype(BF16)
        xh_ref[rows, cols] = value
        scaled[rows, cols] = (value.astype(F32) * wide[rows, cols]).astype(BF16)

    conv_rows(
        lambda lo, hi, cols: feat_ref[lo:hi, cols], feat_ref.shape[0], halo_ref[...], taps_ref[...].astype(F32), put_feat
    )
    state = dot(turned_ref[...], scaled[...])
    decay = dot(edev_ref[...], spread)[15:16]

    @pl.when(j < blocks)
    def _():
        write_sent(sent_ref, state, decay)

    @pl.when(j >= blocks)
    def _():
        write_kept(kept_ref, state, decay)


def front(chunk, where, features, halo, conv_feat, dev, edev, spread, turned, after):
    tokens = features.shape[0]
    start, width = chunk
    half = width // 2
    block = min(512, half)
    blocks = half // block
    base = start // block
    count = conv_feat.shape[0]
    heads2 = dev.shape[1]

    def place(j, where):
        sending = (j < blocks).astype(jnp.int32)
        which = sending * (1 - where[1]) + (1 - sending) * where[1]
        return which * blocks + j - (1 - sending) * blocks

    def cols(j, where):
        return (0, base + place(j, where))

    def same(j, where):
        return (0, 0)

    return pl.pallas_call(
        functools.partial(front_kernel, len(after), blocks),
        grid_spec=pltpu.PrefetchScalarGridSpec(
            num_scalar_prefetch=1,
            grid=(2 * blocks,),
            in_specs=[
                pl.BlockSpec((tokens, block), cols),
                pl.BlockSpec((HALO, block), cols),
                pl.BlockSpec((count, block), cols),
                pl.BlockSpec((tokens, heads2), same),
                pl.BlockSpec((16, heads2), lambda j, where: (tokens // 16 - 1, 0)),
                pl.BlockSpec((heads2, block), cols),
                pl.BlockSpec((STATE, tokens), same),
                *behind(len(after)),
            ],
            out_specs=[
                pl.BlockSpec((tokens, block), lambda j, where: (0, place(j, where))),
                pl.BlockSpec((MSG, block), lambda j, where: (0, jnp.minimum(j, blocks - 1))),
                pl.BlockSpec((KEPT, block), lambda j, where: (0, jnp.maximum(j - blocks, 0))),
            ],
            scratch_shapes=[pltpu.VMEM((tokens, block), BF16), pltpu.VMEM((tokens, block), F32)],
        ),
        out_shape=[
            jax.ShapeDtypeStruct((tokens, width), BF16),
            jax.ShapeDtypeStruct((MSG, half), BF16),
            jax.ShapeDtypeStruct((KEPT, half), F32),
        ],
        compiler_params=params(),
        name="front",
        cost_estimate=cost(4),
    )(where, features, halo, conv_feat, dev, edev, spread, turned, *after)


def span_kernel(
    first_head, order, xh_ref, in_ref, out_ref, col_ref, row_ref, loc_ref, ecum_ref, spread_ref, skips_ref, halves_ref,
    *refs,
):
    y_ref, state = refs[order:]
    width = xh_ref.shape[1]
    head_dim = width // row_ref.shape[0]

    @pl.when(pl.program_id(0) == 0)
    def _():
        state[...] = jnp.zeros_like(state)

    t = lax.broadcasted_iota(jnp.int32, (SPAN, SPAN), 0)
    s = lax.broadcasted_iota(jnp.int32, (SPAN, SPAN), 1)
    first = halves_ref[0:1, :]
    second = halves_ref[1:2, :]
    block = 256
    for k in range(xh_ref.shape[0] // SPAN):
        rows = slice(k * SPAN, (k + 1) * SPAN)
        in_map = in_ref[rows, :]
        out_map = out_ref[rows, :]
        scores = lax.dot_general(out_map, in_map, (((1,), (1,)), ((), ())), preferred_element_type=F32)
        scores = jnp.where(s <= t, scores, 0.0)
        in_turned = in_map.T
        tables = jnp.concatenate([loc_ref[rows, :], ecum_ref[rows, :], skips_ref[...]], axis=0)
        for q in range(width // block):
            cols = slice(q * block, (q + 1) * block)
            feats = xh_ref[rows, cols]
            feats32 = feats.astype(F32)
            wide = dot(tables, spread_ref[:, cols])
            scaled = (feats32 * wide[:SPAN]).astype(BF16)
            ecum = wide[SPAN : 2 * SPAN]
            skip = wide[2 * SPAN : 2 * SPAN + 1]
            pairs = []
            for p in range(block // 128):
                weights = []
                for i in range(2):
                    h = (q * block + p * 128) // head_dim + i
                    gap = col_ref[rows, first_head + h : first_head + h + 1] - row_ref[h : h + 1, rows]
                    weights.append((scores * jnp.exp(jnp.minimum(gap, 0.0))).astype(BF16))
                pair = feats[:, p * 128 : (p + 1) * 128]
                stacked = jnp.concatenate([pair * first, pair * second], axis=0)
                pairs.append(dot(jnp.concatenate(weights, axis=1), stacked))
            diag = jnp.concatenate(pairs, axis=1)
            held = state[:, cols]
            carried = dot(out_map, held.astype(BF16)) * ecum
            y_ref[rows, cols] = (diag + carried + skip * feats32).astype(BF16)
            state[:, cols] = ecum[SPAN - 1 :] * held + dot(in_turned, scaled)


def spans_of(chunk, part, parts, micros, head_dim, xh, in_map, out_map, col, row, loc, ecum, spread, skips, halves, after):
    tokens = xh.shape[0]
    width = chunk[1] // parts
    index = chunk[0] // width + part
    some = width // head_dim
    heads2 = loc.shape[1]
    tile = 2 * SPAN
    return pl.pallas_call(
        functools.partial(span_kernel, index * some, len(after)),
        grid=(tokens // tile,),
        in_specs=[
            pl.BlockSpec((tile, width), lambda k: (k, part)),
            pl.BlockSpec((tile, STATE), lambda k: (k, 0)),
            pl.BlockSpec((tile, STATE), lambda k: (k, 0)),
            pl.BlockSpec((tile, heads2), lambda k: (k, 0)),
            pl.BlockSpec((some, tile), lambda k: (index, k)),
            pl.BlockSpec((tile, heads2), lambda k: (k, 0)),
            pl.BlockSpec((tile, heads2), lambda k: (k, 0)),
            pl.BlockSpec((heads2, width), lambda k: (0, index)),
            pl.BlockSpec(skips.shape, lambda k: (0, 0)),
            pl.BlockSpec(halves.shape, lambda k: (0, 0)),
            *behind(len(after)),
        ],
        out_specs=pl.BlockSpec((tile, width), lambda k: (k, 0)),
        out_shape=jax.ShapeDtypeStruct((tokens, width), BF16),
        scratch_shapes=[pltpu.VMEM((STATE, width), F32)],
        compiler_params=params(),
        name="spans",
        cost_estimate=cost(micros),
    )(xh, in_map, out_map, col, row, loc, ecum, spread, skips, halves, *after)


def pair_kernel(where_ref, kept_ref, got_ref, *refs):
    total_ref, sent_ref = refs[-2:]
    kept, kept_decay = read_state(kept_ref)
    got, got_decay = read_state(got_ref)

    def put(first, second, decay):
        total = decay * first + second
        write_kept(total_ref, total, kept_decay * got_decay)
        write_sent(sent_ref, total, kept_decay * got_decay)

    @pl.when(where_ref[1] == 0)
    def _():
        put(kept, got, got_decay)

    @pl.when(where_ref[1] == 1)
    def _():
        put(got, kept, kept_decay)


def inclusive_kernel(total_ref, before_ref, *refs):
    sent_ref = refs[-1]
    total, decay = read_state(total_ref)
    before, before_decay = read_state(before_ref)
    write_sent(sent_ref, total + decay * before, decay * before_decay)


def extend_kernel(before_ref, far_ref, *refs):
    before, decay = read_state(before_ref)
    far, far_decay = read_state(far_ref)
    write_kept(refs[-1], before + decay * far, decay * far_decay)


def last_kernel(where_ref, before_ref, far_ref, kept_ref, got_ref, *refs):
    mine_ref, sent_ref = refs[-2:]
    before, before_decay = read_state(before_ref)
    far, _ = read_state(far_ref)
    carried = before + before_decay * far

    @pl.when(where_ref[1] == 0)
    def _():
        kept, decay = read_state(kept_ref)
        mine_ref[...] = carried.astype(BF16)
        sent_ref[...] = (decay * carried + kept).astype(BF16)

    @pl.when(where_ref[1] == 1)
    def _():
        got, decay = read_state(got_ref)
        mine_ref[...] = (decay * carried + got).astype(BF16)
        sent_ref[...] = carried.astype(BF16)


def join(kernel, name, where, operands, outs, after):
    width = operands[0].shape[1]
    shapes = {
        "kept": jax.ShapeDtypeStruct((KEPT, width), F32),
        "sent": jax.ShapeDtypeStruct((MSG, width), BF16),
        "state": jax.ShapeDtypeStruct((STATE, width), BF16),
    }
    scalars = [] if where is None else [where]
    return pl.pallas_call(
        kernel,
        in_specs=[pl.BlockSpec(memory_space=pltpu.SMEM)] * len(scalars)
        + [pl.BlockSpec(memory_space=pltpu.VMEM)] * len(operands)
        + behind(len(after)),
        out_specs=[pl.BlockSpec(memory_space=pltpu.VMEM)] * len(outs),
        out_shape=[shapes[out] for out in outs],
        compiler_params=params(VMEM_SMALL),
        name=name,
        cost_estimate=cost(0.7),
    )(*scalars, *operands, *after)


def back_kernel(mode, counts, partners, order, where_ref, out_ref, edev_ref, *refs):
    chunks = []
    for pieces in counts:
        chunks.append((refs[:pieces], *refs[pieces : pieces + 5]))
        refs = refs[pieces + 5 :]
    if mode == "rest":
        squares_ref, *refs = refs
    refs = refs[order:]
    o_refs = refs[:partners]
    if mode == "first":
        squares_ref = refs[partners]
    gated, sums = refs[-2:]
    out_map = out_ref[...]
    edev = edev_ref[...]
    rows = out_map.shape[0]
    block = 256
    steps = pl.num_programs(0) // partners
    odd = where_ref[1] == 1
    sums[...] = squares_ref[...] if mode == "rest" else jnp.zeros((rows, 128), F32)
    at = 0
    for y_refs, mine_ref, other_ref, spread_ref, gate_ref, gain_ref in chunks:
        half = mine_ref.shape[1]
        for q in range(2 * half // block):
            cols = slice(q * block, (q + 1) * block)
            inner = slice(q * block % half, q * block % half + block)
            mine = mine_ref[:, inner]
            other = other_ref[:, inner]
            state = jnp.where(odd, other, mine) if q * block < half else jnp.where(odd, mine, other)
            gated[:, at : at + block] = dot(out_map, state) * dot(edev, spread_ref[:, cols])
            y_ref = y_refs[q * block // y_refs[0].shape[1]]
            y_at = q * block % y_refs[0].shape[1]
            for c in range(block // 128):
                y_cols = slice(y_at + c * 128, y_at + (c + 1) * 128)
                to = slice(at + c * 128, at + (c + 1) * 128)
                cols = slice(q * block + c * 128, q * block + (c + 1) * 128)
                gain = gain_ref[:, cols]
                for b in range(rows // 64):
                    part = slice(b * 64, (b + 1) * 64)
                    value = (y_ref[part, y_cols].astype(F32) + gated[part, to]) * silu(gate_ref[part, cols].astype(F32))
                    sums[part, :] = sums[part, :] + value * value
                    gated[part, to] = value * gain
            at += block
    if mode == "first":
        squares_ref[...] = sums[...]
    else:
        width = at if mode == "whole" else 2 * at
        mean = jnp.sum(sums[...], axis=1, keepdims=True) * (1.0 / width)
        scale = lax.rsqrt(mean + EPS)
    for p in range(partners):

        @pl.when(pl.program_id(0) // steps == p)
        def _(o_ref=o_refs[p]):
            if mode == "rest":
                step = pl.program_id(0) - p * steps
                start = pl.multiple_of(step * rows, rows)
                high = scale.astype(BF16).astype(F32)
                parts = [jnp.broadcast_to(part, (rows, 128)).T[:8] for part in (high, scale - high)]
                o_ref[steps * rows :, pl.ds(start, rows)] = jnp.concatenate(parts, axis=0).astype(BF16)
            for q in range(at // block):
                cols = slice(q * block, (q + 1) * block)
                value = gated[:, cols] if mode == "first" else gated[:, cols] * scale
                if mode == "rest":
                    o_ref[pl.ds(start, rows), cols] = value.astype(BF16)
                else:
                    o_ref[:, cols] = value.astype(BF16)


def back(mode, some, where, rows, chunks, out_map, edev, spread, gates, gain_row, squares, after, own=None):
    heads2 = edev.shape[1]
    tile = 128
    steps = rows // tile
    partners = len(some)

    def at(i, where):
        turn = some[0]
        for p in range(1, partners):
            turn = jnp.where(i >= p * steps, some[p], turn)
        return ((where[0] ^ turn) * steps + i % steps, 0)

    specs = [pl.BlockSpec((tile, STATE), at), pl.BlockSpec((tile, heads2), at)]
    operands = [out_map, edev]
    total = 0
    for (start, width), ys, mine, other in chunks:
        index = start // width
        half = width // 2
        total += width
        specs += [pl.BlockSpec((tile, y.shape[1]), at) for y in ys]
        specs += [
            pl.BlockSpec((STATE, half), lambda i, where: (0, 0)),
            pl.BlockSpec((STATE, half), lambda i, where: (0, 0)),
            pl.BlockSpec((heads2, width), lambda i, where, index=index: (0, index)),
            pl.BlockSpec((tile, width), lambda i, where, index=index: (at(i, where)[0], index)),
            pl.BlockSpec((1, width), lambda i, where, index=index: (0, index)),
        ]
        operands += [*ys, mine, other, spread, gates, gain_row]
    if mode == "rest":
        specs.append(pl.BlockSpec((tile, 128), lambda i, where: (i, 0)))
        operands.append(squares)
    aliases = {}
    if own is not None and own[2] is not None:
        after = [own[2], *after]
        aliases = {1 + len(operands): partners - 1}
    specs += behind(len(after))
    operands += after
    sent = rows + 16 if mode == "rest" else rows
    part = sent if mode == "rest" else tile

    def part_of(p):
        if mode == "rest":
            return lambda i, where: (0, 0)
        return lambda i, where: (jnp.clip(i - p * steps, 0, steps - 1), 0)

    out_specs = [pl.BlockSpec((part, total), part_of(p)) for p in range(partners)]
    out_shape = [jax.ShapeDtypeStruct((sent, total), BF16)] * partners
    if own is not None:
        group, groups, _ = own
        out_specs[-1] = pl.BlockSpec(
            (tile, total),
            lambda i, where: (jnp.clip(i - (partners - 1) * steps, 0, steps - 1), (where[0] ^ some[-1]) * groups + group),
        )
        out_shape[-1] = jax.ShapeDtypeStruct((rows, groups * total * (gates.shape[0] // rows)), BF16)
    if mode == "first":
        out_specs.append(pl.BlockSpec((tile, 128), lambda i, where: (i, 0)))
        out_shape.append(jax.ShapeDtypeStruct((partners * rows, 128), F32))
    return pl.pallas_call(
        functools.partial(back_kernel, mode, [len(ys) for _, ys, _, _ in chunks], partners, len(after)),
        grid_spec=pltpu.PrefetchScalarGridSpec(
            num_scalar_prefetch=1,
            grid=(partners * steps,),
            in_specs=specs,
            out_specs=out_specs,
            scratch_shapes=[pltpu.VMEM((tile, total), F32), pltpu.VMEM((tile, 128), F32)],
        ),
        out_shape=out_shape,
        input_output_aliases=aliases,
        compiler_params=params(),
        name=f"back_{mode}",
        cost_estimate=cost(1),
    )(where, *operands)


def mark_kernel(order, *refs):
    refs[order][...] = jnp.zeros((8, 128), F32)


def mark(after):
    return pl.pallas_call(
        functools.partial(mark_kernel, len(after)),
        grid=(1,),
        in_specs=behind(len(after)),
        out_specs=pl.BlockSpec((8, 128), lambda i: (0, 0)),
        out_shape=jax.ShapeDtypeStruct((8, 128), F32),
        compiler_params=params(VMEM_SMALL),
        name="mark",
        cost_estimate=cost(200),
    )(*after)


def shifted(value, pairs, steps):
    return lax.ppermute(
        value,
        "ctx",
        [(2 * q + y, 2 * (q + steps) + y) for q in range(pairs - steps) for y in range(2)],
    )


def swapped(value, pairs):
    return lax.ppermute(value, "ctx", [(2 * q + y, 2 * q + 1 - y) for q in range(pairs) for y in range(2)])


class Line:
    def __init__(self):
        self.last = []

    def run(self, make, *args, **kwargs):
        made = make(*args, after=self.last, **kwargs)
        self.last = [made[0] if isinstance(made, (list, tuple)) else made]
        return made


class Exchange:
    def __init__(self, line, where, pairs, sent, kept):
        self.line = line
        self.where = where
        self.pairs = pairs
        self.kept = kept
        self.got = swapped(sent, pairs)

    def pair(self):
        self.total, sent = self.line.run(
            join, pair_kernel, "pair", self.where, [self.kept, self.got], ["kept", "sent"]
        )
        self.before = shifted(sent, self.pairs, 1)
        self.reach = 1

    def double(self):
        (sent,) = self.line.run(join, inclusive_kernel, "inclusive", None, [self.total, self.before], ["sent"])
        self.far = shifted(sent, self.pairs, self.reach + 1)
        self.reach = 2 * self.reach + 1

    def extend(self):
        while self.reach < self.pairs - 1:
            (self.before,) = self.line.run(join, extend_kernel, "extend", None, [self.before, self.far], ["kept"])
            self.double()

    def finish(self):
        self.extend()
        self.mine, sent = self.line.run(
            join, last_kernel, "last", self.where, [self.before, self.far, self.kept, self.got], ["state", "state"]
        )
        self.other = swapped(sent, self.pairs)


def shards(
    features, gates, state_io, step_size, log_decay, conv_feat, conv_state, skip_gain, norm_gain
):
    tokens, channels = features.shape
    heads = step_size.shape[0]
    head_dim = channels // heads
    groups = state_io.shape[2] // STATE
    group_width = channels // groups
    width = group_width // 2
    count = conv_feat.shape[0]
    rim = count - 1
    ctx_size = lax.axis_size("ctx")
    head_size = lax.axis_size("head")
    pairs = ctx_size // 2
    rows = tokens // head_size
    me = lax.axis_index("head").astype(jnp.int32)
    where = jnp.stack([me, lax.axis_index("ctx").astype(jnp.int32) % 2])

    onward = [(i, i + 1) for i in range(ctx_size - 1)]
    pad = HALO - rim
    halo = jnp.pad(lax.ppermute(features[tokens - rim :], "ctx", onward), ((pad, 0), (0, 0)))
    io_halo = jnp.pad(lax.ppermute(state_io[tokens - rim :], "ctx", onward), ((pad, 0), (0, 0), (0, 0)))
    spread = jnp.asarray(spread_table(heads, head_dim), BF16)
    halves = jnp.asarray(np.arange(128)[None, :] // head_dim == np.arange(2)[:, None], BF16)
    col, row, loc, dev, ecum, edev, skips = decay_tables(log_decay, step_size, skip_gain)
    gain_row = norm_gain[None]

    line = Line()
    chunks = [(0, width), (width, width)] + [(g * group_width, group_width) for g in range(1, groups)]
    of_group = [[0, 1]] + [[g + 1] for g in range(1, groups)]
    group_of = [0, 0] + list(range(1, groups))
    fronts = {}
    maps = {}
    exchanges = {}
    ys = {}

    def run_maps(g):
        maps[g] = line.run(maps_of, g, state_io, io_halo, conv_state)

    def run_front(c):
        made = line.run(
            front, chunks[c], where, features, halo, conv_feat, dev, edev, spread, maps[group_of[c]][2]
        )
        fronts[c] = made[0]
        exchanges[c] = Exchange(line, where, pairs, made[1], made[2])

    def run_spans(c, part=0, parts=1, micros=200):
        g = group_of[c]
        made = line.run(
            spans_of, chunks[c], part, parts, micros, head_dim, fronts[c], *maps[g][:2], col, row, loc, ecum, spread,
            skips, halves,
        )
        ys.setdefault(c, []).append(made)

    def part(c):
        return (chunks[c], ys[c], exchanges[c].mine, exchanges[c].other)

    partners = list(range(head_size - 1, 1, -1))
    squares = {}
    pieces = {}

    def ship(piece, r):
        return lax.ppermute(piece, "head", [(i, i ^ r) for i in range(head_size)])

    def run_back(mode, some, g, parts, squares, own=None):
        return line.run(
            back, mode, some, where, rows, [part(c) for c in parts], maps[g][1], edev, spread, gates, gain_row,
            squares, own=own,
        )

    def arrived(g, index, some):
        line.last += [pieces[g, r][index] for r in some]

    def run_first(g, apart=False):
        squares[g] = []
        for some in [[r] for r in partners] if apart else [partners]:
            *made, square = run_back("first", some, g, [0], None)
            squares[g].append((some, square))
            for r, piece in zip(some, made):
                pieces[g, r] = [ship(piece, r)]

    def run_rest(g):
        for some, square in squares[g]:
            made = run_back("rest", some, g, [1], square)
            for r, piece in zip(some, made):
                pieces[g, r].append(ship(piece, r))

    result = None

    def run_one(g, r):
        (piece,) = run_back("whole", [r], g, of_group[g], None)
        pieces[g, r] = [ship(piece, r)]

    def run_own(g):
        nonlocal result
        before = line.last
        (result,) = run_back("whole", [0], g, of_group[g], None, own=(g, groups, result))
        line.last = before

    def run_put(g, r):
        nonlocal result
        start = (me ^ r) * channels + g * group_width
        zero = jnp.int32(0)
        if len(pieces[g, r]) == 2:
            first, rest = pieces[g, r]
            scale = rest[rows, :rows].astype(F32) + rest[rows + 8, :rows].astype(F32)
            first = (first.astype(F32) * scale[:, None]).astype(BF16)
            result = lax.dynamic_update_slice(result, first, (zero, start))
            result = lax.dynamic_update_slice(result, rest[:rows], (zero, start + width))
        else:
            result = lax.dynamic_update_slice(result, pieces[g, r][0], (zero, start))

    ex = exchanges
    later = range(1, groups)
    run_maps(0)
    run_front(0)
    run_front(1)
    ex[0].pair()
    for g in later:
        run_maps(g)
    ex[0].double()
    ex[1].pair()
    for g in later:
        run_front(g + 1)
    run_spans(0)
    ex[0].finish()
    ex[1].double()
    for g in later:
        ex[g + 1].pair()
    run_first(0, apart=True)
    if groups > 1:
        line.run(mark)
    for g in later:
        ex[g + 1].double()
    run_spans(1, micros=1)
    ex[1].finish()
    for g in later:
        run_spans(g + 1, 0, 2, 1)
    arrived(0, 0, partners)
    run_rest(0)
    for g in later:
        ex[g + 1].finish()
        run_spans(g + 1, 1, 2, 1)
    run_one(0, 1)
    for g in later:
        arrived(0, 1, partners[:1])
        run_one(g, partners[0])
        run_one(g, 1)
        arrived(0, 1, partners[1:])
        for r in partners[1:]:
            run_one(g, r)
    run_own(0)
    for r in [*partners, 1]:
        run_put(0, r)
    for g in later:
        run_own(g)
        for r in [partners[0], 1, *partners[1:]]:
            run_put(g, r)
    return result


def solution(mesh):
    in_specs = (
        P("ctx", "head"),
        P("ctx", "head"),
        P("ctx", None, "head"),
        P("head", "ctx"),
        P("head", "ctx"),
        P(None, "head"),
        P(None, None, "head"),
        P("head"),
        P("head"),
    )
    out_specs = P(("ctx", "head"), None)
    return jax.shard_map(shards, mesh=mesh, in_specs=in_specs, out_specs=out_specs, check_vma=False)
```

```python
import functools

import jax
import jax.numpy as jnp
import numpy as np
from jax import lax
from jax.experimental import pallas as pl
from jax.experimental.pallas import tpu as pltpu
from jax.sharding import PartitionSpec as P

STATE = 256
SPAN = 128
HALO = 16
EPS = 1e-05
LOC, ECUM, DEV, EDEV = range(4)
F32 = jnp.float32
BF16 = jnp.bfloat16
VMEM_BYTES = 48 * 1024 * 1024
VMEM_SMALL = 8 * 1024 * 1024
COST_SCALE = 10**9
MSG = STATE + 16
KEPT = STATE + 8


def dot(a, b):
    return jnp.dot(a, b, preferred_element_type=F32)


def silu(v):
    half = 0.5 * v
    return half * jnp.tanh(half) + half


def cost(micros):
    return pl.CostEstimate(flops=int(micros * COST_SCALE), bytes_accessed=1, transcendentals=0)


def params(limit=VMEM_BYTES):
    return pltpu.CompilerParams(vmem_limit_bytes=limit)


def lanes_of(heads):
    return -(-2 * heads // 128) * 128


def spread_table(heads, head_dim):
    row = np.arange(lanes_of(heads))
    head = np.where(row < 2 * heads, row % heads, heads)
    return (head[:, None] == (np.arange(heads * head_dim) // head_dim)[None, :]).astype(np.float32)


def decay_kernel(log_ref, step_ref, skip_ref, col_ref, row_ref, table_ref, skips_ref):
    heads, tokens = log_ref.shape
    lanes = lanes_of(heads)
    spans = tokens // SPAN
    r = lax.broadcasted_iota(jnp.int32, (SPAN, SPAN), 0)
    c = lax.broadcasted_iota(jnp.int32, (SPAN, SPAN), 1)
    upper = (r <= c).astype(F32)
    cums = []
    for k in range(spans):
        cums.append(
            jnp.dot(
                log_ref[:, k * SPAN : (k + 1) * SPAN],
                upper,
                precision=lax.Precision.HIGHEST,
                preferred_element_type=F32,
            )
        )
    totals = [cum[:, SPAN - 1 :] for cum in cums]
    before = [jnp.zeros_like(totals[0])]
    for k in range(spans - 1):
        before.append(before[-1] + totals[k])
    after = [jnp.zeros_like(totals[0])]
    for k in range(spans - 1, 0, -1):
        after.insert(0, after[0] + totals[k])

    def put(index, k, value):
        high = value.astype(BF16).astype(F32)
        rest = [jnp.zeros((lanes - 2 * heads, SPAN), F32)] if lanes > 2 * heads else []
        both = jnp.concatenate([high, value - high, *rest], axis=0)
        table_ref[k * SPAN : (k + 1) * SPAN, index * lanes : (index + 1) * lanes] = both.T.astype(BF16)

    skip = skip_ref[...]
    high = skip.astype(BF16).astype(F32)
    none = [jnp.zeros((1, lanes - 2 * heads), F32)] if lanes > 2 * heads else []
    parts = jnp.concatenate([high, skip - high, *none], axis=1)
    skips_ref[...] = jnp.broadcast_to(parts, skips_ref.shape).astype(BF16)
    for k in range(spans):
        cum = cums[k]
        step = step_ref[:, k * SPAN : (k + 1) * SPAN]
        col_ref[k * SPAN : (k + 1) * SPAN, :] = jnp.concatenate([cum] * (lanes // heads), axis=0).T
        row_ref[:, k * SPAN : (k + 1) * SPAN] = cum - jnp.log(step)
        to_end = totals[k] - cum
        put(LOC, k, jnp.exp(to_end) * step)
        put(DEV, k, jnp.exp(to_end + after[k]) * step)
        put(ECUM, k, jnp.exp(cum))
        put(EDEV, k, jnp.exp(cum + before[k]))


def behind(count):
    return [pl.BlockSpec(memory_space=pl.ANY)] * count


def decay_tables(log_decay, step_size, skip_gain):
    heads, tokens = log_decay.shape
    lanes = lanes_of(heads)
    return pl.pallas_call(
        decay_kernel,
        out_shape=(
            jax.ShapeDtypeStruct((tokens, lanes), F32),
            jax.ShapeDtypeStruct((heads, tokens), F32),
            jax.ShapeDtypeStruct((tokens, 4 * lanes), BF16),
            jax.ShapeDtypeStruct((16, lanes), BF16),
        ),
        compiler_params=params(),
        name="decays",
        cost_estimate=cost(1.5),
    )(log_decay, step_size, skip_gain[None])


def conv_rows(read, rows, halo, taps, store):
    count, width = taps.shape
    tile = SPAN
    for b in range(rows // tile):
        for c in range(1):
            cols = slice(0, width)
            own = read(b * tile, (b + 1) * tile, cols).astype(F32)
            prev = (halo[:, cols] if b == 0 else read(b * tile - HALO, b * tile, cols)).astype(F32)
            both = jnp.concatenate([prev[HALO - 8 :], own], axis=0)
            total = own * taps[count - 1 : count, cols]
            for k in range(1, count):
                total = total + both[8 - k : 8 - k + tile] * taps[count - 1 - k : count - k, cols]
            store(slice(b * tile, (b + 1) * tile), cols, silu(total))


def read_state(ref):
    if ref.dtype == F32:
        return ref[:STATE, :], ref[STATE : STATE + 1, :]
    tail = ref[STATE:MSG, :].astype(F32)
    return ref[:STATE, :].astype(F32), tail[0:1] + tail[8:9]


def write_kept(ref, value, decay):
    ref[:STATE, :] = value
    ref[STATE:KEPT, :] = jnp.broadcast_to(decay, (KEPT - STATE, decay.shape[1]))


def write_sent(ref, value, decay):
    ref[:STATE, :] = value.astype(BF16)
    high = decay.astype(BF16).astype(F32)
    shape = (8, decay.shape[1])
    rows = jnp.concatenate([jnp.broadcast_to(high, shape), jnp.broadcast_to(decay - high, shape)], axis=0)
    ref[STATE:MSG, :] = rows.astype(BF16)


def maps_kernel(order, io_ref, halo_ref, taps_ref, *refs):
    map_ref, turned_ref = refs[order:]

    def put_in(rows, cols, value):
        map_ref[rows, :STATE] = value.astype(BF16)

    def put_out(rows, cols, value):
        map_ref[rows, STATE:] = value.astype(BF16)

    tokens = io_ref.shape[0]
    for i, put in ((0, put_in), (1, put_out)):
        conv_rows(
            lambda lo, hi, cols: io_ref[lo:hi, i, cols], tokens, halo_ref[:, i, :], taps_ref[:, i, :].astype(F32), put
        )
    for b in range(tokens // SPAN):
        rows = slice(b * SPAN, (b + 1) * SPAN)
        turned_ref[:, rows] = map_ref[rows, :STATE].T


def maps_of(group, state_io, halo, conv_state, after):
    tokens = state_io.shape[0]
    count = conv_state.shape[0]

    def mine(j):
        return (0, 0, group)

    return pl.pallas_call(
        functools.partial(maps_kernel, len(after)),
        grid=(1,),
        in_specs=[
            pl.BlockSpec((tokens, 2, STATE), mine),
            pl.BlockSpec((HALO, 2, STATE), mine),
            pl.BlockSpec((count, 2, STATE), mine),
            *behind(len(after)),
        ],
        out_specs=[
            pl.BlockSpec((tokens, 2 * STATE), lambda j: (0, 0)),
            pl.BlockSpec((STATE, tokens), lambda j: (0, 0)),
        ],
        out_shape=[
            jax.ShapeDtypeStruct((tokens, 2 * STATE), BF16),
            jax.ShapeDtypeStruct((STATE, tokens), BF16),
        ],
        compiler_params=params(),
        name="maps",
        cost_estimate=cost(3),
    )(state_io, halo, conv_state, *after)


def front_kernel(order, blocks, where_ref, feat_ref, halo_ref, taps_ref, dev_ref, edev_ref, spread_ref, turned_ref, *refs):
    xh_ref, sent_ref, kept_ref, scaled, wide = refs[order:]
    j = pl.program_id(0)
    spread = spread_ref[...]
    wide[...] = dot(dev_ref[...], spread)

    def put_feat(rows, cols, value):
        value = value.astype(BF16)
        xh_ref[rows, cols] = value
        scaled[rows, cols] = (value.astype(F32) * wide[rows, cols]).astype(BF16)

    conv_rows(
        lambda lo, hi, cols: feat_ref[lo:hi, cols], feat_ref.shape[0], halo_ref[...], taps_ref[...].astype(F32), put_feat
    )
    state = dot(turned_ref[...], scaled[...])
    decay = dot(edev_ref[...], spread)[15:16]

    @pl.when(j < blocks)
    def _():
        write_sent(sent_ref, state, decay)

    @pl.when(j >= blocks)
    def _():
        write_kept(kept_ref, state, decay)


def front(chunk, where, features, halo, conv_feat, table, spread, turned, after):
    tokens = features.shape[0]
    start, width = chunk
    half = width // 2
    block = min(512, half)
    blocks = half // block
    base = start // block
    count = conv_feat.shape[0]
    heads2 = spread.shape[0]

    def place(j, where):
        sending = (j < blocks).astype(jnp.int32)
        which = sending * (1 - where[1]) + (1 - sending) * where[1]
        return which * blocks + j - (1 - sending) * blocks

    def cols(j, where):
        return (0, base + place(j, where))

    def same(j, where):
        return (0, 0)

    return pl.pallas_call(
        functools.partial(front_kernel, len(after), blocks),
        grid_spec=pltpu.PrefetchScalarGridSpec(
            num_scalar_prefetch=1,
            grid=(2 * blocks,),
            in_specs=[
                pl.BlockSpec((tokens, block), cols),
                pl.BlockSpec((HALO, block), cols),
                pl.BlockSpec((count, block), cols),
                pl.BlockSpec((tokens, heads2), lambda j, where: (0, DEV)),
                pl.BlockSpec((16, heads2), lambda j, where: (tokens // 16 - 1, EDEV)),
                pl.BlockSpec((heads2, block), cols),
                pl.BlockSpec((STATE, tokens), same),
                *behind(len(after)),
            ],
            out_specs=[
                pl.BlockSpec((tokens, block), lambda j, where: (0, place(j, where))),
                pl.BlockSpec((MSG, block), lambda j, where: (0, jnp.minimum(j, blocks - 1))),
                pl.BlockSpec((KEPT, block), lambda j, where: (0, jnp.maximum(j - blocks, 0))),
            ],
            scratch_shapes=[pltpu.VMEM((tokens, block), BF16), pltpu.VMEM((tokens, block), F32)],
        ),
        out_shape=[
            jax.ShapeDtypeStruct((tokens, width), BF16),
            jax.ShapeDtypeStruct((MSG, half), BF16),
            jax.ShapeDtypeStruct((KEPT, half), F32),
        ],
        compiler_params=params(),
        name="front",
        cost_estimate=cost(4),
    )(where, features, halo, conv_feat, table, table, spread, turned, *after)


def span_kernel(
    first_head, order, xh_ref, map_ref, col_ref, row_ref, table_ref, spread_ref, skips_ref, halves_ref,
    *refs,
):
    y_ref, state = refs[order:]
    width = xh_ref.shape[1]
    head_dim = width // row_ref.shape[0]
    heads2 = spread_ref.shape[0]

    @pl.when(pl.program_id(0) == 0)
    def _():
        state[...] = jnp.zeros_like(state)

    t = lax.broadcasted_iota(jnp.int32, (SPAN, SPAN), 0)
    s = lax.broadcasted_iota(jnp.int32, (SPAN, SPAN), 1)
    first = halves_ref[0:1, :]
    second = halves_ref[1:2, :]
    block = 256
    for k in range(xh_ref.shape[0] // SPAN):
        rows = slice(k * SPAN, (k + 1) * SPAN)
        in_map = map_ref[rows, :STATE]
        out_map = map_ref[rows, STATE:]
        scores = lax.dot_general(out_map, in_map, (((1,), (1,)), ((), ())), preferred_element_type=F32)
        scores = jnp.where(s <= t, scores, 0.0)
        in_turned = in_map.T
        tables = jnp.concatenate([table_ref[rows, :heads2], table_ref[rows, heads2:], skips_ref[...]], axis=0)
        for q in range(width // block):
            cols = slice(q * block, (q + 1) * block)
            feats = xh_ref[rows, cols]
            feats32 = feats.astype(F32)
            wide = dot(tables, spread_ref[:, cols])
            scaled = (feats32 * wide[:SPAN]).astype(BF16)
            ecum = wide[SPAN : 2 * SPAN]
            skip = wide[2 * SPAN : 2 * SPAN + 1]
            pairs = []
            for p in range(block // 128):
                weights = []
                for i in range(2):
                    h = (q * block + p * 128) // head_dim + i
                    gap = col_ref[rows, first_head + h : first_head + h + 1] - row_ref[h : h + 1, rows]
                    weights.append((scores * jnp.exp(jnp.minimum(gap, 0.0))).astype(BF16))
                pair = feats[:, p * 128 : (p + 1) * 128]
                stacked = jnp.concatenate([pair * first, pair * second], axis=0)
                pairs.append(dot(jnp.concatenate(weights, axis=1), stacked))
            diag = jnp.concatenate(pairs, axis=1)
            held = state[:, cols]
            carried = dot(out_map, held.astype(BF16)) * ecum
            y_ref[rows, cols] = (diag + carried + skip * feats32).astype(BF16)
            state[:, cols] = ecum[SPAN - 1 :] * held + dot(in_turned, scaled)


def spans_of(chunk, part, parts, micros, head_dim, xh, both_maps, col, row, table, spread, skips, halves, after):
    tokens = xh.shape[0]
    width = chunk[1] // parts
    index = chunk[0] // width + part
    some = width // head_dim
    heads2 = spread.shape[0]
    tile = 2 * SPAN
    return pl.pallas_call(
        functools.partial(span_kernel, index * some, len(after)),
        grid=(tokens // tile,),
        in_specs=[
            pl.BlockSpec((tile, width), lambda k: (k, part)),
            pl.BlockSpec((tile, 2 * STATE), lambda k: (k, 0)),
            pl.BlockSpec((tile, heads2), lambda k: (k, 0)),
            pl.BlockSpec((some, tile), lambda k: (index, k)),
            pl.BlockSpec((tile, 2 * heads2), lambda k: (k, 0)),
            pl.BlockSpec((heads2, width), lambda k: (0, index)),
            pl.BlockSpec(skips.shape, lambda k: (0, 0)),
            pl.BlockSpec(halves.shape, lambda k: (0, 0)),
            *behind(len(after)),
        ],
        out_specs=pl.BlockSpec((tile, width), lambda k: (k, 0)),
        out_shape=jax.ShapeDtypeStruct((tokens, width), BF16),
        scratch_shapes=[pltpu.VMEM((STATE, width), F32)],
        compiler_params=params(),
        name="spans",
        cost_estimate=cost(micros),
    )(xh, both_maps, col, row, table, spread, skips, halves, *after)


def pair_kernel(where_ref, kept_ref, got_ref, *refs):
    total_ref, sent_ref = refs[-2:]
    kept, kept_decay = read_state(kept_ref)
    got, got_decay = read_state(got_ref)

    def put(first, second, decay):
        total = decay * first + second
        write_kept(total_ref, total, kept_decay * got_decay)
        write_sent(sent_ref, total, kept_decay * got_decay)

    @pl.when(where_ref[1] == 0)
    def _():
        put(kept, got, got_decay)

    @pl.when(where_ref[1] == 1)
    def _():
        put(got, kept, kept_decay)


def inclusive_kernel(total_ref, before_ref, *refs):
    sent_ref = refs[-1]
    total, decay = read_state(total_ref)
    before, before_decay = read_state(before_ref)
    write_sent(sent_ref, total + decay * before, decay * before_decay)


def extend_kernel(before_ref, far_ref, *refs):
    before, decay = read_state(before_ref)
    far, far_decay = read_state(far_ref)
    write_kept(refs[-1], before + decay * far, decay * far_decay)


def last_kernel(where_ref, before_ref, far_ref, kept_ref, got_ref, *refs):
    mine_ref, sent_ref = refs[-2:]
    before, before_decay = read_state(before_ref)
    far, _ = read_state(far_ref)
    carried = before + before_decay * far

    @pl.when(where_ref[1] == 0)
    def _():
        kept, decay = read_state(kept_ref)
        mine_ref[...] = carried.astype(BF16)
        sent_ref[...] = (decay * carried + kept).astype(BF16)

    @pl.when(where_ref[1] == 1)
    def _():
        got, decay = read_state(got_ref)
        mine_ref[...] = (decay * carried + got).astype(BF16)
        sent_ref[...] = carried.astype(BF16)


def join(kernel, name, where, operands, outs, after):
    width = operands[0].shape[1]
    shapes = {
        "kept": jax.ShapeDtypeStruct((KEPT, width), F32),
        "sent": jax.ShapeDtypeStruct((MSG, width), BF16),
        "state": jax.ShapeDtypeStruct((STATE, width), BF16),
    }
    scalars = [] if where is None else [where]
    return pl.pallas_call(
        kernel,
        in_specs=[pl.BlockSpec(memory_space=pltpu.SMEM)] * len(scalars)
        + [pl.BlockSpec(memory_space=pltpu.VMEM)] * len(operands)
        + behind(len(after)),
        out_specs=[pl.BlockSpec(memory_space=pltpu.VMEM)] * len(outs),
        out_shape=[shapes[out] for out in outs],
        compiler_params=params(VMEM_SMALL),
        name=name,
        cost_estimate=cost(0.7),
    )(*scalars, *operands, *after)


def back_kernel(mode, counts, partners, order, where_ref, out_ref, edev_ref, *refs):
    chunks = []
    for pieces in counts:
        chunks.append((refs[:pieces], *refs[pieces : pieces + 5]))
        refs = refs[pieces + 5 :]
    if mode == "rest":
        squares_ref, *refs = refs
    refs = refs[order:]
    o_refs = refs[:partners]
    if mode == "first":
        squares_ref = refs[partners]
    gated, sums = refs[-2:]
    out_map = out_ref[...]
    edev = edev_ref[...]
    rows = out_map.shape[0]
    block = 256
    steps = pl.num_programs(0) // partners
    odd = where_ref[1] == 1
    sums[...] = squares_ref[...] if mode == "rest" else jnp.zeros((rows, 128), F32)
    at = 0
    for y_refs, mine_ref, other_ref, spread_ref, gate_ref, gain_ref in chunks:
        half = mine_ref.shape[1]
        for q in range(2 * half // block):
            cols = slice(q * block, (q + 1) * block)
            inner = slice(q * block % half, q * block % half + block)
            mine = mine_ref[:, inner]
            other = other_ref[:, inner]
            state = jnp.where(odd, other, mine) if q * block < half else jnp.where(odd, mine, other)
            gated[:, at : at + block] = dot(out_map, state) * dot(edev, spread_ref[:, cols])
            y_ref = y_refs[q * block // y_refs[0].shape[1]]
            y_at = q * block % y_refs[0].shape[1]
            for c in range(block // 128):
                y_cols = slice(y_at + c * 128, y_at + (c + 1) * 128)
                to = slice(at + c * 128, at + (c + 1) * 128)
                cols = slice(q * block + c * 128, q * block + (c + 1) * 128)
                gain = gain_ref[:, cols]
                for b in range(rows // 64):
                    part = slice(b * 64, (b + 1) * 64)
                    value = (y_ref[part, y_cols].astype(F32) + gated[part, to]) * silu(gate_ref[part, cols].astype(F32))
                    sums[part, :] = sums[part, :] + value * value
                    gated[part, to] = value * gain
            at += block
    if mode == "first":
        squares_ref[...] = sums[...]
    else:
        width = at if mode == "whole" else 2 * at
        mean = jnp.sum(sums[...], axis=1, keepdims=True) * (1.0 / width)
        scale = lax.rsqrt(mean + EPS)
    for p in range(partners):

        @pl.when(pl.program_id(0) // steps == p)
        def _(o_ref=o_refs[p]):
            if mode == "rest":
                step = pl.program_id(0) - p * steps
                start = pl.multiple_of(step * rows, rows)
                high = scale.astype(BF16).astype(F32)
                parts = [jnp.broadcast_to(part, (rows, 128)).T[:8] for part in (high, scale - high)]
                o_ref[steps * rows :, pl.ds(start, rows)] = jnp.concatenate(parts, axis=0).astype(BF16)
            for q in range(at // block):
                cols = slice(q * block, (q + 1) * block)
                value = gated[:, cols] if mode == "first" else gated[:, cols] * scale
                if mode == "rest":
                    o_ref[pl.ds(start, rows), cols] = value.astype(BF16)
                else:
                    o_ref[:, cols] = value.astype(BF16)


def back(mode, some, where, rows, chunks, both_maps, table, spread, gates, gain_row, squares, after, own=None):
    heads2 = spread.shape[0]
    tile = 128
    steps = rows // tile
    partners = len(some)

    def at(i, where):
        turn = some[0]
        for p in range(1, partners):
            turn = jnp.where(i >= p * steps, some[p], turn)
        return ((where[0] ^ turn) * steps + i % steps, 0)

    specs = [
        pl.BlockSpec((tile, STATE), lambda i, where: (at(i, where)[0], 1)),
        pl.BlockSpec((tile, heads2), lambda i, where: (at(i, where)[0], EDEV)),
    ]
    operands = [both_maps, table]
    total = 0
    for (start, width), ys, mine, other in chunks:
        index = start // width
        half = width // 2
        total += width
        specs += [pl.BlockSpec((tile, y.shape[1]), at) for y in ys]
        specs += [
            pl.BlockSpec((STATE, half), lambda i, where: (0, 0)),
            pl.BlockSpec((STATE, half), lambda i, where: (0, 0)),
            pl.BlockSpec((heads2, width), lambda i, where, index=index: (0, index)),
            pl.BlockSpec((tile, width), lambda i, where, index=index: (at(i, where)[0], index)),
            pl.BlockSpec((1, width), lambda i, where, index=index: (0, index)),
        ]
        operands += [*ys, mine, other, spread, gates, gain_row]
    if mode == "rest":
        specs.append(pl.BlockSpec((tile, 128), lambda i, where: (i, 0)))
        operands.append(squares)
    aliases = {}
    if own is not None and own[2] is not None:
        after = [own[2], *after]
        aliases = {1 + len(operands): partners - 1}
    specs += behind(len(after))
    operands += after
    sent = rows + 16 if mode == "rest" else rows
    part = sent if mode == "rest" else tile

    def part_of(p):
        if mode == "rest":
            return lambda i, where: (0, 0)
        return lambda i, where: (jnp.clip(i - p * steps, 0, steps - 1), 0)

    out_specs = [pl.BlockSpec((part, total), part_of(p)) for p in range(partners)]
    out_shape = [jax.ShapeDtypeStruct((sent, total), BF16)] * partners
    if own is not None:
        group, groups, _ = own
        out_specs[-1] = pl.BlockSpec(
            (tile, total),
            lambda i, where: (jnp.clip(i - (partners - 1) * steps, 0, steps - 1), (where[0] ^ some[-1]) * groups + group),
        )
        out_shape[-1] = jax.ShapeDtypeStruct((rows, groups * total * (gates.shape[0] // rows)), BF16)
    if mode == "first":
        out_specs.append(pl.BlockSpec((tile, 128), lambda i, where: (i, 0)))
        out_shape.append(jax.ShapeDtypeStruct((partners * rows, 128), F32))
    return pl.pallas_call(
        functools.partial(back_kernel, mode, [len(ys) for _, ys, _, _ in chunks], partners, len(after)),
        grid_spec=pltpu.PrefetchScalarGridSpec(
            num_scalar_prefetch=1,
            grid=(partners * steps,),
            in_specs=specs,
            out_specs=out_specs,
            scratch_shapes=[pltpu.VMEM((tile, total), F32), pltpu.VMEM((tile, 128), F32)],
        ),
        out_shape=out_shape,
        input_output_aliases=aliases,
        compiler_params=params(),
        name=f"back_{mode}",
        cost_estimate=cost(1),
    )(where, *operands)


def mark_kernel(order, *refs):
    refs[order][...] = jnp.zeros((8, 128), F32)


def mark(after):
    return pl.pallas_call(
        functools.partial(mark_kernel, len(after)),
        grid=(1,),
        in_specs=behind(len(after)),
        out_specs=pl.BlockSpec((8, 128), lambda i: (0, 0)),
        out_shape=jax.ShapeDtypeStruct((8, 128), F32),
        compiler_params=params(VMEM_SMALL),
        name="mark",
        cost_estimate=cost(200),
    )(*after)


def shifted(value, pairs, steps):
    return lax.ppermute(
        value,
        "ctx",
        [(2 * q + y, 2 * (q + steps) + y) for q in range(pairs - steps) for y in range(2)],
    )


def swapped(value, pairs):
    return lax.ppermute(value, "ctx", [(2 * q + y, 2 * q + 1 - y) for q in range(pairs) for y in range(2)])


class Line:
    def __init__(self):
        self.last = []

    def run(self, make, *args, **kwargs):
        made = make(*args, after=self.last, **kwargs)
        self.last = [made[0] if isinstance(made, (list, tuple)) else made]
        return made


class Exchange:
    def __init__(self, line, where, pairs, sent, kept):
        self.line = line
        self.where = where
        self.pairs = pairs
        self.kept = kept
        self.got = swapped(sent, pairs)

    def pair(self):
        self.total, sent = self.line.run(
            join, pair_kernel, "pair", self.where, [self.kept, self.got], ["kept", "sent"]
        )
        self.before = shifted(sent, self.pairs, 1)
        self.reach = 1

    def double(self):
        (sent,) = self.line.run(join, inclusive_kernel, "inclusive", None, [self.total, self.before], ["sent"])
        self.far = shifted(sent, self.pairs, self.reach + 1)
        self.reach = 2 * self.reach + 1

    def extend(self):
        while self.reach < self.pairs - 1:
            (self.before,) = self.line.run(join, extend_kernel, "extend", None, [self.before, self.far], ["kept"])
            self.double()

    def finish(self):
        self.extend()
        self.mine, sent = self.line.run(
            join, last_kernel, "last", self.where, [self.before, self.far, self.kept, self.got], ["state", "state"]
        )
        self.other = swapped(sent, self.pairs)


def shards(
    features, gates, state_io, step_size, log_decay, conv_feat, conv_state, skip_gain, norm_gain
):
    tokens, channels = features.shape
    heads = step_size.shape[0]
    head_dim = channels // heads
    groups = state_io.shape[2] // STATE
    group_width = channels // groups
    width = group_width // 2
    count = conv_feat.shape[0]
    rim = count - 1
    ctx_size = lax.axis_size("ctx")
    head_size = lax.axis_size("head")
    pairs = ctx_size // 2
    rows = tokens // head_size
    me = lax.axis_index("head").astype(jnp.int32)
    where = jnp.stack([me, lax.axis_index("ctx").astype(jnp.int32) % 2])

    onward = [(i, i + 1) for i in range(ctx_size - 1)]
    pad = HALO - rim
    halo = jnp.pad(lax.ppermute(features[tokens - rim :], "ctx", onward), ((pad, 0), (0, 0)))
    io_halo = jnp.pad(lax.ppermute(state_io[tokens - rim :], "ctx", onward), ((pad, 0), (0, 0), (0, 0)))
    spread = jnp.asarray(spread_table(heads, head_dim), BF16)
    halves = jnp.asarray(np.arange(128)[None, :] // head_dim == np.arange(2)[:, None], BF16)
    col, row, table, skips = decay_tables(log_decay, step_size, skip_gain)
    gain_row = norm_gain[None]

    line = Line()
    chunks = [(0, width), (width, width)] + [(g * group_width, group_width) for g in range(1, groups)]
    of_group = [[0, 1]] + [[g + 1] for g in range(1, groups)]
    group_of = [0, 0] + list(range(1, groups))
    fronts = {}
    maps = {}
    exchanges = {}
    ys = {}

    def run_maps(g):
        maps[g] = line.run(maps_of, g, state_io, io_halo, conv_state)

    def run_front(c):
        made = line.run(
            front, chunks[c], where, features, halo, conv_feat, table, spread, maps[group_of[c]][1]
        )
        fronts[c] = made[0]
        exchanges[c] = Exchange(line, where, pairs, made[1], made[2])

    def run_spans(c, part=0, parts=1, micros=200):
        g = group_of[c]
        made = line.run(
            spans_of, chunks[c], part, parts, micros, head_dim, fronts[c], maps[g][0], col, row, table, spread,
            skips, halves,
        )
        ys.setdefault(c, []).append(made)

    def part(c):
        return (chunks[c], ys[c], exchanges[c].mine, exchanges[c].other)

    partners = list(range(head_size - 1, 1, -1))
    squares = {}
    pieces = {}

    def ship(piece, r):
        return lax.ppermute(piece, "head", [(i, i ^ r) for i in range(head_size)])

    def run_back(mode, some, g, parts, squares, own=None):
        return line.run(
            back, mode, some, where, rows, [part(c) for c in parts], maps[g][0], table, spread, gates, gain_row,
            squares, own=own,
        )

    def arrived(g, index, some):
        line.last += [pieces[g, r][index] for r in some]

    def run_first(g, apart=False):
        squares[g] = []
        for some in [[r] for r in partners] if apart else [partners]:
            *made, square = run_back("first", some, g, [0], None)
            squares[g].append((some, square))
            for r, piece in zip(some, made):
                pieces[g, r] = [ship(piece, r)]

    def run_rest(g):
        for some, square in squares[g]:
            made = run_back("rest", some, g, [1], square)
            for r, piece in zip(some, made):
                pieces[g, r].append(ship(piece, r))

    result = None

    def run_one(g, r):
        (piece,) = run_back("whole", [r], g, of_group[g], None)
        pieces[g, r] = [ship(piece, r)]

    def run_own(g):
        nonlocal result
        before = line.last
        (result,) = run_back("whole", [0], g, of_group[g], None, own=(g, groups, result))
        line.last = before

    def run_put(g, r):
        nonlocal result
        start = (me ^ r) * channels + g * group_width
        zero = jnp.int32(0)
        if len(pieces[g, r]) == 2:
            first, rest = pieces[g, r]
            scale = rest[rows, :rows].astype(F32) + rest[rows + 8, :rows].astype(F32)
            first = (first.astype(F32) * scale[:, None]).astype(BF16)
            result = lax.dynamic_update_slice(result, first, (zero, start))
            result = lax.dynamic_update_slice(result, rest[:rows], (zero, start + width))
        else:
            result = lax.dynamic_update_slice(result, pieces[g, r][0], (zero, start))

    ex = exchanges
    later = range(1, groups)
    run_maps(0)
    run_front(0)
    run_front(1)
    ex[0].pair()
    for g in later:
        run_maps(g)
    ex[0].double()
    ex[1].pair()
    for g in later:
        run_front(g + 1)
    run_spans(0)
    ex[0].finish()
    ex[1].double()
    for g in later:
        ex[g + 1].pair()
    run_first(0, apart=True)
    if groups > 1:
        line.run(mark)
    run_spans(1, micros=1)
    ex[1].finish()
    for g in later:
        ex[g + 1].double()
    for g in later:
        run_spans(g + 1, 0, 2, 1)
    arrived(0, 0, partners)
    run_rest(0)
    for g in later:
        ex[g + 1].finish()
        run_spans(g + 1, 1, 2, 1)
    run_one(0, 1)
    for g in later:
        arrived(0, 1, partners[:1])
        run_one(g, partners[0])
        run_one(g, 1)
        arrived(0, 1, partners[1:])
        for r in partners[1:]:
            run_one(g, r)
    run_own(0)
    for r in [*partners, 1]:
        run_put(0, r)
    for g in later:
        run_own(g)
        for r in [partners[0], 1, *partners[1:]]:
            run_put(g, r)
    return result


def solution(mesh):
    in_specs = (
        P("ctx", "head"),
        P("ctx", "head"),
        P("ctx", None, "head"),
        P("head", "ctx"),
        P("head", "ctx"),
        P(None, "head"),
        P(None, None, "head"),
        P("head"),
        P("head"),
    )
    out_specs = P(("ctx", "head"), None)
    return jax.shard_map(shards, mesh=mesh, in_specs=in_specs, out_specs=out_specs, check_vma=False)
```

```python
import functools

import jax
import jax.numpy as jnp
import numpy as np
from jax import lax
from jax.experimental import pallas as pl
from jax.experimental.pallas import tpu as pltpu
from jax.sharding import PartitionSpec as P

STATE = 256
SPAN = 128
HALO = 16
EPS = 1e-05
LOC, ECUM, DEV, EDEV = range(4)
F32 = jnp.float32
BF16 = jnp.bfloat16
VMEM_BYTES = 48 * 1024 * 1024
VMEM_SMALL = 8 * 1024 * 1024
COST_SCALE = 10**9
MSG = STATE + 16
KEPT = STATE + 8


def dot(a, b):
    return jnp.dot(a, b, preferred_element_type=F32)


def silu(v):
    half = 0.5 * v
    return half * jnp.tanh(half) + half


def cost(micros):
    return pl.CostEstimate(flops=int(micros * COST_SCALE), bytes_accessed=1, transcendentals=0)


def params(limit=VMEM_BYTES):
    return pltpu.CompilerParams(vmem_limit_bytes=limit)


def lanes_of(heads):
    return -(-2 * heads // 128) * 128


def spread_table(heads, head_dim):
    row = np.arange(lanes_of(heads))
    head = np.where(row < 2 * heads, row % heads, heads)
    return (head[:, None] == (np.arange(heads * head_dim) // head_dim)[None, :]).astype(np.float32)


def decay_kernel(log_ref, step_ref, skip_ref, col_ref, row_ref, table_ref, skips_ref):
    heads, tokens = log_ref.shape
    lanes = lanes_of(heads)
    spans = tokens // SPAN
    r = lax.broadcasted_iota(jnp.int32, (SPAN, SPAN), 0)
    c = lax.broadcasted_iota(jnp.int32, (SPAN, SPAN), 1)
    upper = (r <= c).astype(F32)
    cums = []
    for k in range(spans):
        cums.append(
            jnp.dot(
                log_ref[:, k * SPAN : (k + 1) * SPAN],
                upper,
                precision=lax.Precision.HIGHEST,
                preferred_element_type=F32,
            )
        )
    totals = [cum[:, SPAN - 1 :] for cum in cums]
    before = [jnp.zeros_like(totals[0])]
    for k in range(spans - 1):
        before.append(before[-1] + totals[k])
    after = [jnp.zeros_like(totals[0])]
    for k in range(spans - 1, 0, -1):
        after.insert(0, after[0] + totals[k])

    def put(index, k, value):
        high = value.astype(BF16).astype(F32)
        rest = [jnp.zeros((lanes - 2 * heads, SPAN), F32)] if lanes > 2 * heads else []
        both = jnp.concatenate([high, value - high, *rest], axis=0)
        table_ref[k * SPAN : (k + 1) * SPAN, index * lanes : (index + 1) * lanes] = both.T.astype(BF16)

    skip = skip_ref[...]
    high = skip.astype(BF16).astype(F32)
    none = [jnp.zeros((1, lanes - 2 * heads), F32)] if lanes > 2 * heads else []
    parts = jnp.concatenate([high, skip - high, *none], axis=1)
    skips_ref[...] = jnp.broadcast_to(parts, skips_ref.shape).astype(BF16)
    for k in range(spans):
        cum = cums[k]
        step = step_ref[:, k * SPAN : (k + 1) * SPAN]
        col_ref[k * SPAN : (k + 1) * SPAN, :] = jnp.concatenate([cum] * (lanes // heads), axis=0).T
        row_ref[:, k * SPAN : (k + 1) * SPAN] = cum - jnp.log(step)
        to_end = totals[k] - cum
        put(LOC, k, jnp.exp(to_end) * step)
        put(DEV, k, jnp.exp(to_end + after[k]) * step)
        put(ECUM, k, jnp.exp(cum))
        put(EDEV, k, jnp.exp(cum + before[k]))


def behind(count):
    return [pl.BlockSpec(memory_space=pl.ANY)] * count


def decay_tables(log_decay, step_size, skip_gain):
    heads, tokens = log_decay.shape
    lanes = lanes_of(heads)
    return pl.pallas_call(
        decay_kernel,
        out_shape=(
            jax.ShapeDtypeStruct((tokens, lanes), F32),
            jax.ShapeDtypeStruct((heads, tokens), F32),
            jax.ShapeDtypeStruct((tokens, 4 * lanes), BF16),
            jax.ShapeDtypeStruct((16, lanes), BF16),
        ),
        compiler_params=params(),
        name="decays",
        cost_estimate=cost(1.5),
    )(log_decay, step_size, skip_gain[None])


def conv_rows(read, rows, halo, taps, store):
    count, width = taps.shape
    tile = SPAN
    for b in range(rows // tile):
        for c in range(1):
            cols = slice(0, width)
            own = read(b * tile, (b + 1) * tile, cols).astype(F32)
            prev = (halo[:, cols] if b == 0 else read(b * tile - HALO, b * tile, cols)).astype(F32)
            both = jnp.concatenate([prev[HALO - 8 :], own], axis=0)
            total = own * taps[count - 1 : count, cols]
            for k in range(1, count):
                total = total + both[8 - k : 8 - k + tile] * taps[count - 1 - k : count - k, cols]
            store(slice(b * tile, (b + 1) * tile), cols, silu(total))


def read_state(ref):
    if ref.dtype == F32:
        return ref[:STATE, :], ref[STATE : STATE + 1, :]
    tail = ref[STATE:MSG, :].astype(F32)
    return ref[:STATE, :].astype(F32), tail[0:1] + tail[8:9]


def write_kept(ref, value, decay):
    ref[:STATE, :] = value
    ref[STATE:KEPT, :] = jnp.broadcast_to(decay, (KEPT - STATE, decay.shape[1]))


def write_sent(ref, value, decay):
    ref[:STATE, :] = value.astype(BF16)
    high = decay.astype(BF16).astype(F32)
    shape = (8, decay.shape[1])
    rows = jnp.concatenate([jnp.broadcast_to(high, shape), jnp.broadcast_to(decay - high, shape)], axis=0)
    ref[STATE:MSG, :] = rows.astype(BF16)


def maps_kernel(order, io_ref, halo_ref, taps_ref, *refs):
    map_ref, turned_ref = refs[order:]

    def put_in(rows, cols, value):
        map_ref[rows, :STATE] = value.astype(BF16)

    def put_out(rows, cols, value):
        map_ref[rows, STATE:] = value.astype(BF16)

    tokens = io_ref.shape[0]
    for i, put in ((0, put_in), (1, put_out)):
        conv_rows(
            lambda lo, hi, cols: io_ref[lo:hi, i, cols], tokens, halo_ref[:, i, :], taps_ref[:, i, :].astype(F32), put
        )
    for b in range(tokens // SPAN):
        rows = slice(b * SPAN, (b + 1) * SPAN)
        turned_ref[:, rows] = map_ref[rows, :STATE].T


def maps_of(group, state_io, halo, conv_state, after):
    tokens = state_io.shape[0]
    count = conv_state.shape[0]

    def mine(j):
        return (0, 0, group)

    return pl.pallas_call(
        functools.partial(maps_kernel, len(after)),
        grid=(1,),
        in_specs=[
            pl.BlockSpec((tokens, 2, STATE), mine),
            pl.BlockSpec((HALO, 2, STATE), mine),
            pl.BlockSpec((count, 2, STATE), mine),
            *behind(len(after)),
        ],
        out_specs=[
            pl.BlockSpec((tokens, 2 * STATE), lambda j: (0, 0)),
            pl.BlockSpec((STATE, tokens), lambda j: (0, 0)),
        ],
        out_shape=[
            jax.ShapeDtypeStruct((tokens, 2 * STATE), BF16),
            jax.ShapeDtypeStruct((STATE, tokens), BF16),
        ],
        compiler_params=params(),
        name="maps",
        cost_estimate=cost(3),
    )(state_io, halo, conv_state, *after)


def front_kernel(order, blocks, where_ref, feat_ref, halo_ref, taps_ref, dev_ref, edev_ref, spread_ref, turned_ref, *refs):
    xh_ref, sent_ref, kept_ref, scaled, wide = refs[order:]
    j = pl.program_id(0)
    spread = spread_ref[...]
    wide[...] = dot(dev_ref[...], spread)

    def put_feat(rows, cols, value):
        value = value.astype(BF16)
        xh_ref[rows, cols] = value
        scaled[rows, cols] = (value.astype(F32) * wide[rows, cols]).astype(BF16)

    conv_rows(
        lambda lo, hi, cols: feat_ref[lo:hi, cols], feat_ref.shape[0], halo_ref[...], taps_ref[...].astype(F32), put_feat
    )
    state = dot(turned_ref[...], scaled[...])
    decay = dot(edev_ref[...], spread)[15:16]

    @pl.when(j < blocks)
    def _():
        write_sent(sent_ref, state, decay)

    @pl.when(j >= blocks)
    def _():
        write_kept(kept_ref, state, decay)


def front(chunk, where, features, halo, conv_feat, table, spread, turned, after):
    tokens = features.shape[0]
    start, width = chunk
    half = width // 2
    block = min(512, half)
    blocks = half // block
    base = start // block
    count = conv_feat.shape[0]
    heads2 = spread.shape[0]

    def place(j, where):
        sending = (j < blocks).astype(jnp.int32)
        which = sending * (1 - where[1]) + (1 - sending) * where[1]
        return which * blocks + j - (1 - sending) * blocks

    def cols(j, where):
        return (0, base + place(j, where))

    def same(j, where):
        return (0, 0)

    return pl.pallas_call(
        functools.partial(front_kernel, len(after), blocks),
        grid_spec=pltpu.PrefetchScalarGridSpec(
            num_scalar_prefetch=1,
            grid=(2 * blocks,),
            in_specs=[
                pl.BlockSpec((tokens, block), cols),
                pl.BlockSpec((HALO, block), cols),
                pl.BlockSpec((count, block), cols),
                pl.BlockSpec((tokens, heads2), lambda j, where: (0, DEV)),
                pl.BlockSpec((16, heads2), lambda j, where: (tokens // 16 - 1, EDEV)),
                pl.BlockSpec((heads2, block), cols),
                pl.BlockSpec((STATE, tokens), same),
                *behind(len(after)),
            ],
            out_specs=[
                pl.BlockSpec((tokens, block), lambda j, where: (0, place(j, where))),
                pl.BlockSpec((MSG, block), lambda j, where: (0, jnp.minimum(j, blocks - 1))),
                pl.BlockSpec((KEPT, block), lambda j, where: (0, jnp.maximum(j - blocks, 0))),
            ],
            scratch_shapes=[pltpu.VMEM((tokens, block), BF16), pltpu.VMEM((tokens, block), F32)],
        ),
        out_shape=[
            jax.ShapeDtypeStruct((tokens, width), BF16),
            jax.ShapeDtypeStruct((MSG, half), BF16),
            jax.ShapeDtypeStruct((KEPT, half), F32),
        ],
        compiler_params=params(),
        name="front",
        cost_estimate=cost(4),
    )(where, features, halo, conv_feat, table, table, spread, turned, *after)


def span_kernel(
    first_head, order, xh_ref, map_ref, col_ref, row_ref, table_ref, spread_ref, skips_ref, halves_ref,
    *refs,
):
    y_ref, state = refs[order:]
    width = xh_ref.shape[1]
    head_dim = width // row_ref.shape[0]
    heads2 = spread_ref.shape[0]

    @pl.when(pl.program_id(0) == 0)
    def _():
        state[...] = jnp.zeros_like(state)

    t = lax.broadcasted_iota(jnp.int32, (SPAN, SPAN), 0)
    s = lax.broadcasted_iota(jnp.int32, (SPAN, SPAN), 1)
    first = halves_ref[0:1, :]
    second = halves_ref[1:2, :]
    block = 256
    for k in range(xh_ref.shape[0] // SPAN):
        rows = slice(k * SPAN, (k + 1) * SPAN)
        in_map = map_ref[rows, :STATE]
        out_map = map_ref[rows, STATE:]
        scores = lax.dot_general(out_map, in_map, (((1,), (1,)), ((), ())), preferred_element_type=F32)
        scores = jnp.where(s <= t, scores, 0.0)
        in_turned = in_map.T
        tables = jnp.concatenate([table_ref[rows, :heads2], table_ref[rows, heads2:], skips_ref[...]], axis=0)
        for q in range(width // block):
            cols = slice(q * block, (q + 1) * block)
            feats = xh_ref[rows, cols]
            feats32 = feats.astype(F32)
            wide = dot(tables, spread_ref[:, cols])
            scaled = (feats32 * wide[:SPAN]).astype(BF16)
            ecum = wide[SPAN : 2 * SPAN]
            skip = wide[2 * SPAN : 2 * SPAN + 1]
            pairs = []
            for p in range(block // 128):
                weights = []
                for i in range(2):
                    h = (q * block + p * 128) // head_dim + i
                    gap = col_ref[rows, first_head + h : first_head + h + 1] - row_ref[h : h + 1, rows]
                    weights.append((scores * jnp.exp(jnp.minimum(gap, 0.0))).astype(BF16))
                pair = feats[:, p * 128 : (p + 1) * 128]
                stacked = jnp.concatenate([pair * first, pair * second], axis=0)
                pairs.append(dot(jnp.concatenate(weights, axis=1), stacked))
            diag = jnp.concatenate(pairs, axis=1)
            held = state[:, cols]
            carried = dot(out_map, held.astype(BF16)) * ecum
            y_ref[rows, cols] = (diag + carried + skip * feats32).astype(BF16)
            state[:, cols] = ecum[SPAN - 1 :] * held + dot(in_turned, scaled)


def spans_of(chunk, part, parts, micros, head_dim, xh, both_maps, col, row, table, spread, skips, halves, after):
    tokens = xh.shape[0]
    width = chunk[1] // parts
    index = chunk[0] // width + part
    some = width // head_dim
    heads2 = spread.shape[0]
    tile = 2 * SPAN
    return pl.pallas_call(
        functools.partial(span_kernel, index * some, len(after)),
        grid=(tokens // tile,),
        in_specs=[
            pl.BlockSpec((tile, width), lambda k: (k, part)),
            pl.BlockSpec((tile, 2 * STATE), lambda k: (k, 0)),
            pl.BlockSpec((tile, heads2), lambda k: (k, 0)),
            pl.BlockSpec((some, tile), lambda k: (index, k)),
            pl.BlockSpec((tile, 2 * heads2), lambda k: (k, 0)),
            pl.BlockSpec((heads2, width), lambda k: (0, index)),
            pl.BlockSpec(skips.shape, lambda k: (0, 0)),
            pl.BlockSpec(halves.shape, lambda k: (0, 0)),
            *behind(len(after)),
        ],
        out_specs=pl.BlockSpec((tile, width), lambda k: (k, 0)),
        out_shape=jax.ShapeDtypeStruct((tokens, width), BF16),
        scratch_shapes=[pltpu.VMEM((STATE, width), F32)],
        compiler_params=params(),
        name="spans",
        cost_estimate=cost(micros),
    )(xh, both_maps, col, row, table, spread, skips, halves, *after)


def pair_kernel(where_ref, kept_ref, got_ref, *refs):
    total_ref, sent_ref = refs[-2:]
    kept, kept_decay = read_state(kept_ref)
    got, got_decay = read_state(got_ref)

    def put(first, second, decay):
        total = decay * first + second
        write_kept(total_ref, total, kept_decay * got_decay)
        write_sent(sent_ref, total, kept_decay * got_decay)

    @pl.when(where_ref[1] == 0)
    def _():
        put(kept, got, got_decay)

    @pl.when(where_ref[1] == 1)
    def _():
        put(got, kept, kept_decay)


def inclusive_kernel(total_ref, before_ref, *refs):
    sent_ref = refs[-1]
    total, decay = read_state(total_ref)
    before, before_decay = read_state(before_ref)
    write_sent(sent_ref, total + decay * before, decay * before_decay)


def extend_kernel(before_ref, far_ref, *refs):
    before, decay = read_state(before_ref)
    far, far_decay = read_state(far_ref)
    write_kept(refs[-1], before + decay * far, decay * far_decay)


def last_kernel(where_ref, before_ref, far_ref, kept_ref, got_ref, *refs):
    mine_ref, sent_ref = refs[-2:]
    before, before_decay = read_state(before_ref)
    far, _ = read_state(far_ref)
    carried = before + before_decay * far

    @pl.when(where_ref[1] == 0)
    def _():
        kept, decay = read_state(kept_ref)
        mine_ref[...] = carried.astype(BF16)
        sent_ref[...] = (decay * carried + kept).astype(BF16)

    @pl.when(where_ref[1] == 1)
    def _():
        got, decay = read_state(got_ref)
        mine_ref[...] = (decay * carried + got).astype(BF16)
        sent_ref[...] = carried.astype(BF16)


def join(kernel, name, where, operands, outs, after):
    width = operands[0].shape[1]
    shapes = {
        "kept": jax.ShapeDtypeStruct((KEPT, width), F32),
        "sent": jax.ShapeDtypeStruct((MSG, width), BF16),
        "state": jax.ShapeDtypeStruct((STATE, width), BF16),
    }
    scalars = [] if where is None else [where]
    return pl.pallas_call(
        kernel,
        in_specs=[pl.BlockSpec(memory_space=pltpu.SMEM)] * len(scalars)
        + [pl.BlockSpec(memory_space=pltpu.VMEM)] * len(operands)
        + behind(len(after)),
        out_specs=[pl.BlockSpec(memory_space=pltpu.VMEM)] * len(outs),
        out_shape=[shapes[out] for out in outs],
        compiler_params=params(VMEM_SMALL),
        name=name,
        cost_estimate=cost(0.7),
    )(*scalars, *operands, *after)


def back_kernel(mode, counts, partners, order, where_ref, out_ref, edev_ref, *refs):
    chunks = []
    for pieces in counts:
        chunks.append((refs[:pieces], *refs[pieces : pieces + 5]))
        refs = refs[pieces + 5 :]
    if mode == "rest":
        squares_ref, *refs = refs
    refs = refs[order:]
    o_refs = refs[:partners]
    if mode == "first":
        squares_ref = refs[partners]
    gated, sums = refs[-2:]
    out_map = out_ref[...]
    edev = edev_ref[...]
    rows = out_map.shape[0]
    block = 256
    steps = pl.num_programs(0) // partners
    odd = where_ref[1] == 1
    sums[...] = squares_ref[...] if mode == "rest" else jnp.zeros((rows, 128), F32)
    at = 0
    for y_refs, mine_ref, other_ref, spread_ref, gate_ref, gain_ref in chunks:
        half = mine_ref.shape[1]
        for q in range(2 * half // block):
            cols = slice(q * block, (q + 1) * block)
            inner = slice(q * block % half, q * block % half + block)
            mine = mine_ref[:, inner]
            other = other_ref[:, inner]
            state = jnp.where(odd, other, mine) if q * block < half else jnp.where(odd, mine, other)
            gated[:, at : at + block] = dot(out_map, state) * dot(edev, spread_ref[:, cols])
            y_ref = y_refs[q * block // y_refs[0].shape[1]]
            y_at = q * block % y_refs[0].shape[1]
            for c in range(block // 128):
                y_cols = slice(y_at + c * 128, y_at + (c + 1) * 128)
                to = slice(at + c * 128, at + (c + 1) * 128)
                cols = slice(q * block + c * 128, q * block + (c + 1) * 128)
                gain = gain_ref[:, cols]
                for b in range(rows // 64):
                    part = slice(b * 64, (b + 1) * 64)
                    value = (y_ref[part, y_cols].astype(F32) + gated[part, to]) * silu(gate_ref[part, cols].astype(F32))
                    sums[part, :] = sums[part, :] + value * value
                    gated[part, to] = value * gain
            at += block
    if mode == "first":
        squares_ref[...] = sums[...]
    else:
        width = at if mode == "whole" else 2 * at
        mean = jnp.sum(sums[...], axis=1, keepdims=True) * (1.0 / width)
        scale = lax.rsqrt(mean + EPS)
    for p in range(partners):

        @pl.when(pl.program_id(0) // steps == p)
        def _(o_ref=o_refs[p]):
            if mode == "rest":
                step = pl.program_id(0) - p * steps
                start = pl.multiple_of(step * rows, rows)
                high = scale.astype(BF16).astype(F32)
                parts = [jnp.broadcast_to(part, (rows, 128)).T[:8] for part in (high, scale - high)]
                o_ref[steps * rows :, pl.ds(start, rows)] = jnp.concatenate(parts, axis=0).astype(BF16)
            for q in range(at // block):
                cols = slice(q * block, (q + 1) * block)
                value = gated[:, cols] if mode == "first" else gated[:, cols] * scale
                if mode == "rest":
                    o_ref[pl.ds(start, rows), cols] = value.astype(BF16)
                else:
                    o_ref[:, cols] = value.astype(BF16)


def back(mode, some, where, rows, chunks, both_maps, table, spread, gates, gain_row, squares, after, own=None):
    heads2 = spread.shape[0]
    tile = 128
    steps = rows // tile
    partners = len(some)

    def at(i, where):
        turn = some[0]
        for p in range(1, partners):
            turn = jnp.where(i >= p * steps, some[p], turn)
        return ((where[0] ^ turn) * steps + i % steps, 0)

    specs = [
        pl.BlockSpec((tile, STATE), lambda i, where: (at(i, where)[0], 1)),
        pl.BlockSpec((tile, heads2), lambda i, where: (at(i, where)[0], EDEV)),
    ]
    operands = [both_maps, table]
    total = 0
    for (start, width), ys, mine, other in chunks:
        index = start // width
        half = width // 2
        total += width
        specs += [pl.BlockSpec((tile, y.shape[1]), at) for y in ys]
        specs += [
            pl.BlockSpec((STATE, half), lambda i, where: (0, 0)),
            pl.BlockSpec((STATE, half), lambda i, where: (0, 0)),
            pl.BlockSpec((heads2, width), lambda i, where, index=index: (0, index)),
            pl.BlockSpec((tile, width), lambda i, where, index=index: (at(i, where)[0], index)),
            pl.BlockSpec((1, width), lambda i, where, index=index: (0, index)),
        ]
        operands += [*ys, mine, other, spread, gates, gain_row]
    if mode == "rest":
        specs.append(pl.BlockSpec((tile, 128), lambda i, where: (i, 0)))
        operands.append(squares)
    aliases = {}
    if own is not None and own[2] is not None:
        after = [own[2], *after]
        aliases = {1 + len(operands): partners - 1}
    specs += behind(len(after))
    operands += after
    sent = rows + 16 if mode == "rest" else rows
    part = sent if mode == "rest" else tile

    def part_of(p):
        if mode == "rest":
            return lambda i, where: (0, 0)
        return lambda i, where: (jnp.clip(i - p * steps, 0, steps - 1), 0)

    out_specs = [pl.BlockSpec((part, total), part_of(p)) for p in range(partners)]
    out_shape = [jax.ShapeDtypeStruct((sent, total), BF16)] * partners
    if own is not None:
        group, groups, _ = own
        out_specs[-1] = pl.BlockSpec(
            (tile, total),
            lambda i, where: (jnp.clip(i - (partners - 1) * steps, 0, steps - 1), (where[0] ^ some[-1]) * groups + group),
        )
        out_shape[-1] = jax.ShapeDtypeStruct((rows, groups * total * (gates.shape[0] // rows)), BF16)
    if mode == "first":
        out_specs.append(pl.BlockSpec((tile, 128), lambda i, where: (i, 0)))
        out_shape.append(jax.ShapeDtypeStruct((partners * rows, 128), F32))
    return pl.pallas_call(
        functools.partial(back_kernel, mode, [len(ys) for _, ys, _, _ in chunks], partners, len(after)),
        grid_spec=pltpu.PrefetchScalarGridSpec(
            num_scalar_prefetch=1,
            grid=(partners * steps,),
            in_specs=specs,
            out_specs=out_specs,
            scratch_shapes=[pltpu.VMEM((tile, total), F32), pltpu.VMEM((tile, 128), F32)],
        ),
        out_shape=out_shape,
        input_output_aliases=aliases,
        compiler_params=params(),
        name=f"back_{mode}",
        cost_estimate=cost(1),
    )(where, *operands)


def mark_kernel(order, *refs):
    refs[order][...] = jnp.zeros((8, 128), F32)


def mark(after):
    return pl.pallas_call(
        functools.partial(mark_kernel, len(after)),
        grid=(1,),
        in_specs=behind(len(after)),
        out_specs=pl.BlockSpec((8, 128), lambda i: (0, 0)),
        out_shape=jax.ShapeDtypeStruct((8, 128), F32),
        compiler_params=params(VMEM_SMALL),
        name="mark",
        cost_estimate=cost(200),
    )(*after)


def shifted(value, pairs, steps):
    return lax.ppermute(
        value,
        "ctx",
        [(2 * q + y, 2 * (q + steps) + y) for q in range(pairs - steps) for y in range(2)],
    )


def swapped(value, pairs):
    return lax.ppermute(value, "ctx", [(2 * q + y, 2 * q + 1 - y) for q in range(pairs) for y in range(2)])


class Line:
    def __init__(self):
        self.last = []

    def run(self, make, *args, **kwargs):
        made = make(*args, after=self.last, **kwargs)
        self.last = [made[0] if isinstance(made, (list, tuple)) else made]
        return made


class Exchange:
    def __init__(self, line, where, pairs, sent, kept):
        self.line = line
        self.where = where
        self.pairs = pairs
        self.kept = kept
        self.got = swapped(sent, pairs)

    def pair(self):
        self.total, sent = self.line.run(
            join, pair_kernel, "pair", self.where, [self.kept, self.got], ["kept", "sent"]
        )
        self.before = shifted(sent, self.pairs, 1)
        self.reach = 1

    def double(self):
        (sent,) = self.line.run(join, inclusive_kernel, "inclusive", None, [self.total, self.before], ["sent"])
        self.far = shifted(sent, self.pairs, self.reach + 1)
        self.reach = 2 * self.reach + 1

    def extend(self):
        while self.reach < self.pairs - 1:
            (self.before,) = self.line.run(join, extend_kernel, "extend", None, [self.before, self.far], ["kept"])
            self.double()

    def finish(self):
        self.extend()
        self.mine, sent = self.line.run(
            join, last_kernel, "last", self.where, [self.before, self.far, self.kept, self.got], ["state", "state"]
        )
        self.other = swapped(sent, self.pairs)


def shards(
    features, gates, state_io, step_size, log_decay, conv_feat, conv_state, skip_gain, norm_gain
):
    tokens, channels = features.shape
    heads = step_size.shape[0]
    head_dim = channels // heads
    groups = state_io.shape[2] // STATE
    group_width = channels // groups
    width = group_width // 2
    count = conv_feat.shape[0]
    rim = count - 1
    ctx_size = lax.axis_size("ctx")
    head_size = lax.axis_size("head")
    pairs = ctx_size // 2
    rows = tokens // head_size
    me = lax.axis_index("head").astype(jnp.int32)
    where = jnp.stack([me, lax.axis_index("ctx").astype(jnp.int32) % 2])

    onward = [(i, i + 1) for i in range(ctx_size - 1)]
    pad = HALO - rim
    halo = jnp.pad(lax.ppermute(features[tokens - rim :], "ctx", onward), ((pad, 0), (0, 0)))
    io_halo = jnp.pad(lax.ppermute(state_io[tokens - rim :], "ctx", onward), ((pad, 0), (0, 0), (0, 0)))
    spread = jnp.asarray(spread_table(heads, head_dim), BF16)
    halves = jnp.asarray(np.arange(128)[None, :] // head_dim == np.arange(2)[:, None], BF16)
    col, row, table, skips = decay_tables(log_decay, step_size, skip_gain)
    gain_row = norm_gain[None]

    line = Line()
    chunks = [(0, width), (width, width)] + [(g * group_width, group_width) for g in range(1, groups)]
    of_group = [[0, 1]] + [[g + 1] for g in range(1, groups)]
    group_of = [0, 0] + list(range(1, groups))
    fronts = {}
    maps = {}
    exchanges = {}
    ys = {}

    def run_maps(g):
        maps[g] = line.run(maps_of, g, state_io, io_halo, conv_state)

    def run_front(c):
        made = line.run(
            front, chunks[c], where, features, halo, conv_feat, table, spread, maps[group_of[c]][1]
        )
        fronts[c] = made[0]
        exchanges[c] = Exchange(line, where, pairs, made[1], made[2])

    def run_spans(c, part=0, parts=1, micros=200):
        g = group_of[c]
        made = line.run(
            spans_of, chunks[c], part, parts, micros, head_dim, fronts[c], maps[g][0], col, row, table, spread,
            skips, halves,
        )
        ys.setdefault(c, []).append(made)

    def part(c):
        return (chunks[c], ys[c], exchanges[c].mine, exchanges[c].other)

    partners = list(range(head_size - 1, 1, -1))
    squares = {}
    pieces = {}

    def ship(piece, r):
        return lax.ppermute(piece, "head", [(i, i ^ r) for i in range(head_size)])

    def run_back(mode, some, g, parts, squares, own=None):
        return line.run(
            back, mode, some, where, rows, [part(c) for c in parts], maps[g][0], table, spread, gates, gain_row,
            squares, own=own,
        )

    def arrived(g, index, some):
        line.last += [pieces[g, r][index] for r in some]

    def run_first(g, apart=False):
        squares[g] = []
        for some in [[r] for r in partners] if apart else [partners]:
            *made, square = run_back("first", some, g, [0], None)
            squares[g].append((some, square))
            for r, piece in zip(some, made):
                pieces[g, r] = [ship(piece, r)]

    def run_rest(g):
        for some, square in squares[g]:
            made = run_back("rest", some, g, [1], square)
            for r, piece in zip(some, made):
                pieces[g, r].append(ship(piece, r))

    result = None

    def run_one(g, r):
        (piece,) = run_back("whole", [r], g, of_group[g], None)
        pieces[g, r] = [ship(piece, r)]

    def run_own(g):
        nonlocal result
        before = line.last
        (result,) = run_back("whole", [0], g, of_group[g], None, own=(g, groups, result))
        line.last = before

    def run_put(g, r):
        nonlocal result
        start = (me ^ r) * channels + g * group_width
        zero = jnp.int32(0)
        if len(pieces[g, r]) == 2:
            first, rest = pieces[g, r]
            scale = rest[rows, :rows].astype(F32) + rest[rows + 8, :rows].astype(F32)
            first = (first.astype(F32) * scale[:, None]).astype(BF16)
            result = lax.dynamic_update_slice(result, first, (zero, start))
            result = lax.dynamic_update_slice(result, rest[:rows], (zero, start + width))
        else:
            result = lax.dynamic_update_slice(result, pieces[g, r][0], (zero, start))

    ex = exchanges
    later = range(1, groups)
    run_maps(0)
    run_front(0)
    run_front(1)
    ex[0].pair()
    for g in later:
        run_maps(g)
    ex[0].double()
    ex[1].pair()
    for g in later:
        run_front(g + 1)
    run_spans(0)
    ex[0].finish()
    ex[1].double()
    for g in later:
        ex[g + 1].pair()
    run_first(0, apart=True)
    if groups > 1:
        line.run(mark)
    run_spans(1, micros=1)
    ex[1].finish()
    for g in later:
        ex[g + 1].double()
    for g in later:
        run_spans(g + 1, 0, 2, 1)
    arrived(0, 0, partners)
    run_rest(0)
    for g in later:
        run_spans(g + 1, 1, 2, 1)
        ex[g + 1].finish()
    run_one(0, 1)
    for g in later:
        arrived(0, 1, partners[:1])
        run_one(g, partners[0])
        run_one(g, 1)
        arrived(0, 1, partners[1:])
        for r in partners[1:]:
            run_one(g, r)
    run_own(0)
    for r in [*partners, 1]:
        run_put(0, r)
    for g in later:
        run_own(g)
        for r in [partners[0], 1, *partners[1:]]:
            run_put(g, r)
    return result


def solution(mesh):
    in_specs = (
        P("ctx", "head"),
        P("ctx", "head"),
        P("ctx", None, "head"),
        P("head", "ctx"),
        P("head", "ctx"),
        P(None, "head"),
        P(None, None, "head"),
        P("head"),
        P("head"),
    )
    out_specs = P(("ctx", "head"), None)
    return jax.shard_map(shards, mesh=mesh, in_specs=in_specs, out_specs=out_specs, check_vma=False)
```

```python
import functools

import jax
import jax.numpy as jnp
import numpy as np
from jax import lax
from jax.experimental import pallas as pl
from jax.experimental.pallas import tpu as pltpu
from jax.sharding import PartitionSpec as P

STATE = 256
SPAN = 128
HALO = 16
EPS = 1e-05
LOC, ECUM, DEV, EDEV = range(4)
F32 = jnp.float32
BF16 = jnp.bfloat16
VMEM_BYTES = 48 * 1024 * 1024
VMEM_SMALL = 8 * 1024 * 1024
COST_SCALE = 10**9
MSG = STATE + 16
KEPT = STATE + 8


def dot(a, b):
    return jnp.dot(a, b, preferred_element_type=F32)


def silu(v):
    half = 0.5 * v
    return half * jnp.tanh(half) + half


def cost(micros):
    return pl.CostEstimate(flops=int(micros * COST_SCALE), bytes_accessed=1, transcendentals=0)


def params(limit=VMEM_BYTES):
    return pltpu.CompilerParams(vmem_limit_bytes=limit)


def lanes_of(heads):
    return -(-2 * heads // 128) * 128


def spread_table(heads, head_dim):
    row = np.arange(lanes_of(heads))
    head = np.where(row < 2 * heads, row % heads, heads)
    return (head[:, None] == (np.arange(heads * head_dim) // head_dim)[None, :]).astype(np.float32)


def decay_kernel(log_ref, step_ref, skip_ref, col_ref, row_ref, table_ref, skips_ref):
    heads, tokens = log_ref.shape
    lanes = lanes_of(heads)
    spans = tokens // SPAN
    r = lax.broadcasted_iota(jnp.int32, (SPAN, SPAN), 0)
    c = lax.broadcasted_iota(jnp.int32, (SPAN, SPAN), 1)
    upper = (r <= c).astype(F32)
    cums = []
    for k in range(spans):
        cums.append(
            jnp.dot(
                log_ref[:, k * SPAN : (k + 1) * SPAN],
                upper,
                precision=lax.Precision.HIGHEST,
                preferred_element_type=F32,
            )
        )
    totals = [cum[:, SPAN - 1 :] for cum in cums]
    before = [jnp.zeros_like(totals[0])]
    for k in range(spans - 1):
        before.append(before[-1] + totals[k])
    after = [jnp.zeros_like(totals[0])]
    for k in range(spans - 1, 0, -1):
        after.insert(0, after[0] + totals[k])

    def put(index, k, value):
        high = value.astype(BF16).astype(F32)
        rest = [jnp.zeros((lanes - 2 * heads, SPAN), F32)] if lanes > 2 * heads else []
        both = jnp.concatenate([high, value - high, *rest], axis=0)
        table_ref[k * SPAN : (k + 1) * SPAN, index * lanes : (index + 1) * lanes] = both.T.astype(BF16)

    skip = skip_ref[...]
    high = skip.astype(BF16).astype(F32)
    none = [jnp.zeros((1, lanes - 2 * heads), F32)] if lanes > 2 * heads else []
    parts = jnp.concatenate([high, skip - high, *none], axis=1)
    skips_ref[...] = jnp.broadcast_to(parts, skips_ref.shape).astype(BF16)
    for k in range(spans):
        cum = cums[k]
        step = step_ref[:, k * SPAN : (k + 1) * SPAN]
        col_ref[k * SPAN : (k + 1) * SPAN, :] = jnp.concatenate([cum] * (lanes // heads), axis=0).T
        row_ref[:, k * SPAN : (k + 1) * SPAN] = cum - jnp.log(step)
        to_end = totals[k] - cum
        put(LOC, k, jnp.exp(to_end) * step)
        put(DEV, k, jnp.exp(to_end + after[k]) * step)
        put(ECUM, k, jnp.exp(cum))
        put(EDEV, k, jnp.exp(cum + before[k]))


def behind(count):
    return [pl.BlockSpec(memory_space=pl.ANY)] * count


def decay_tables(log_decay, step_size, skip_gain):
    heads, tokens = log_decay.shape
    lanes = lanes_of(heads)
    return pl.pallas_call(
        decay_kernel,
        out_shape=(
            jax.ShapeDtypeStruct((tokens, lanes), F32),
            jax.ShapeDtypeStruct((heads, tokens), F32),
            jax.ShapeDtypeStruct((tokens, 4 * lanes), BF16),
            jax.ShapeDtypeStruct((16, lanes), BF16),
        ),
        compiler_params=params(),
        name="decays",
        cost_estimate=cost(1.5),
    )(log_decay, step_size, skip_gain[None])


def conv_rows(read, rows, halo, taps, store):
    count, width = taps.shape
    tile = SPAN
    for b in range(rows // tile):
        for c in range(1):
            cols = slice(0, width)
            own = read(b * tile, (b + 1) * tile, cols).astype(F32)
            prev = (halo[:, cols] if b == 0 else read(b * tile - HALO, b * tile, cols)).astype(F32)
            both = jnp.concatenate([prev[HALO - 8 :], own], axis=0)
            total = own * taps[count - 1 : count, cols]
            for k in range(1, count):
                total = total + both[8 - k : 8 - k + tile] * taps[count - 1 - k : count - k, cols]
            store(slice(b * tile, (b + 1) * tile), cols, silu(total))


def read_state(ref):
    if ref.dtype == F32:
        return ref[:STATE, :], ref[STATE : STATE + 1, :]
    tail = ref[STATE:MSG, :].astype(F32)
    return ref[:STATE, :].astype(F32), tail[0:1] + tail[8:9]


def write_kept(ref, value, decay):
    ref[:STATE, :] = value
    ref[STATE:KEPT, :] = jnp.broadcast_to(decay, (KEPT - STATE, decay.shape[1]))


def write_sent(ref, value, decay):
    ref[:STATE, :] = value.astype(BF16)
    high = decay.astype(BF16).astype(F32)
    shape = (8, decay.shape[1])
    rows = jnp.concatenate([jnp.broadcast_to(high, shape), jnp.broadcast_to(decay - high, shape)], axis=0)
    ref[STATE:MSG, :] = rows.astype(BF16)


def maps_kernel(order, io_ref, halo_ref, taps_ref, *refs):
    map_ref, turned_ref = refs[order:]

    def put_in(rows, cols, value):
        map_ref[rows, :STATE] = value.astype(BF16)

    def put_out(rows, cols, value):
        map_ref[rows, STATE:] = value.astype(BF16)

    tokens = io_ref.shape[0]
    for i, put in ((0, put_in), (1, put_out)):
        conv_rows(
            lambda lo, hi, cols: io_ref[lo:hi, i, cols], tokens, halo_ref[:, i, :], taps_ref[:, i, :].astype(F32), put
        )
    for b in range(tokens // SPAN):
        rows = slice(b * SPAN, (b + 1) * SPAN)
        turned_ref[:, rows] = map_ref[rows, :STATE].T


def maps_of(group, state_io, halo, conv_state, after):
    tokens = state_io.shape[0]
    count = conv_state.shape[0]

    def mine(j):
        return (0, 0, group)

    return pl.pallas_call(
        functools.partial(maps_kernel, len(after)),
        grid=(1,),
        in_specs=[
            pl.BlockSpec((tokens, 2, STATE), mine),
            pl.BlockSpec((HALO, 2, STATE), mine),
            pl.BlockSpec((count, 2, STATE), mine),
            *behind(len(after)),
        ],
        out_specs=[
            pl.BlockSpec((tokens, 2 * STATE), lambda j: (0, 0)),
            pl.BlockSpec((STATE, tokens), lambda j: (0, 0)),
        ],
        out_shape=[
            jax.ShapeDtypeStruct((tokens, 2 * STATE), BF16),
            jax.ShapeDtypeStruct((STATE, tokens), BF16),
        ],
        compiler_params=params(),
        name="maps",
        cost_estimate=cost(3),
    )(state_io, halo, conv_state, *after)


def front_kernel(order, blocks, where_ref, feat_ref, halo_ref, taps_ref, dev_ref, edev_ref, spread_ref, turned_ref, *refs):
    xh_ref, sent_ref, kept_ref, scaled, wide = refs[order:]
    j = pl.program_id(0)
    spread = spread_ref[...]
    wide[...] = dot(dev_ref[...], spread)

    def put_feat(rows, cols, value):
        value = value.astype(BF16)
        xh_ref[rows, cols] = value
        scaled[rows, cols] = (value.astype(F32) * wide[rows, cols]).astype(BF16)

    conv_rows(
        lambda lo, hi, cols: feat_ref[lo:hi, cols], feat_ref.shape[0], halo_ref[...], taps_ref[...].astype(F32), put_feat
    )
    state = dot(turned_ref[...], scaled[...])
    decay = dot(edev_ref[...], spread)[15:16]

    @pl.when(j < blocks)
    def _():
        write_sent(sent_ref, state, decay)

    @pl.when(j >= blocks)
    def _():
        write_kept(kept_ref, state, decay)


def front(chunk, where, features, halo, conv_feat, table, spread, turned, after):
    tokens = features.shape[0]
    start, width = chunk
    half = width // 2
    block = min(512, half)
    blocks = half // block
    base = start // block
    count = conv_feat.shape[0]
    heads2 = spread.shape[0]

    def place(j, where):
        sending = (j < blocks).astype(jnp.int32)
        which = sending * (1 - where[1]) + (1 - sending) * where[1]
        return which * blocks + j - (1 - sending) * blocks

    def cols(j, where):
        return (0, base + place(j, where))

    def same(j, where):
        return (0, 0)

    return pl.pallas_call(
        functools.partial(front_kernel, len(after), blocks),
        grid_spec=pltpu.PrefetchScalarGridSpec(
            num_scalar_prefetch=1,
            grid=(2 * blocks,),
            in_specs=[
                pl.BlockSpec((tokens, block), cols),
                pl.BlockSpec((HALO, block), cols),
                pl.BlockSpec((count, block), cols),
                pl.BlockSpec((tokens, heads2), lambda j, where: (0, DEV)),
                pl.BlockSpec((16, heads2), lambda j, where: (tokens // 16 - 1, EDEV)),
                pl.BlockSpec((heads2, block), cols),
                pl.BlockSpec((STATE, tokens), same),
                *behind(len(after)),
            ],
            out_specs=[
                pl.BlockSpec((tokens, block), lambda j, where: (0, place(j, where))),
                pl.BlockSpec((MSG, block), lambda j, where: (0, jnp.minimum(j, blocks - 1))),
                pl.BlockSpec((KEPT, block), lambda j, where: (0, jnp.maximum(j - blocks, 0))),
            ],
            scratch_shapes=[pltpu.VMEM((tokens, block), BF16), pltpu.VMEM((tokens, block), F32)],
        ),
        out_shape=[
            jax.ShapeDtypeStruct((tokens, width), BF16),
            jax.ShapeDtypeStruct((MSG, half), BF16),
            jax.ShapeDtypeStruct((KEPT, half), F32),
        ],
        compiler_params=params(),
        name="front",
        cost_estimate=cost(4),
    )(where, features, halo, conv_feat, table, table, spread, turned, *after)


def span_kernel(
    first_head, order, xh_ref, map_ref, col_ref, row_ref, table_ref, spread_ref, skips_ref, halves_ref,
    *refs,
):
    y_ref, state = refs[order:]
    width = xh_ref.shape[1]
    head_dim = width // row_ref.shape[0]
    heads2 = spread_ref.shape[0]

    @pl.when(pl.program_id(0) == 0)
    def _():
        state[...] = jnp.zeros_like(state)

    t = lax.broadcasted_iota(jnp.int32, (SPAN, SPAN), 0)
    s = lax.broadcasted_iota(jnp.int32, (SPAN, SPAN), 1)
    first = halves_ref[0:1, :]
    second = halves_ref[1:2, :]
    block = 256
    for k in range(xh_ref.shape[0] // SPAN):
        rows = slice(k * SPAN, (k + 1) * SPAN)
        in_map = map_ref[rows, :STATE]
        out_map = map_ref[rows, STATE:]
        scores = lax.dot_general(out_map, in_map, (((1,), (1,)), ((), ())), preferred_element_type=F32)
        scores = jnp.where(s <= t, scores, 0.0)
        in_turned = in_map.T
        tables = jnp.concatenate([table_ref[rows, :heads2], table_ref[rows, heads2:], skips_ref[...]], axis=0)
        for q in range(width // block):
            cols = slice(q * block, (q + 1) * block)
            feats = xh_ref[rows, cols]
            feats32 = feats.astype(F32)
            wide = dot(tables, spread_ref[:, cols])
            scaled = (feats32 * wide[:SPAN]).astype(BF16)
            ecum = wide[SPAN : 2 * SPAN]
            skip = wide[2 * SPAN : 2 * SPAN + 1]
            pairs = []
            for p in range(block // 128):
                weights = []
                for i in range(2):
                    h = (q * block + p * 128) // head_dim + i
                    gap = col_ref[rows, first_head + h : first_head + h + 1] - row_ref[h : h + 1, rows]
                    weights.append((scores * jnp.exp(jnp.minimum(gap, 0.0))).astype(BF16))
                pair = feats[:, p * 128 : (p + 1) * 128]
                stacked = jnp.concatenate([pair * first, pair * second], axis=0)
                pairs.append(dot(jnp.concatenate(weights, axis=1), stacked))
            diag = jnp.concatenate(pairs, axis=1)
            held = state[:, cols]
            carried = dot(out_map, held.astype(BF16)) * ecum
            y_ref[rows, cols] = (diag + carried + skip * feats32).astype(BF16)
            state[:, cols] = ecum[SPAN - 1 :] * held + dot(in_turned, scaled)


def spans_of(chunk, part, parts, micros, head_dim, xh, both_maps, col, row, table, spread, skips, halves, after):
    tokens = xh.shape[0]
    width = chunk[1] // parts
    index = chunk[0] // width + part
    some = width // head_dim
    heads2 = spread.shape[0]
    tile = 2 * SPAN
    return pl.pallas_call(
        functools.partial(span_kernel, index * some, len(after)),
        grid=(tokens // tile,),
        in_specs=[
            pl.BlockSpec((tile, width), lambda k: (k, part)),
            pl.BlockSpec((tile, 2 * STATE), lambda k: (k, 0)),
            pl.BlockSpec((tile, heads2), lambda k: (k, 0)),
            pl.BlockSpec((some, tile), lambda k: (index, k)),
            pl.BlockSpec((tile, 2 * heads2), lambda k: (k, 0)),
            pl.BlockSpec((heads2, width), lambda k: (0, index)),
            pl.BlockSpec(skips.shape, lambda k: (0, 0)),
            pl.BlockSpec(halves.shape, lambda k: (0, 0)),
            *behind(len(after)),
        ],
        out_specs=pl.BlockSpec((tile, width), lambda k: (k, 0)),
        out_shape=jax.ShapeDtypeStruct((tokens, width), BF16),
        scratch_shapes=[pltpu.VMEM((STATE, width), F32)],
        compiler_params=params(),
        name="spans",
        cost_estimate=cost(micros),
    )(xh, both_maps, col, row, table, spread, skips, halves, *after)


def pair_kernel(where_ref, kept_ref, got_ref, *refs):
    total_ref, sent_ref = refs[-2:]
    kept, kept_decay = read_state(kept_ref)
    got, got_decay = read_state(got_ref)

    def put(first, second, decay):
        total = decay * first + second
        write_kept(total_ref, total, kept_decay * got_decay)
        write_sent(sent_ref, total, kept_decay * got_decay)

    @pl.when(where_ref[1] == 0)
    def _():
        put(kept, got, got_decay)

    @pl.when(where_ref[1] == 1)
    def _():
        put(got, kept, kept_decay)


def inclusive_kernel(total_ref, before_ref, *refs):
    sent_ref = refs[-1]
    total, decay = read_state(total_ref)
    before, before_decay = read_state(before_ref)
    write_sent(sent_ref, total + decay * before, decay * before_decay)


def extend_kernel(before_ref, far_ref, *refs):
    before, decay = read_state(before_ref)
    far, far_decay = read_state(far_ref)
    write_kept(refs[-1], before + decay * far, decay * far_decay)


def last_kernel(where_ref, before_ref, far_ref, kept_ref, got_ref, *refs):
    mine_ref, sent_ref = refs[-2:]
    before, before_decay = read_state(before_ref)
    far, _ = read_state(far_ref)
    carried = before + before_decay * far

    @pl.when(where_ref[1] == 0)
    def _():
        kept, decay = read_state(kept_ref)
        mine_ref[...] = carried.astype(BF16)
        sent_ref[...] = (decay * carried + kept).astype(BF16)

    @pl.when(where_ref[1] == 1)
    def _():
        got, decay = read_state(got_ref)
        mine_ref[...] = (decay * carried + got).astype(BF16)
        sent_ref[...] = carried.astype(BF16)


def join(kernel, name, where, operands, outs, after):
    width = operands[0].shape[1]
    shapes = {
        "kept": jax.ShapeDtypeStruct((KEPT, width), F32),
        "sent": jax.ShapeDtypeStruct((MSG, width), BF16),
        "state": jax.ShapeDtypeStruct((STATE, width), BF16),
    }
    scalars = [] if where is None else [where]
    return pl.pallas_call(
        kernel,
        in_specs=[pl.BlockSpec(memory_space=pltpu.SMEM)] * len(scalars)
        + [pl.BlockSpec(memory_space=pltpu.VMEM)] * len(operands)
        + behind(len(after)),
        out_specs=[pl.BlockSpec(memory_space=pltpu.VMEM)] * len(outs),
        out_shape=[shapes[out] for out in outs],
        compiler_params=params(VMEM_SMALL),
        name=name,
        cost_estimate=cost(0.7),
    )(*scalars, *operands, *after)


def back_kernel(mode, counts, partners, order, where_ref, out_ref, edev_ref, *refs):
    chunks = []
    for pieces in counts:
        chunks.append((refs[:pieces], *refs[pieces : pieces + 5]))
        refs = refs[pieces + 5 :]
    if mode == "rest":
        squares_ref, *refs = refs
    refs = refs[order:]
    o_refs = refs[:partners]
    if mode == "first":
        squares_ref = refs[partners]
    gated, sums = refs[-2:]
    out_map = out_ref[...]
    edev = edev_ref[...]
    rows = out_map.shape[0]
    block = 256
    steps = pl.num_programs(0) // partners
    odd = where_ref[1] == 1
    sums[...] = squares_ref[...] if mode == "rest" else jnp.zeros((rows, 128), F32)
    at = 0
    for y_refs, mine_ref, other_ref, spread_ref, gate_ref, gain_ref in chunks:
        half = mine_ref.shape[1]
        for q in range(2 * half // block):
            cols = slice(q * block, (q + 1) * block)
            inner = slice(q * block % half, q * block % half + block)
            mine = mine_ref[:, inner]
            other = other_ref[:, inner]
            state = jnp.where(odd, other, mine) if q * block < half else jnp.where(odd, mine, other)
            gated[:, at : at + block] = dot(out_map, state) * dot(edev, spread_ref[:, cols])
            y_ref = y_refs[q * block // y_refs[0].shape[1]]
            y_at = q * block % y_refs[0].shape[1]
            for c in range(block // 128):
                y_cols = slice(y_at + c * 128, y_at + (c + 1) * 128)
                to = slice(at + c * 128, at + (c + 1) * 128)
                cols = slice(q * block + c * 128, q * block + (c + 1) * 128)
                gain = gain_ref[:, cols]
                for b in range(rows // 64):
                    part = slice(b * 64, (b + 1) * 64)
                    value = (y_ref[part, y_cols].astype(F32) + gated[part, to]) * silu(gate_ref[part, cols].astype(F32))
                    sums[part, :] = sums[part, :] + value * value
                    gated[part, to] = value * gain
            at += block
    if mode == "first":
        squares_ref[...] = sums[...]
    else:
        width = at if mode == "whole" else 2 * at
        mean = jnp.sum(sums[...], axis=1, keepdims=True) * (1.0 / width)
        scale = lax.rsqrt(mean + EPS)
    for p in range(partners):

        @pl.when(pl.program_id(0) // steps == p)
        def _(o_ref=o_refs[p]):
            if mode == "rest":
                step = pl.program_id(0) - p * steps
                start = pl.multiple_of(step * rows, rows)
                high = scale.astype(BF16).astype(F32)
                parts = [jnp.broadcast_to(part, (rows, 128)).T[:8] for part in (high, scale - high)]
                o_ref[steps * rows :, pl.ds(start, rows)] = jnp.concatenate(parts, axis=0).astype(BF16)
            for q in range(at // block):
                cols = slice(q * block, (q + 1) * block)
                value = gated[:, cols] if mode == "first" else gated[:, cols] * scale
                if mode == "rest":
                    o_ref[pl.ds(start, rows), cols] = value.astype(BF16)
                else:
                    o_ref[:, cols] = value.astype(BF16)


def back(mode, some, where, rows, chunks, both_maps, table, spread, gates, gain_row, squares, after, own=None):
    heads2 = spread.shape[0]
    tile = 128
    steps = rows // tile
    partners = len(some)

    def at(i, where):
        turn = some[0]
        for p in range(1, partners):
            turn = jnp.where(i >= p * steps, some[p], turn)
        return ((where[0] ^ turn) * steps + i % steps, 0)

    specs = [
        pl.BlockSpec((tile, STATE), lambda i, where: (at(i, where)[0], 1)),
        pl.BlockSpec((tile, heads2), lambda i, where: (at(i, where)[0], EDEV)),
    ]
    operands = [both_maps, table]
    total = 0
    for (start, width), ys, mine, other in chunks:
        index = start // width
        half = width // 2
        total += width
        specs += [pl.BlockSpec((tile, y.shape[1]), at) for y in ys]
        specs += [
            pl.BlockSpec((STATE, half), lambda i, where: (0, 0)),
            pl.BlockSpec((STATE, half), lambda i, where: (0, 0)),
            pl.BlockSpec((heads2, width), lambda i, where, index=index: (0, index)),
            pl.BlockSpec((tile, width), lambda i, where, index=index: (at(i, where)[0], index)),
            pl.BlockSpec((1, width), lambda i, where, index=index: (0, index)),
        ]
        operands += [*ys, mine, other, spread, gates, gain_row]
    if mode == "rest":
        specs.append(pl.BlockSpec((tile, 128), lambda i, where: (i, 0)))
        operands.append(squares)
    aliases = {}
    if own is not None and own[2] is not None:
        after = [own[2], *after]
        aliases = {1 + len(operands): partners - 1}
    specs += behind(len(after))
    operands += after
    sent = rows + 16 if mode == "rest" else rows
    part = sent if mode == "rest" else tile

    def part_of(p):
        if mode == "rest":
            return lambda i, where: (0, 0)
        return lambda i, where: (jnp.clip(i - p * steps, 0, steps - 1), 0)

    out_specs = [pl.BlockSpec((part, total), part_of(p)) for p in range(partners)]
    out_shape = [jax.ShapeDtypeStruct((sent, total), BF16)] * partners
    if own is not None:
        group, groups, _ = own
        out_specs[-1] = pl.BlockSpec(
            (tile, total),
            lambda i, where: (jnp.clip(i - (partners - 1) * steps, 0, steps - 1), (where[0] ^ some[-1]) * groups + group),
        )
        out_shape[-1] = jax.ShapeDtypeStruct((rows, groups * total * (gates.shape[0] // rows)), BF16)
    if mode == "first":
        out_specs.append(pl.BlockSpec((tile, 128), lambda i, where: (i, 0)))
        out_shape.append(jax.ShapeDtypeStruct((partners * rows, 128), F32))
    return pl.pallas_call(
        functools.partial(back_kernel, mode, [len(ys) for _, ys, _, _ in chunks], partners, len(after)),
        grid_spec=pltpu.PrefetchScalarGridSpec(
            num_scalar_prefetch=1,
            grid=(partners * steps,),
            in_specs=specs,
            out_specs=out_specs,
            scratch_shapes=[pltpu.VMEM((tile, total), F32), pltpu.VMEM((tile, 128), F32)],
        ),
        out_shape=out_shape,
        input_output_aliases=aliases,
        compiler_params=params(),
        name=f"back_{mode}",
        cost_estimate=cost(1),
    )(where, *operands)


def mark_kernel(order, *refs):
    refs[order][...] = jnp.zeros((8, 128), F32)


def mark(after):
    return pl.pallas_call(
        functools.partial(mark_kernel, len(after)),
        grid=(1,),
        in_specs=behind(len(after)),
        out_specs=pl.BlockSpec((8, 128), lambda i: (0, 0)),
        out_shape=jax.ShapeDtypeStruct((8, 128), F32),
        compiler_params=params(VMEM_SMALL),
        name="mark",
        cost_estimate=cost(200),
    )(*after)


def shifted(value, pairs, steps):
    return lax.ppermute(
        value,
        "ctx",
        [(2 * q + y, 2 * (q + steps) + y) for q in range(pairs - steps) for y in range(2)],
    )


def swapped(value, pairs):
    return lax.ppermute(value, "ctx", [(2 * q + y, 2 * q + 1 - y) for q in range(pairs) for y in range(2)])


class Line:
    def __init__(self):
        self.last = []

    def run(self, make, *args, **kwargs):
        made = make(*args, after=self.last, **kwargs)
        self.last = [made[0] if isinstance(made, (list, tuple)) else made]
        return made


class Exchange:
    def __init__(self, line, where, pairs, sent, kept):
        self.line = line
        self.where = where
        self.pairs = pairs
        self.kept = kept
        self.got = swapped(sent, pairs)

    def pair(self):
        self.total, sent = self.line.run(
            join, pair_kernel, "pair", self.where, [self.kept, self.got], ["kept", "sent"]
        )
        self.before = shifted(sent, self.pairs, 1)
        self.reach = 1

    def double(self):
        (sent,) = self.line.run(join, inclusive_kernel, "inclusive", None, [self.total, self.before], ["sent"])
        self.far = shifted(sent, self.pairs, self.reach + 1)
        self.reach = 2 * self.reach + 1

    def extend(self):
        while self.reach < self.pairs - 1:
            (self.before,) = self.line.run(join, extend_kernel, "extend", None, [self.before, self.far], ["kept"])
            self.double()

    def finish(self):
        self.extend()
        self.mine, sent = self.line.run(
            join, last_kernel, "last", self.where, [self.before, self.far, self.kept, self.got], ["state", "state"]
        )
        self.other = swapped(sent, self.pairs)


def shards(
    features, gates, state_io, step_size, log_decay, conv_feat, conv_state, skip_gain, norm_gain
):
    tokens, channels = features.shape
    heads = step_size.shape[0]
    head_dim = channels // heads
    groups = state_io.shape[2] // STATE
    group_width = channels // groups
    width = group_width // 2
    count = conv_feat.shape[0]
    rim = count - 1
    ctx_size = lax.axis_size("ctx")
    head_size = lax.axis_size("head")
    pairs = ctx_size // 2
    rows = tokens // head_size
    me = lax.axis_index("head").astype(jnp.int32)
    where = jnp.stack([me, lax.axis_index("ctx").astype(jnp.int32) % 2])

    onward = [(i, i + 1) for i in range(ctx_size - 1)]
    pad = HALO - rim
    halo = jnp.pad(lax.ppermute(features[tokens - rim :], "ctx", onward), ((pad, 0), (0, 0)))
    io_halo = jnp.pad(lax.ppermute(state_io[tokens - rim :], "ctx", onward), ((pad, 0), (0, 0), (0, 0)))
    spread = jnp.asarray(spread_table(heads, head_dim), BF16)
    halves = jnp.asarray(np.arange(128)[None, :] // head_dim == np.arange(2)[:, None], BF16)
    col, row, table, skips = decay_tables(log_decay, step_size, skip_gain)
    gain_row = norm_gain[None]

    line = Line()
    chunks = [(0, width), (width, width)] + [(g * group_width, group_width) for g in range(1, groups)]
    of_group = [[0, 1]] + [[g + 1] for g in range(1, groups)]
    group_of = [0, 0] + list(range(1, groups))
    fronts = {}
    maps = {}
    exchanges = {}
    ys = {}

    def run_maps(g):
        maps[g] = line.run(maps_of, g, state_io, io_halo, conv_state)

    def run_front(c):
        made = line.run(
            front, chunks[c], where, features, halo, conv_feat, table, spread, maps[group_of[c]][1]
        )
        fronts[c] = made[0]
        exchanges[c] = Exchange(line, where, pairs, made[1], made[2])

    def run_spans(c, part=0, parts=1, micros=200):
        g = group_of[c]
        made = line.run(
            spans_of, chunks[c], part, parts, micros, head_dim, fronts[c], maps[g][0], col, row, table, spread,
            skips, halves,
        )
        ys.setdefault(c, []).append(made)

    def part(c):
        return (chunks[c], ys[c], exchanges[c].mine, exchanges[c].other)

    partners = list(range(head_size - 1, 1, -1))
    squares = {}
    pieces = {}

    def ship(piece, r):
        return lax.ppermute(piece, "head", [(i, i ^ r) for i in range(head_size)])

    def run_back(mode, some, g, parts, squares, own=None):
        return line.run(
            back, mode, some, where, rows, [part(c) for c in parts], maps[g][0], table, spread, gates, gain_row,
            squares, own=own,
        )

    def arrived(g, index, some):
        line.last += [pieces[g, r][index] for r in some]

    def run_first(g, apart=False):
        squares[g] = []
        for some in [[r] for r in partners] if apart else [partners]:
            *made, square = run_back("first", some, g, [0], None)
            squares[g].append((some, square))
            for r, piece in zip(some, made):
                pieces[g, r] = [ship(piece, r)]

    def run_rest(g, turns):
        for some, square in squares[g][turns]:
            made = run_back("rest", some, g, [1], square)
            for r, piece in zip(some, made):
                pieces[g, r].append(ship(piece, r))

    result = None

    def run_one(g, r):
        (piece,) = run_back("whole", [r], g, of_group[g], None)
        pieces[g, r] = [ship(piece, r)]

    def run_own(g):
        nonlocal result
        before = line.last
        (result,) = run_back("whole", [0], g, of_group[g], None, own=(g, groups, result))
        line.last = before

    def run_put(g, r):
        nonlocal result
        start = (me ^ r) * channels + g * group_width
        zero = jnp.int32(0)
        if len(pieces[g, r]) == 2:
            first, rest = pieces[g, r]
            scale = rest[rows, :rows].astype(F32) + rest[rows + 8, :rows].astype(F32)
            first = (first.astype(F32) * scale[:, None]).astype(BF16)
            result = lax.dynamic_update_slice(result, first, (zero, start))
            result = lax.dynamic_update_slice(result, rest[:rows], (zero, start + width))
        else:
            result = lax.dynamic_update_slice(result, pieces[g, r][0], (zero, start))

    ex = exchanges
    later = range(1, groups)
    run_maps(0)
    run_front(0)
    run_front(1)
    ex[0].pair()
    for g in later:
        run_maps(g)
    ex[0].double()
    ex[1].pair()
    for g in later:
        run_front(g + 1)
    run_spans(0)
    ex[0].finish()
    ex[1].double()
    for g in later:
        ex[g + 1].pair()
    run_first(0, apart=True)
    if groups > 1:
        line.run(mark)
    run_spans(1, micros=1)
    ex[1].finish()
    for g in later:
        ex[g + 1].double()
    for g in later:
        run_spans(g + 1, micros=1)
    arrived(0, 0, partners)
    run_rest(0, slice(0, 1))
    for g in later:
        ex[g + 1].finish()
    run_rest(0, slice(1, None))
    run_one(0, 1)
    for g in later:
        arrived(0, 1, partners[:1])
        run_one(g, partners[0])
        run_one(g, 1)
        arrived(0, 1, partners[1:])
        for r in partners[1:]:
            run_one(g, r)
    run_own(0)
    for r in [*partners, 1]:
        run_put(0, r)
    for g in later:
        run_own(g)
        for r in [partners[0], 1, *partners[1:]]:
            run_put(g, r)
    return result


def solution(mesh):
    in_specs = (
        P("ctx", "head"),
        P("ctx", "head"),
        P("ctx", None, "head"),
        P("head", "ctx"),
        P("head", "ctx"),
        P(None, "head"),
        P(None, None, "head"),
        P("head"),
        P("head"),
    )
    out_specs = P(("ctx", "head"), None)
    return jax.shard_map(shards, mesh=mesh, in_specs=in_specs, out_specs=out_specs, check_vma=False)
```

```python
import functools

import jax
import jax.numpy as jnp
import numpy as np
from jax import lax
from jax.experimental import pallas as pl
from jax.experimental.pallas import tpu as pltpu
from jax.sharding import PartitionSpec as P

STATE = 256
SPAN = 128
HALO = 16
EPS = 1e-05
LOC, ECUM, DEV, EDEV = range(4)
F32 = jnp.float32
BF16 = jnp.bfloat16
VMEM_BYTES = 44 * 1024 * 1024
VMEM_SMALL = 8 * 1024 * 1024
COST_SCALE = 10**9
MSG = STATE + 16
KEPT = STATE + 8


def dot(a, b):
    return jnp.dot(a, b, preferred_element_type=F32)


def silu(v):
    half = 0.5 * v
    return half * jnp.tanh(half) + half


def cost(micros):
    return pl.CostEstimate(flops=int(micros * COST_SCALE), bytes_accessed=1, transcendentals=0)


def params(limit=VMEM_BYTES):
    return pltpu.CompilerParams(vmem_limit_bytes=limit)


def lanes_of(heads):
    return -(-2 * heads // 128) * 128


def spread_table(heads, head_dim):
    row = np.arange(lanes_of(heads))
    head = np.where(row < 2 * heads, row % heads, heads)
    return (head[:, None] == (np.arange(heads * head_dim) // head_dim)[None, :]).astype(np.float32)


def decay_kernel(log_ref, step_ref, skip_ref, col_ref, row_ref, table_ref, skips_ref):
    heads, tokens = log_ref.shape
    lanes = lanes_of(heads)
    spans = tokens // SPAN
    r = lax.broadcasted_iota(jnp.int32, (SPAN, SPAN), 0)
    c = lax.broadcasted_iota(jnp.int32, (SPAN, SPAN), 1)
    upper = (r <= c).astype(F32)
    cums = []
    for k in range(spans):
        cums.append(
            jnp.dot(
                log_ref[:, k * SPAN : (k + 1) * SPAN],
                upper,
                precision=lax.Precision.HIGHEST,
                preferred_element_type=F32,
            )
        )
    totals = [cum[:, SPAN - 1 :] for cum in cums]
    before = [jnp.zeros_like(totals[0])]
    for k in range(spans - 1):
        before.append(before[-1] + totals[k])
    after = [jnp.zeros_like(totals[0])]
    for k in range(spans - 1, 0, -1):
        after.insert(0, after[0] + totals[k])

    def put(index, k, value):
        high = value.astype(BF16).astype(F32)
        rest = [jnp.zeros((lanes - 2 * heads, SPAN), F32)] if lanes > 2 * heads else []
        both = jnp.concatenate([high, value - high, *rest], axis=0)
        table_ref[k * SPAN : (k + 1) * SPAN, index * lanes : (index + 1) * lanes] = both.T.astype(BF16)

    skip = skip_ref[...]
    high = skip.astype(BF16).astype(F32)
    none = [jnp.zeros((1, lanes - 2 * heads), F32)] if lanes > 2 * heads else []
    parts = jnp.concatenate([high, skip - high, *none], axis=1)
    skips_ref[...] = jnp.broadcast_to(parts, skips_ref.shape).astype(BF16)
    for k in range(spans):
        cum = cums[k]
        step = step_ref[:, k * SPAN : (k + 1) * SPAN]
        col_ref[k * SPAN : (k + 1) * SPAN, :] = jnp.concatenate([cum] * (lanes // heads), axis=0).T
        row_ref[:, k * SPAN : (k + 1) * SPAN] = cum - jnp.log(step)
        to_end = totals[k] - cum
        put(LOC, k, jnp.exp(to_end) * step)
        put(DEV, k, jnp.exp(to_end + after[k]) * step)
        put(ECUM, k, jnp.exp(cum))
        put(EDEV, k, jnp.exp(cum + before[k]))


def behind(count):
    return [pl.BlockSpec(memory_space=pl.ANY)] * count


def decay_tables(log_decay, step_size, skip_gain):
    heads, tokens = log_decay.shape
    lanes = lanes_of(heads)
    return pl.pallas_call(
        decay_kernel,
        out_shape=(
            jax.ShapeDtypeStruct((tokens, lanes), F32),
            jax.ShapeDtypeStruct((heads, tokens), F32),
            jax.ShapeDtypeStruct((tokens, 4 * lanes), BF16),
            jax.ShapeDtypeStruct((16, lanes), BF16),
        ),
        compiler_params=params(),
        name="decays",
        cost_estimate=cost(1.5),
    )(log_decay, step_size, skip_gain[None])


def conv_rows(read, rows, halo, taps, store):
    count, width = taps.shape
    tile = SPAN
    for b in range(rows // tile):
        for c in range(1):
            cols = slice(0, width)
            own = read(b * tile, (b + 1) * tile, cols).astype(F32)
            prev = (halo[:, cols] if b == 0 else read(b * tile - HALO, b * tile, cols)).astype(F32)
            both = jnp.concatenate([prev[HALO - 8 :], own], axis=0)
            total = own * taps[count - 1 : count, cols]
            for k in range(1, count):
                total = total + both[8 - k : 8 - k + tile] * taps[count - 1 - k : count - k, cols]
            store(slice(b * tile, (b + 1) * tile), cols, silu(total))


def read_state(ref):
    if ref.dtype == F32:
        return ref[:STATE, :], ref[STATE : STATE + 1, :]
    tail = ref[STATE:MSG, :].astype(F32)
    return ref[:STATE, :].astype(F32), tail[0:1] + tail[8:9]


def write_kept(ref, value, decay):
    ref[:STATE, :] = value
    ref[STATE:KEPT, :] = jnp.broadcast_to(decay, (KEPT - STATE, decay.shape[1]))


def write_sent(ref, value, decay):
    ref[:STATE, :] = value.astype(BF16)
    high = decay.astype(BF16).astype(F32)
    shape = (8, decay.shape[1])
    rows = jnp.concatenate([jnp.broadcast_to(high, shape), jnp.broadcast_to(decay - high, shape)], axis=0)
    ref[STATE:MSG, :] = rows.astype(BF16)


def maps_kernel(order, io_ref, halo_ref, taps_ref, *refs):
    map_ref, turned_ref = refs[order:]

    def put_in(rows, cols, value):
        map_ref[rows, :STATE] = value.astype(BF16)

    def put_out(rows, cols, value):
        map_ref[rows, STATE:] = value.astype(BF16)

    tokens = io_ref.shape[0]
    for i, put in ((0, put_in), (1, put_out)):
        conv_rows(
            lambda lo, hi, cols: io_ref[lo:hi, i, cols], tokens, halo_ref[:, i, :], taps_ref[:, i, :].astype(F32), put
        )
    for b in range(tokens // SPAN):
        rows = slice(b * SPAN, (b + 1) * SPAN)
        turned_ref[:, rows] = map_ref[rows, :STATE].T


def maps_of(group, state_io, halo, conv_state, after):
    tokens = state_io.shape[0]
    count = conv_state.shape[0]

    def mine(j):
        return (0, 0, group)

    return pl.pallas_call(
        functools.partial(maps_kernel, len(after)),
        grid=(1,),
        in_specs=[
            pl.BlockSpec((tokens, 2, STATE), mine),
            pl.BlockSpec((HALO, 2, STATE), mine),
            pl.BlockSpec((count, 2, STATE), mine),
            *behind(len(after)),
        ],
        out_specs=[
            pl.BlockSpec((tokens, 2 * STATE), lambda j: (0, 0)),
            pl.BlockSpec((STATE, tokens), lambda j: (0, 0)),
        ],
        out_shape=[
            jax.ShapeDtypeStruct((tokens, 2 * STATE), BF16),
            jax.ShapeDtypeStruct((STATE, tokens), BF16),
        ],
        compiler_params=params(),
        name="maps",
        cost_estimate=cost(3),
    )(state_io, halo, conv_state, *after)


def front_kernel(order, blocks, where_ref, feat_ref, halo_ref, taps_ref, dev_ref, edev_ref, spread_ref, turned_ref, *refs):
    xh_ref, sent_ref, kept_ref, scaled, wide = refs[order:]
    j = pl.program_id(0)
    spread = spread_ref[...]
    wide[...] = dot(dev_ref[...], spread)

    def put_feat(rows, cols, value):
        value = value.astype(BF16)
        xh_ref[rows, cols] = value
        scaled[rows, cols] = (value.astype(F32) * wide[rows, cols]).astype(BF16)

    conv_rows(
        lambda lo, hi, cols: feat_ref[lo:hi, cols], feat_ref.shape[0], halo_ref[...], taps_ref[...].astype(F32), put_feat
    )
    state = dot(turned_ref[...], scaled[...])
    decay = dot(edev_ref[...], spread)[15:16]

    @pl.when(j < blocks)
    def _():
        write_sent(sent_ref, state, decay)

    @pl.when(j >= blocks)
    def _():
        write_kept(kept_ref, state, decay)


def front(chunk, where, features, halo, conv_feat, table, spread, turned, after):
    tokens = features.shape[0]
    start, width = chunk
    half = width // 2
    block = min(512, half)
    blocks = half // block
    base = start // block
    count = conv_feat.shape[0]
    heads2 = spread.shape[0]

    def place(j, where):
        sending = (j < blocks).astype(jnp.int32)
        which = sending * (1 - where[1]) + (1 - sending) * where[1]
        return which * blocks + j - (1 - sending) * blocks

    def cols(j, where):
        return (0, base + place(j, where))

    def same(j, where):
        return (0, 0)

    return pl.pallas_call(
        functools.partial(front_kernel, len(after), blocks),
        grid_spec=pltpu.PrefetchScalarGridSpec(
            num_scalar_prefetch=1,
            grid=(2 * blocks,),
            in_specs=[
                pl.BlockSpec((tokens, block), cols),
                pl.BlockSpec((HALO, block), cols),
                pl.BlockSpec((count, block), cols),
                pl.BlockSpec((tokens, heads2), lambda j, where: (0, DEV)),
                pl.BlockSpec((16, heads2), lambda j, where: (tokens // 16 - 1, EDEV)),
                pl.BlockSpec((heads2, block), cols),
                pl.BlockSpec((STATE, tokens), same),
                *behind(len(after)),
            ],
            out_specs=[
                pl.BlockSpec((tokens, block), lambda j, where: (0, place(j, where))),
                pl.BlockSpec((MSG, block), lambda j, where: (0, jnp.minimum(j, blocks - 1))),
                pl.BlockSpec((KEPT, block), lambda j, where: (0, jnp.maximum(j - blocks, 0))),
            ],
            scratch_shapes=[pltpu.VMEM((tokens, block), BF16), pltpu.VMEM((tokens, block), F32)],
        ),
        out_shape=[
            jax.ShapeDtypeStruct((tokens, width), BF16),
            jax.ShapeDtypeStruct((MSG, half), BF16),
            jax.ShapeDtypeStruct((KEPT, half), F32),
        ],
        compiler_params=params(),
        name="front",
        cost_estimate=cost(4),
    )(where, features, halo, conv_feat, table, table, spread, turned, *after)


def span_kernel(
    first_head, order, xh_ref, map_ref, col_ref, row_ref, table_ref, spread_ref, skips_ref, halves_ref,
    *refs,
):
    y_ref, state = refs[order:]
    width = xh_ref.shape[1]
    head_dim = width // row_ref.shape[0]
    heads2 = spread_ref.shape[0]

    @pl.when(pl.program_id(0) == 0)
    def _():
        state[...] = jnp.zeros_like(state)

    t = lax.broadcasted_iota(jnp.int32, (SPAN, SPAN), 0)
    s = lax.broadcasted_iota(jnp.int32, (SPAN, SPAN), 1)
    first = halves_ref[0:1, :]
    second = halves_ref[1:2, :]
    block = 256
    for k in range(xh_ref.shape[0] // SPAN):
        rows = slice(k * SPAN, (k + 1) * SPAN)
        in_map = map_ref[rows, :STATE]
        out_map = map_ref[rows, STATE:]
        scores = lax.dot_general(out_map, in_map, (((1,), (1,)), ((), ())), preferred_element_type=F32)
        scores = jnp.where(s <= t, scores, 0.0)
        in_turned = in_map.T
        tables = jnp.concatenate([table_ref[rows, :heads2], table_ref[rows, heads2:], skips_ref[...]], axis=0)
        for q in range(width // block):
            cols = slice(q * block, (q + 1) * block)
            feats = xh_ref[rows, cols]
            feats32 = feats.astype(F32)
            wide = dot(tables, spread_ref[:, cols])
            scaled = (feats32 * wide[:SPAN]).astype(BF16)
            ecum = wide[SPAN : 2 * SPAN]
            skip = wide[2 * SPAN : 2 * SPAN + 1]
            pairs = []
            for p in range(block // 128):
                weights = []
                for i in range(2):
                    h = (q * block + p * 128) // head_dim + i
                    gap = col_ref[rows, first_head + h : first_head + h + 1] - row_ref[h : h + 1, rows]
                    weights.append((scores * jnp.exp(jnp.minimum(gap, 0.0))).astype(BF16))
                pair = feats[:, p * 128 : (p + 1) * 128]
                stacked = jnp.concatenate([pair * first, pair * second], axis=0)
                pairs.append(dot(jnp.concatenate(weights, axis=1), stacked))
            diag = jnp.concatenate(pairs, axis=1)
            held = state[:, cols]
            carried = dot(out_map, held.astype(BF16)) * ecum
            y_ref[rows, cols] = (diag + carried + skip * feats32).astype(BF16)
            state[:, cols] = ecum[SPAN - 1 :] * held + dot(in_turned, scaled)


def spans_of(chunk, part, parts, micros, head_dim, xh, both_maps, col, row, table, spread, skips, halves, after):
    tokens = xh.shape[0]
    width = chunk[1] // parts
    index = chunk[0] // width + part
    some = width // head_dim
    heads2 = spread.shape[0]
    tile = 2 * SPAN
    return pl.pallas_call(
        functools.partial(span_kernel, index * some, len(after)),
        grid=(tokens // tile,),
        in_specs=[
            pl.BlockSpec((tile, width), lambda k: (k, part)),
            pl.BlockSpec((tile, 2 * STATE), lambda k: (k, 0)),
            pl.BlockSpec((tile, heads2), lambda k: (k, 0)),
            pl.BlockSpec((some, tile), lambda k: (index, k)),
            pl.BlockSpec((tile, 2 * heads2), lambda k: (k, 0)),
            pl.BlockSpec((heads2, width), lambda k: (0, index)),
            pl.BlockSpec(skips.shape, lambda k: (0, 0)),
            pl.BlockSpec(halves.shape, lambda k: (0, 0)),
            *behind(len(after)),
        ],
        out_specs=pl.BlockSpec((tile, width), lambda k: (k, 0)),
        out_shape=jax.ShapeDtypeStruct((tokens, width), BF16),
        scratch_shapes=[pltpu.VMEM((STATE, width), F32)],
        compiler_params=params(),
        name="spans",
        cost_estimate=cost(micros),
    )(xh, both_maps, col, row, table, spread, skips, halves, *after)


def pair_kernel(where_ref, kept_ref, got_ref, *refs):
    total_ref, sent_ref = refs[-2:]
    kept, kept_decay = read_state(kept_ref)
    got, got_decay = read_state(got_ref)

    def put(first, second, decay):
        total = decay * first + second
        write_kept(total_ref, total, kept_decay * got_decay)
        write_sent(sent_ref, total, kept_decay * got_decay)

    @pl.when(where_ref[1] == 0)
    def _():
        put(kept, got, got_decay)

    @pl.when(where_ref[1] == 1)
    def _():
        put(got, kept, kept_decay)


def inclusive_kernel(total_ref, before_ref, *refs):
    sent_ref = refs[-1]
    total, decay = read_state(total_ref)
    before, before_decay = read_state(before_ref)
    write_sent(sent_ref, total + decay * before, decay * before_decay)


def extend_kernel(before_ref, far_ref, *refs):
    before, decay = read_state(before_ref)
    far, far_decay = read_state(far_ref)
    write_kept(refs[-1], before + decay * far, decay * far_decay)


def last_kernel(where_ref, before_ref, far_ref, kept_ref, got_ref, *refs):
    mine_ref, sent_ref = refs[-2:]
    before, before_decay = read_state(before_ref)
    far, _ = read_state(far_ref)
    carried = before + before_decay * far

    @pl.when(where_ref[1] == 0)
    def _():
        kept, decay = read_state(kept_ref)
        mine_ref[...] = carried.astype(BF16)
        sent_ref[...] = (decay * carried + kept).astype(BF16)

    @pl.when(where_ref[1] == 1)
    def _():
        got, decay = read_state(got_ref)
        mine_ref[...] = (decay * carried + got).astype(BF16)
        sent_ref[...] = carried.astype(BF16)


def join(kernel, name, where, operands, outs, after):
    width = operands[0].shape[1]
    shapes = {
        "kept": jax.ShapeDtypeStruct((KEPT, width), F32),
        "sent": jax.ShapeDtypeStruct((MSG, width), BF16),
        "state": jax.ShapeDtypeStruct((STATE, width), BF16),
    }
    scalars = [] if where is None else [where]
    return pl.pallas_call(
        kernel,
        in_specs=[pl.BlockSpec(memory_space=pltpu.SMEM)] * len(scalars)
        + [pl.BlockSpec(memory_space=pltpu.VMEM)] * len(operands)
        + behind(len(after)),
        out_specs=[pl.BlockSpec(memory_space=pltpu.VMEM)] * len(outs),
        out_shape=[shapes[out] for out in outs],
        compiler_params=params(VMEM_SMALL),
        name=name,
        cost_estimate=cost(0.7),
    )(*scalars, *operands, *after)


def back_kernel(mode, counts, partners, order, where_ref, out_ref, edev_ref, *refs):
    chunks = []
    for pieces in counts:
        chunks.append((refs[:pieces], *refs[pieces : pieces + 5]))
        refs = refs[pieces + 5 :]
    if mode == "rest":
        squares_ref, *refs = refs
    refs = refs[order:]
    o_refs = refs[:partners]
    if mode == "first":
        squares_ref = refs[partners]
    gated, sums = refs[-2:]
    out_map = out_ref[...]
    edev = edev_ref[...]
    rows = out_map.shape[0]
    block = 256
    steps = pl.num_programs(0) // partners
    odd = where_ref[1] == 1
    sums[...] = squares_ref[...] if mode == "rest" else jnp.zeros((rows, 128), F32)
    at = 0
    for y_refs, mine_ref, other_ref, spread_ref, gate_ref, gain_ref in chunks:
        half = mine_ref.shape[1]
        for q in range(2 * half // block):
            cols = slice(q * block, (q + 1) * block)
            inner = slice(q * block % half, q * block % half + block)
            mine = mine_ref[:, inner]
            other = other_ref[:, inner]
            state = jnp.where(odd, other, mine) if q * block < half else jnp.where(odd, mine, other)
            gated[:, at : at + block] = dot(out_map, state) * dot(edev, spread_ref[:, cols])
            y_ref = y_refs[q * block // y_refs[0].shape[1]]
            y_at = q * block % y_refs[0].shape[1]
            for c in range(block // 128):
                y_cols = slice(y_at + c * 128, y_at + (c + 1) * 128)
                to = slice(at + c * 128, at + (c + 1) * 128)
                cols = slice(q * block + c * 128, q * block + (c + 1) * 128)
                gain = gain_ref[:, cols]
                for b in range(rows // 64):
                    part = slice(b * 64, (b + 1) * 64)
                    value = (y_ref[part, y_cols].astype(F32) + gated[part, to]) * silu(gate_ref[part, cols].astype(F32))
                    sums[part, :] = sums[part, :] + value * value
                    gated[part, to] = value * gain
            at += block
    if mode == "first":
        squares_ref[...] = sums[...]
    else:
        width = at if mode == "whole" else 2 * at
        mean = jnp.sum(sums[...], axis=1, keepdims=True) * (1.0 / width)
        scale = lax.rsqrt(mean + EPS)
    for p in range(partners):

        @pl.when(pl.program_id(0) // steps == p)
        def _(o_ref=o_refs[p]):
            if mode == "rest":
                step = pl.program_id(0) - p * steps
                start = pl.multiple_of(step * rows, rows)
                high = scale.astype(BF16).astype(F32)
                parts = [jnp.broadcast_to(part, (rows, 128)).T[:8] for part in (high, scale - high)]
                o_ref[steps * rows :, pl.ds(start, rows)] = jnp.concatenate(parts, axis=0).astype(BF16)
            for q in range(at // block):
                cols = slice(q * block, (q + 1) * block)
                value = gated[:, cols] if mode == "first" else gated[:, cols] * scale
                if mode == "rest":
                    o_ref[pl.ds(start, rows), cols] = value.astype(BF16)
                else:
                    o_ref[:, cols] = value.astype(BF16)


def back(mode, some, where, rows, chunks, both_maps, table, spread, gates, gain_row, squares, after, own=None):
    heads2 = spread.shape[0]
    tile = 128
    steps = rows // tile
    partners = len(some)

    def at(i, where):
        turn = some[0]
        for p in range(1, partners):
            turn = jnp.where(i >= p * steps, some[p], turn)
        return ((where[0] ^ turn) * steps + i % steps, 0)

    specs = [
        pl.BlockSpec((tile, STATE), lambda i, where: (at(i, where)[0], 1)),
        pl.BlockSpec((tile, heads2), lambda i, where: (at(i, where)[0], EDEV)),
    ]
    operands = [both_maps, table]
    total = 0
    for (start, width), ys, mine, other in chunks:
        index = start // width
        half = width // 2
        total += width
        specs += [pl.BlockSpec((tile, y.shape[1]), at) for y in ys]
        specs += [
            pl.BlockSpec((STATE, half), lambda i, where: (0, 0)),
            pl.BlockSpec((STATE, half), lambda i, where: (0, 0)),
            pl.BlockSpec((heads2, width), lambda i, where, index=index: (0, index)),
            pl.BlockSpec((tile, width), lambda i, where, index=index: (at(i, where)[0], index)),
            pl.BlockSpec((1, width), lambda i, where, index=index: (0, index)),
        ]
        operands += [*ys, mine, other, spread, gates, gain_row]
    if mode == "rest":
        specs.append(pl.BlockSpec((tile, 128), lambda i, where: (i, 0)))
        operands.append(squares)
    aliases = {}
    if own is not None and own[2] is not None:
        after = [own[2], *after]
        aliases = {1 + len(operands): partners - 1}
    specs += behind(len(after))
    operands += after
    sent = rows + 16 if mode == "rest" else rows
    part = sent if mode == "rest" else tile

    def part_of(p):
        if mode == "rest":
            return lambda i, where: (0, 0)
        return lambda i, where: (jnp.clip(i - p * steps, 0, steps - 1), 0)

    out_specs = [pl.BlockSpec((part, total), part_of(p)) for p in range(partners)]
    out_shape = [jax.ShapeDtypeStruct((sent, total), BF16)] * partners
    if own is not None:
        group, groups, _ = own
        out_specs[-1] = pl.BlockSpec(
            (tile, total),
            lambda i, where: (jnp.clip(i - (partners - 1) * steps, 0, steps - 1), (where[0] ^ some[-1]) * groups + group),
        )
        out_shape[-1] = jax.ShapeDtypeStruct((rows, groups * total * (gates.shape[0] // rows)), BF16)
    if mode == "first":
        out_specs.append(pl.BlockSpec((tile, 128), lambda i, where: (i, 0)))
        out_shape.append(jax.ShapeDtypeStruct((partners * rows, 128), F32))
    return pl.pallas_call(
        functools.partial(back_kernel, mode, [len(ys) for _, ys, _, _ in chunks], partners, len(after)),
        grid_spec=pltpu.PrefetchScalarGridSpec(
            num_scalar_prefetch=1,
            grid=(partners * steps,),
            in_specs=specs,
            out_specs=out_specs,
            scratch_shapes=[pltpu.VMEM((tile, total), F32), pltpu.VMEM((tile, 128), F32)],
        ),
        out_shape=out_shape,
        input_output_aliases=aliases,
        compiler_params=params(),
        name=f"back_{mode}",
        cost_estimate=cost(1),
    )(where, *operands)


def mark_kernel(order, *refs):
    refs[order][...] = jnp.zeros((8, 128), F32)


def mark(after):
    return pl.pallas_call(
        functools.partial(mark_kernel, len(after)),
        grid=(1,),
        in_specs=behind(len(after)),
        out_specs=pl.BlockSpec((8, 128), lambda i: (0, 0)),
        out_shape=jax.ShapeDtypeStruct((8, 128), F32),
        compiler_params=params(VMEM_SMALL),
        name="mark",
        cost_estimate=cost(200),
    )(*after)


def shifted(value, pairs, steps):
    return lax.ppermute(
        value,
        "ctx",
        [(2 * q + y, 2 * (q + steps) + y) for q in range(pairs - steps) for y in range(2)],
    )


def swapped(value, pairs):
    return lax.ppermute(value, "ctx", [(2 * q + y, 2 * q + 1 - y) for q in range(pairs) for y in range(2)])


class Line:
    def __init__(self):
        self.last = []

    def run(self, make, *args, **kwargs):
        made = make(*args, after=self.last, **kwargs)
        self.last = [made[0] if isinstance(made, (list, tuple)) else made]
        return made


class Exchange:
    def __init__(self, line, where, pairs, sent, kept):
        self.line = line
        self.where = where
        self.pairs = pairs
        self.kept = kept
        self.got = swapped(sent, pairs)

    def pair(self):
        self.total, sent = self.line.run(
            join, pair_kernel, "pair", self.where, [self.kept, self.got], ["kept", "sent"]
        )
        self.before = shifted(sent, self.pairs, 1)
        self.reach = 1

    def double(self):
        (sent,) = self.line.run(join, inclusive_kernel, "inclusive", None, [self.total, self.before], ["sent"])
        self.far = shifted(sent, self.pairs, self.reach + 1)
        self.reach = 2 * self.reach + 1

    def extend(self):
        while self.reach < self.pairs - 1:
            (self.before,) = self.line.run(join, extend_kernel, "extend", None, [self.before, self.far], ["kept"])
            self.double()

    def finish(self):
        self.extend()
        self.mine, sent = self.line.run(
            join, last_kernel, "last", self.where, [self.before, self.far, self.kept, self.got], ["state", "state"]
        )
        self.other = swapped(sent, self.pairs)


def shards(
    features, gates, state_io, step_size, log_decay, conv_feat, conv_state, skip_gain, norm_gain
):
    tokens, channels = features.shape
    heads = step_size.shape[0]
    head_dim = channels // heads
    groups = state_io.shape[2] // STATE
    group_width = channels // groups
    width = group_width // 2
    count = conv_feat.shape[0]
    rim = count - 1
    ctx_size = lax.axis_size("ctx")
    head_size = lax.axis_size("head")
    pairs = ctx_size // 2
    rows = tokens // head_size
    me = lax.axis_index("head").astype(jnp.int32)
    where = jnp.stack([me, lax.axis_index("ctx").astype(jnp.int32) % 2])

    onward = [(i, i + 1) for i in range(ctx_size - 1)]
    pad = HALO - rim
    halo = jnp.pad(lax.ppermute(features[tokens - rim :], "ctx", onward), ((pad, 0), (0, 0)))
    io_halo = jnp.pad(lax.ppermute(state_io[tokens - rim :], "ctx", onward), ((pad, 0), (0, 0), (0, 0)))
    spread = jnp.asarray(spread_table(heads, head_dim), BF16)
    halves = jnp.asarray(np.arange(128)[None, :] // head_dim == np.arange(2)[:, None], BF16)
    col, row, table, skips = decay_tables(log_decay, step_size, skip_gain)
    gain_row = norm_gain[None]

    line = Line()
    chunks = [(0, width), (width, width)] + [(g * group_width, group_width) for g in range(1, groups)]
    of_group = [[0, 1]] + [[g + 1] for g in range(1, groups)]
    group_of = [0, 0] + list(range(1, groups))
    fronts = {}
    maps = {}
    exchanges = {}
    ys = {}

    def run_maps(g):
        maps[g] = line.run(maps_of, g, state_io, io_halo, conv_state)

    def run_front(c):
        made = line.run(
            front, chunks[c], where, features, halo, conv_feat, table, spread, maps[group_of[c]][1]
        )
        fronts[c] = made[0]
        exchanges[c] = Exchange(line, where, pairs, made[1], made[2])

    def run_spans(c, part=0, parts=1, micros=200):
        g = group_of[c]
        made = line.run(
            spans_of, chunks[c], part, parts, micros, head_dim, fronts[c], maps[g][0], col, row, table, spread,
            skips, halves,
        )
        ys.setdefault(c, []).append(made)

    def part(c):
        return (chunks[c], ys[c], exchanges[c].mine, exchanges[c].other)

    partners = list(range(head_size - 1, 1, -1))
    squares = {}
    pieces = {}

    def ship(piece, r):
        return lax.ppermute(piece, "head", [(i, i ^ r) for i in range(head_size)])

    def run_back(mode, some, g, parts, squares, own=None):
        return line.run(
            back, mode, some, where, rows, [part(c) for c in parts], maps[g][0], table, spread, gates, gain_row,
            squares, own=own,
        )

    def arrived(g, index, some):
        line.last += [pieces[g, r][index] for r in some]

    def run_first(g, apart=False):
        squares[g] = []
        for some in [[r] for r in partners] if apart else [partners]:
            *made, square = run_back("first", some, g, [0], None)
            squares[g].append((some, square))
            for r, piece in zip(some, made):
                pieces[g, r] = [ship(piece, r)]

    def run_rest(g, turns):
        for some, square in squares[g][turns]:
            made = run_back("rest", some, g, [1], square)
            for r, piece in zip(some, made):
                pieces[g, r].append(ship(piece, r))

    result = None

    def run_one(g, r):
        (piece,) = run_back("whole", [r], g, of_group[g], None)
        pieces[g, r] = [ship(piece, r)]

    def run_own(g):
        nonlocal result
        before = line.last
        (result,) = run_back("whole", [0], g, of_group[g], None, own=(g, groups, result))
        line.last = before

    def run_put(g, r):
        nonlocal result
        start = (me ^ r) * channels + g * group_width
        zero = jnp.int32(0)
        if len(pieces[g, r]) == 2:
            first, rest = pieces[g, r]
            scale = rest[rows, :rows].astype(F32) + rest[rows + 8, :rows].astype(F32)
            first = (first.astype(F32) * scale[:, None]).astype(BF16)
            result = lax.dynamic_update_slice(result, first, (zero, start))
            result = lax.dynamic_update_slice(result, rest[:rows], (zero, start + width))
        else:
            result = lax.dynamic_update_slice(result, pieces[g, r][0], (zero, start))

    ex = exchanges
    later = range(1, groups)
    run_maps(0)
    run_front(0)
    run_front(1)
    ex[0].pair()
    for g in later:
        run_maps(g)
        run_front(g + 1)
    ex[0].double()
    ex[1].pair()
    run_spans(0)
    ex[0].finish()
    ex[1].double()
    for g in later:
        ex[g + 1].pair()
    run_first(0, apart=True)
    if groups > 1:
        line.run(mark)
    for g in later:
        ex[g + 1].double()
    ex[1].finish()
    run_spans(1, micros=1)
    for g in later:
        run_spans(g + 1, micros=1)
    arrived(0, 0, partners)
    run_rest(0, slice(0, 1))
    for g in later:
        ex[g + 1].finish()
    run_rest(0, slice(1, None))
    run_one(0, 1)
    for g in later:
        arrived(0, 1, partners[:1])
        run_one(g, partners[0])
        run_one(g, 1)
        arrived(0, 1, partners[1:])
        for r in partners[1:]:
            run_one(g, r)
    run_own(0)
    for r in [*partners, 1]:
        run_put(0, r)
    for g in later:
        run_own(g)
        for r in [partners[0], 1, *partners[1:]]:
            run_put(g, r)
    return result


def solution(mesh):
    in_specs = (
        P("ctx", "head"),
        P("ctx", "head"),
        P("ctx", None, "head"),
        P("head", "ctx"),
        P("head", "ctx"),
        P(None, "head"),
        P(None, None, "head"),
        P("head"),
        P("head"),
    )
    out_specs = P(("ctx", "head"), None)
    return jax.shard_map(shards, mesh=mesh, in_specs=in_specs, out_specs=out_specs, check_vma=False)
```

```python
import functools

import jax
import jax.numpy as jnp
import numpy as np
from jax import lax
from jax.experimental import pallas as pl
from jax.experimental.pallas import tpu as pltpu
from jax.sharding import PartitionSpec as P

STATE = 256
SPAN = 128
HALO = 16
EPS = 1e-05
LOC, ECUM, DEV, EDEV = range(4)
F32 = jnp.float32
BF16 = jnp.bfloat16
VMEM_BYTES = 48 * 1024 * 1024
VMEM_SMALL = 8 * 1024 * 1024
COST_SCALE = 10**9
MSG = STATE + 16
KEPT = STATE + 8


def dot(a, b):
    return jnp.dot(a, b, preferred_element_type=F32)


def silu(v):
    half = 0.5 * v
    return half * jnp.tanh(half) + half


def cost(micros):
    return pl.CostEstimate(flops=int(micros * COST_SCALE), bytes_accessed=1, transcendentals=0)


def params(limit=VMEM_BYTES):
    return pltpu.CompilerParams(vmem_limit_bytes=limit)


def lanes_of(heads):
    return -(-2 * heads // 128) * 128


def spread_table(heads, head_dim):
    row = np.arange(lanes_of(heads))
    head = np.where(row < 2 * heads, row % heads, heads)
    return (head[:, None] == (np.arange(heads * head_dim) // head_dim)[None, :]).astype(np.float32)


def decay_kernel(log_ref, step_ref, skip_ref, col_ref, row_ref, table_ref, skips_ref):
    heads, tokens = log_ref.shape
    lanes = lanes_of(heads)
    spans = tokens // SPAN
    r = lax.broadcasted_iota(jnp.int32, (SPAN, SPAN), 0)
    c = lax.broadcasted_iota(jnp.int32, (SPAN, SPAN), 1)
    upper = (r <= c).astype(F32)
    cums = []
    for k in range(spans):
        cums.append(
            jnp.dot(
                log_ref[:, k * SPAN : (k + 1) * SPAN],
                upper,
                precision=lax.Precision.HIGHEST,
                preferred_element_type=F32,
            )
        )
    totals = [cum[:, SPAN - 1 :] for cum in cums]
    before = [jnp.zeros_like(totals[0])]
    for k in range(spans - 1):
        before.append(before[-1] + totals[k])
    after = [jnp.zeros_like(totals[0])]
    for k in range(spans - 1, 0, -1):
        after.insert(0, after[0] + totals[k])

    def put(index, k, value):
        high = value.astype(BF16).astype(F32)
        rest = [jnp.zeros((lanes - 2 * heads, SPAN), F32)] if lanes > 2 * heads else []
        both = jnp.concatenate([high, value - high, *rest], axis=0)
        table_ref[k * SPAN : (k + 1) * SPAN, index * lanes : (index + 1) * lanes] = both.T.astype(BF16)

    skip = skip_ref[...]
    high = skip.astype(BF16).astype(F32)
    none = [jnp.zeros((1, lanes - 2 * heads), F32)] if lanes > 2 * heads else []
    parts = jnp.concatenate([high, skip - high, *none], axis=1)
    skips_ref[...] = jnp.broadcast_to(parts, skips_ref.shape).astype(BF16)
    for k in range(spans):
        cum = cums[k]
        step = step_ref[:, k * SPAN : (k + 1) * SPAN]
        col_ref[k * SPAN : (k + 1) * SPAN, :] = jnp.concatenate([cum] * (lanes // heads), axis=0).T
        row_ref[:, k * SPAN : (k + 1) * SPAN] = cum - jnp.log(step)
        to_end = totals[k] - cum
        put(LOC, k, jnp.exp(to_end) * step)
        put(DEV, k, jnp.exp(to_end + after[k]) * step)
        put(ECUM, k, jnp.exp(cum))
        put(EDEV, k, jnp.exp(cum + before[k]))


def behind(count):
    return [pl.BlockSpec(memory_space=pl.ANY)] * count


def decay_tables(log_decay, step_size, skip_gain):
    heads, tokens = log_decay.shape
    lanes = lanes_of(heads)
    return pl.pallas_call(
        decay_kernel,
        out_shape=(
            jax.ShapeDtypeStruct((tokens, lanes), F32),
            jax.ShapeDtypeStruct((heads, tokens), F32),
            jax.ShapeDtypeStruct((tokens, 4 * lanes), BF16),
            jax.ShapeDtypeStruct((16, lanes), BF16),
        ),
        compiler_params=params(),
        name="decays",
        cost_estimate=cost(50),
    )(log_decay, step_size, skip_gain[None])


def conv_rows(read, rows, halo, taps, store):
    count, width = taps.shape
    tile = SPAN
    for b in range(rows // tile):
        for c in range(1):
            cols = slice(0, width)
            own = read(b * tile, (b + 1) * tile, cols).astype(F32)
            prev = (halo[:, cols] if b == 0 else read(b * tile - HALO, b * tile, cols)).astype(F32)
            both = jnp.concatenate([prev[HALO - 8 :], own], axis=0)
            total = own * taps[count - 1 : count, cols]
            for k in range(1, count):
                total = total + both[8 - k : 8 - k + tile] * taps[count - 1 - k : count - k, cols]
            store(slice(b * tile, (b + 1) * tile), cols, silu(total))


def read_state(ref):
    if ref.dtype == F32:
        return ref[:STATE, :], ref[STATE : STATE + 1, :]
    tail = ref[STATE:MSG, :].astype(F32)
    return ref[:STATE, :].astype(F32), tail[0:1] + tail[8:9]


def write_kept(ref, value, decay):
    ref[:STATE, :] = value
    ref[STATE:KEPT, :] = jnp.broadcast_to(decay, (KEPT - STATE, decay.shape[1]))


def write_sent(ref, value, decay):
    ref[:STATE, :] = value.astype(BF16)
    high = decay.astype(BF16).astype(F32)
    shape = (8, decay.shape[1])
    rows = jnp.concatenate([jnp.broadcast_to(high, shape), jnp.broadcast_to(decay - high, shape)], axis=0)
    ref[STATE:MSG, :] = rows.astype(BF16)


def maps_kernel(order, io_ref, halo_ref, taps_ref, *refs):
    map_ref, turned_ref = refs[order:]

    def put_in(rows, cols, value):
        map_ref[rows, :STATE] = value.astype(BF16)

    def put_out(rows, cols, value):
        map_ref[rows, STATE:] = value.astype(BF16)

    tokens = io_ref.shape[0]
    for i, put in ((0, put_in), (1, put_out)):
        conv_rows(
            lambda lo, hi, cols: io_ref[lo:hi, i, cols], tokens, halo_ref[:, i, :], taps_ref[:, i, :].astype(F32), put
        )
    for b in range(tokens // SPAN):
        rows = slice(b * SPAN, (b + 1) * SPAN)
        turned_ref[:, rows] = map_ref[rows, :STATE].T


def maps_of(group, state_io, halo, conv_state, after):
    tokens = state_io.shape[0]
    count = conv_state.shape[0]

    def mine(j):
        return (0, 0, group)

    return pl.pallas_call(
        functools.partial(maps_kernel, len(after)),
        grid=(1,),
        in_specs=[
            pl.BlockSpec((tokens, 2, STATE), mine),
            pl.BlockSpec((HALO, 2, STATE), mine),
            pl.BlockSpec((count, 2, STATE), mine),
            *behind(len(after)),
        ],
        out_specs=[
            pl.BlockSpec((tokens, 2 * STATE), lambda j: (0, 0)),
            pl.BlockSpec((STATE, tokens), lambda j: (0, 0)),
        ],
        out_shape=[
            jax.ShapeDtypeStruct((tokens, 2 * STATE), BF16),
            jax.ShapeDtypeStruct((STATE, tokens), BF16),
        ],
        compiler_params=params(),
        name="maps",
        cost_estimate=cost(3),
    )(state_io, halo, conv_state, *after)


def front_kernel(order, blocks, where_ref, feat_ref, halo_ref, taps_ref, dev_ref, edev_ref, spread_ref, turned_ref, *refs):
    xh_ref, sent_ref, kept_ref, scaled, wide = refs[order:]
    j = pl.program_id(0)
    spread = spread_ref[...]
    wide[...] = dot(dev_ref[...], spread)

    def put_feat(rows, cols, value):
        value = value.astype(BF16)
        xh_ref[rows, cols] = value
        scaled[rows, cols] = (value.astype(F32) * wide[rows, cols]).astype(BF16)

    conv_rows(
        lambda lo, hi, cols: feat_ref[lo:hi, cols], feat_ref.shape[0], halo_ref[...], taps_ref[...].astype(F32), put_feat
    )
    state = dot(turned_ref[...], scaled[...])
    decay = dot(edev_ref[...], spread)[15:16]

    @pl.when(j < blocks)
    def _():
        write_sent(sent_ref, state, decay)

    @pl.when(j >= blocks)
    def _():
        write_kept(kept_ref, state, decay)


def front(chunk, where, features, halo, conv_feat, table, spread, turned, after):
    tokens = features.shape[0]
    start, width = chunk
    half = width // 2
    block = min(512, half)
    blocks = half // block
    base = start // block
    count = conv_feat.shape[0]
    heads2 = spread.shape[0]

    def place(j, where):
        sending = (j < blocks).astype(jnp.int32)
        which = sending * (1 - where[1]) + (1 - sending) * where[1]
        return which * blocks + j - (1 - sending) * blocks

    def cols(j, where):
        return (0, base + place(j, where))

    def same(j, where):
        return (0, 0)

    return pl.pallas_call(
        functools.partial(front_kernel, len(after), blocks),
        grid_spec=pltpu.PrefetchScalarGridSpec(
            num_scalar_prefetch=1,
            grid=(2 * blocks,),
            in_specs=[
                pl.BlockSpec((tokens, block), cols),
                pl.BlockSpec((HALO, block), cols),
                pl.BlockSpec((count, block), cols),
                pl.BlockSpec((tokens, heads2), lambda j, where: (0, DEV)),
                pl.BlockSpec((16, heads2), lambda j, where: (tokens // 16 - 1, EDEV)),
                pl.BlockSpec((heads2, block), cols),
                pl.BlockSpec((STATE, tokens), same),
                *behind(len(after)),
            ],
            out_specs=[
                pl.BlockSpec((tokens, block), lambda j, where: (0, place(j, where))),
                pl.BlockSpec((MSG, block), lambda j, where: (0, jnp.minimum(j, blocks - 1))),
                pl.BlockSpec((KEPT, block), lambda j, where: (0, jnp.maximum(j - blocks, 0))),
            ],
            scratch_shapes=[pltpu.VMEM((tokens, block), BF16), pltpu.VMEM((tokens, block), F32)],
        ),
        out_shape=[
            jax.ShapeDtypeStruct((tokens, width), BF16),
            jax.ShapeDtypeStruct((MSG, half), BF16),
            jax.ShapeDtypeStruct((KEPT, half), F32),
        ],
        compiler_params=params(),
        name="front",
        cost_estimate=cost(4),
    )(where, features, halo, conv_feat, table, table, spread, turned, *after)


def span_kernel(
    first_head, order, xh_ref, map_ref, col_ref, row_ref, table_ref, spread_ref, skips_ref, halves_ref,
    *refs,
):
    y_ref, state = refs[order:]
    width = xh_ref.shape[1]
    head_dim = width // row_ref.shape[0]
    heads2 = spread_ref.shape[0]

    @pl.when(pl.program_id(0) == 0)
    def _():
        state[...] = jnp.zeros_like(state)

    t = lax.broadcasted_iota(jnp.int32, (SPAN, SPAN), 0)
    s = lax.broadcasted_iota(jnp.int32, (SPAN, SPAN), 1)
    first = halves_ref[0:1, :]
    second = halves_ref[1:2, :]
    block = 256
    for k in range(xh_ref.shape[0] // SPAN):
        rows = slice(k * SPAN, (k + 1) * SPAN)
        in_map = map_ref[rows, :STATE]
        out_map = map_ref[rows, STATE:]
        scores = lax.dot_general(out_map, in_map, (((1,), (1,)), ((), ())), preferred_element_type=F32)
        scores = jnp.where(s <= t, scores, 0.0)
        in_turned = in_map.T
        tables = jnp.concatenate([table_ref[rows, :heads2], table_ref[rows, heads2:], skips_ref[...]], axis=0)
        for q in range(width // block):
            cols = slice(q * block, (q + 1) * block)
            feats = xh_ref[rows, cols]
            feats32 = feats.astype(F32)
            wide = dot(tables, spread_ref[:, cols])
            scaled = (feats32 * wide[:SPAN]).astype(BF16)
            ecum = wide[SPAN : 2 * SPAN]
            skip = wide[2 * SPAN : 2 * SPAN + 1]
            pairs = []
            for p in range(block // 128):
                weights = []
                for i in range(2):
                    h = (q * block + p * 128) // head_dim + i
                    gap = col_ref[rows, first_head + h : first_head + h + 1] - row_ref[h : h + 1, rows]
                    weights.append((scores * jnp.exp(jnp.minimum(gap, 0.0))).astype(BF16))
                pair = feats[:, p * 128 : (p + 1) * 128]
                stacked = jnp.concatenate([pair * first, pair * second], axis=0)
                pairs.append(dot(jnp.concatenate(weights, axis=1), stacked))
            diag = jnp.concatenate(pairs, axis=1)
            held = state[:, cols]
            carried = dot(out_map, held.astype(BF16)) * ecum
            y_ref[rows, cols] = (diag + carried + skip * feats32).astype(BF16)
            state[:, cols] = ecum[SPAN - 1 :] * held + dot(in_turned, scaled)


def spans_of(chunk, part, parts, micros, head_dim, xh, both_maps, col, row, table, spread, skips, halves, after):
    tokens = xh.shape[0]
    width = chunk[1] // parts
    index = chunk[0] // width + part
    some = width // head_dim
    heads2 = spread.shape[0]
    tile = 2 * SPAN
    return pl.pallas_call(
        functools.partial(span_kernel, index * some, len(after)),
        grid=(tokens // tile,),
        in_specs=[
            pl.BlockSpec((tile, width), lambda k: (k, part)),
            pl.BlockSpec((tile, 2 * STATE), lambda k: (k, 0)),
            pl.BlockSpec((tile, heads2), lambda k: (k, 0)),
            pl.BlockSpec((some, tile), lambda k: (index, k)),
            pl.BlockSpec((tile, 2 * heads2), lambda k: (k, 0)),
            pl.BlockSpec((heads2, width), lambda k: (0, index)),
            pl.BlockSpec(skips.shape, lambda k: (0, 0)),
            pl.BlockSpec(halves.shape, lambda k: (0, 0)),
            *behind(len(after)),
        ],
        out_specs=pl.BlockSpec((tile, width), lambda k: (k, 0)),
        out_shape=jax.ShapeDtypeStruct((tokens, width), BF16),
        scratch_shapes=[pltpu.VMEM((STATE, width), F32)],
        compiler_params=params(),
        name="spans",
        cost_estimate=cost(micros),
    )(xh, both_maps, col, row, table, spread, skips, halves, *after)


def pair_kernel(where_ref, kept_ref, got_ref, *refs):
    total_ref, sent_ref = refs[-2:]
    kept, kept_decay = read_state(kept_ref)
    got, got_decay = read_state(got_ref)

    def put(first, second, decay):
        total = decay * first + second
        write_kept(total_ref, total, kept_decay * got_decay)
        write_sent(sent_ref, total, kept_decay * got_decay)

    @pl.when(where_ref[1] == 0)
    def _():
        put(kept, got, got_decay)

    @pl.when(where_ref[1] == 1)
    def _():
        put(got, kept, kept_decay)


def inclusive_kernel(total_ref, before_ref, *refs):
    sent_ref = refs[-1]
    total, decay = read_state(total_ref)
    before, before_decay = read_state(before_ref)
    write_sent(sent_ref, total + decay * before, decay * before_decay)


def extend_kernel(before_ref, far_ref, *refs):
    before, decay = read_state(before_ref)
    far, far_decay = read_state(far_ref)
    write_kept(refs[-1], before + decay * far, decay * far_decay)


def last_kernel(where_ref, before_ref, far_ref, kept_ref, got_ref, *refs):
    mine_ref, sent_ref = refs[-2:]
    before, before_decay = read_state(before_ref)
    far, _ = read_state(far_ref)
    carried = before + before_decay * far

    @pl.when(where_ref[1] == 0)
    def _():
        kept, decay = read_state(kept_ref)
        mine_ref[...] = carried.astype(BF16)
        sent_ref[...] = (decay * carried + kept).astype(BF16)

    @pl.when(where_ref[1] == 1)
    def _():
        got, decay = read_state(got_ref)
        mine_ref[...] = (decay * carried + got).astype(BF16)
        sent_ref[...] = carried.astype(BF16)


def join(kernel, name, where, operands, outs, after):
    width = operands[0].shape[1]
    shapes = {
        "kept": jax.ShapeDtypeStruct((KEPT, width), F32),
        "sent": jax.ShapeDtypeStruct((MSG, width), BF16),
        "state": jax.ShapeDtypeStruct((STATE, width), BF16),
    }
    scalars = [] if where is None else [where]
    return pl.pallas_call(
        kernel,
        in_specs=[pl.BlockSpec(memory_space=pltpu.SMEM)] * len(scalars)
        + [pl.BlockSpec(memory_space=pltpu.VMEM)] * len(operands)
        + behind(len(after)),
        out_specs=[pl.BlockSpec(memory_space=pltpu.VMEM)] * len(outs),
        out_shape=[shapes[out] for out in outs],
        compiler_params=params(VMEM_SMALL),
        name=name,
        cost_estimate=cost(0.7),
    )(*scalars, *operands, *after)


def back_kernel(mode, counts, partners, order, where_ref, out_ref, edev_ref, *refs):
    chunks = []
    for pieces in counts:
        chunks.append((refs[:pieces], *refs[pieces : pieces + 5]))
        refs = refs[pieces + 5 :]
    if mode == "rest":
        squares_ref, *refs = refs
    refs = refs[order:]
    o_refs = refs[:partners]
    if mode == "first":
        squares_ref = refs[partners]
    gated, sums = refs[-2:]
    out_map = out_ref[...]
    edev = edev_ref[...]
    rows = out_map.shape[0]
    block = 256
    steps = pl.num_programs(0) // partners
    odd = where_ref[1] == 1
    sums[...] = squares_ref[...] if mode == "rest" else jnp.zeros((rows, 128), F32)
    at = 0
    for y_refs, mine_ref, other_ref, spread_ref, gate_ref, gain_ref in chunks:
        half = mine_ref.shape[1]
        for q in range(2 * half // block):
            cols = slice(q * block, (q + 1) * block)
            inner = slice(q * block % half, q * block % half + block)
            mine = mine_ref[:, inner]
            other = other_ref[:, inner]
            state = jnp.where(odd, other, mine) if q * block < half else jnp.where(odd, mine, other)
            gated[:, at : at + block] = dot(out_map, state) * dot(edev, spread_ref[:, cols])
            y_ref = y_refs[q * block // y_refs[0].shape[1]]
            y_at = q * block % y_refs[0].shape[1]
            for c in range(block // 128):
                y_cols = slice(y_at + c * 128, y_at + (c + 1) * 128)
                to = slice(at + c * 128, at + (c + 1) * 128)
                cols = slice(q * block + c * 128, q * block + (c + 1) * 128)
                gain = gain_ref[:, cols]
                for b in range(rows // 64):
                    part = slice(b * 64, (b + 1) * 64)
                    value = (y_ref[part, y_cols].astype(F32) + gated[part, to]) * silu(gate_ref[part, cols].astype(F32))
                    sums[part, :] = sums[part, :] + value * value
                    gated[part, to] = value * gain
            at += block
    if mode == "first":
        squares_ref[...] = sums[...]
    else:
        width = at if mode == "whole" else 2 * at
        mean = jnp.sum(sums[...], axis=1, keepdims=True) * (1.0 / width)
        scale = lax.rsqrt(mean + EPS)
    for p in range(partners):

        @pl.when(pl.program_id(0) // steps == p)
        def _(o_ref=o_refs[p]):
            if mode == "rest":
                step = pl.program_id(0) - p * steps
                start = pl.multiple_of(step * rows, rows)
                high = scale.astype(BF16).astype(F32)
                parts = [jnp.broadcast_to(part, (rows, 128)).T[:8] for part in (high, scale - high)]
                o_ref[steps * rows :, pl.ds(start, rows)] = jnp.concatenate(parts, axis=0).astype(BF16)
            for q in range(at // block):
                cols = slice(q * block, (q + 1) * block)
                value = gated[:, cols] if mode == "first" else gated[:, cols] * scale
                if mode == "rest":
                    o_ref[pl.ds(start, rows), cols] = value.astype(BF16)
                else:
                    o_ref[:, cols] = value.astype(BF16)


def back(mode, some, where, rows, chunks, both_maps, table, spread, gates, gain_row, squares, after, own=None):
    heads2 = spread.shape[0]
    tile = 128
    steps = rows // tile
    partners = len(some)

    def at(i, where):
        turn = some[0]
        for p in range(1, partners):
            turn = jnp.where(i >= p * steps, some[p], turn)
        return ((where[0] ^ turn) * steps + i % steps, 0)

    specs = [
        pl.BlockSpec((tile, STATE), lambda i, where: (at(i, where)[0], 1)),
        pl.BlockSpec((tile, heads2), lambda i, where: (at(i, where)[0], EDEV)),
    ]
    operands = [both_maps, table]
    total = 0
    for (start, width), ys, mine, other in chunks:
        index = start // width
        half = width // 2
        total += width
        specs += [pl.BlockSpec((tile, y.shape[1]), at) for y in ys]
        specs += [
            pl.BlockSpec((STATE, half), lambda i, where: (0, 0)),
            pl.BlockSpec((STATE, half), lambda i, where: (0, 0)),
            pl.BlockSpec((heads2, width), lambda i, where, index=index: (0, index)),
            pl.BlockSpec((tile, width), lambda i, where, index=index: (at(i, where)[0], index)),
            pl.BlockSpec((1, width), lambda i, where, index=index: (0, index)),
        ]
        operands += [*ys, mine, other, spread, gates, gain_row]
    if mode == "rest":
        specs.append(pl.BlockSpec((tile, 128), lambda i, where: (i, 0)))
        operands.append(squares)
    aliases = {}
    if own is not None and own[2] is not None:
        after = [own[2], *after]
        aliases = {1 + len(operands): partners - 1}
    specs += behind(len(after))
    operands += after
    sent = rows + 16 if mode == "rest" else rows
    part = sent if mode == "rest" else tile

    def part_of(p):
        if mode == "rest":
            return lambda i, where: (0, 0)
        return lambda i, where: (jnp.clip(i - p * steps, 0, steps - 1), 0)

    out_specs = [pl.BlockSpec((part, total), part_of(p)) for p in range(partners)]
    out_shape = [jax.ShapeDtypeStruct((sent, total), BF16)] * partners
    if own is not None:
        group, groups, _ = own
        out_specs[-1] = pl.BlockSpec(
            (tile, total),
            lambda i, where: (jnp.clip(i - (partners - 1) * steps, 0, steps - 1), (where[0] ^ some[-1]) * groups + group),
        )
        out_shape[-1] = jax.ShapeDtypeStruct((rows, groups * total * (gates.shape[0] // rows)), BF16)
    if mode == "first":
        out_specs.append(pl.BlockSpec((tile, 128), lambda i, where: (i, 0)))
        out_shape.append(jax.ShapeDtypeStruct((partners * rows, 128), F32))
    return pl.pallas_call(
        functools.partial(back_kernel, mode, [len(ys) for _, ys, _, _ in chunks], partners, len(after)),
        grid_spec=pltpu.PrefetchScalarGridSpec(
            num_scalar_prefetch=1,
            grid=(partners * steps,),
            in_specs=specs,
            out_specs=out_specs,
            scratch_shapes=[pltpu.VMEM((tile, total), F32), pltpu.VMEM((tile, 128), F32)],
        ),
        out_shape=out_shape,
        input_output_aliases=aliases,
        compiler_params=params(),
        name=f"back_{mode}",
        cost_estimate=cost(1),
    )(where, *operands)


def mark_kernel(order, *refs):
    refs[order][...] = jnp.zeros((8, 128), F32)


def mark(after):
    return pl.pallas_call(
        functools.partial(mark_kernel, len(after)),
        grid=(1,),
        in_specs=behind(len(after)),
        out_specs=pl.BlockSpec((8, 128), lambda i: (0, 0)),
        out_shape=jax.ShapeDtypeStruct((8, 128), F32),
        compiler_params=params(VMEM_SMALL),
        name="mark",
        cost_estimate=cost(200),
    )(*after)


def shifted(value, pairs, steps):
    return lax.ppermute(
        value,
        "ctx",
        [(2 * q + y, 2 * (q + steps) + y) for q in range(pairs - steps) for y in range(2)],
    )


def swapped(value, pairs):
    return lax.ppermute(value, "ctx", [(2 * q + y, 2 * q + 1 - y) for q in range(pairs) for y in range(2)])


class Line:
    def __init__(self):
        self.last = []

    def run(self, make, *args, **kwargs):
        made = make(*args, after=self.last, **kwargs)
        self.last = [made[0] if isinstance(made, (list, tuple)) else made]
        return made


class Exchange:
    def __init__(self, line, where, pairs, sent, kept):
        self.line = line
        self.where = where
        self.pairs = pairs
        self.kept = kept
        self.got = swapped(sent, pairs)

    def pair(self):
        self.total, sent = self.line.run(
            join, pair_kernel, "pair", self.where, [self.kept, self.got], ["kept", "sent"]
        )
        self.before = shifted(sent, self.pairs, 1)
        self.reach = 1

    def double(self):
        (sent,) = self.line.run(join, inclusive_kernel, "inclusive", None, [self.total, self.before], ["sent"])
        self.far = shifted(sent, self.pairs, self.reach + 1)
        self.reach = 2 * self.reach + 1

    def extend(self):
        while self.reach < self.pairs - 1:
            (self.before,) = self.line.run(join, extend_kernel, "extend", None, [self.before, self.far], ["kept"])
            self.double()

    def finish(self):
        self.extend()
        self.mine, sent = self.line.run(
            join, last_kernel, "last", self.where, [self.before, self.far, self.kept, self.got], ["state", "state"]
        )
        self.other = swapped(sent, self.pairs)


def shards(
    features, gates, state_io, step_size, log_decay, conv_feat, conv_state, skip_gain, norm_gain
):
    tokens, channels = features.shape
    heads = step_size.shape[0]
    head_dim = channels // heads
    groups = state_io.shape[2] // STATE
    group_width = channels // groups
    width = group_width // 2
    count = conv_feat.shape[0]
    rim = count - 1
    ctx_size = lax.axis_size("ctx")
    head_size = lax.axis_size("head")
    pairs = ctx_size // 2
    rows = tokens // head_size
    me = lax.axis_index("head").astype(jnp.int32)
    where = jnp.stack([me, lax.axis_index("ctx").astype(jnp.int32) % 2])

    onward = [(i, i + 1) for i in range(ctx_size - 1)]
    pad = HALO - rim
    halo = jnp.pad(lax.ppermute(features[tokens - rim :], "ctx", onward), ((pad, 0), (0, 0)))
    io_halo = jnp.pad(lax.ppermute(state_io[tokens - rim :], "ctx", onward), ((pad, 0), (0, 0), (0, 0)))
    spread = jnp.asarray(spread_table(heads, head_dim), BF16)
    halves = jnp.asarray(np.arange(128)[None, :] // head_dim == np.arange(2)[:, None], BF16)
    col, row, table, skips = decay_tables(log_decay, step_size, skip_gain)
    gain_row = norm_gain[None]

    line = Line()
    chunks = [(0, width), (width, width)] + [(g * group_width, group_width) for g in range(1, groups)]
    of_group = [[0, 1]] + [[g + 1] for g in range(1, groups)]
    group_of = [0, 0] + list(range(1, groups))
    fronts = {}
    maps = {}
    exchanges = {}
    ys = {}

    def run_maps(g):
        maps[g] = line.run(maps_of, g, state_io, io_halo, conv_state)

    def run_front(c):
        made = line.run(
            front, chunks[c], where, features, halo, conv_feat, table, spread, maps[group_of[c]][1]
        )
        fronts[c] = made[0]
        exchanges[c] = Exchange(line, where, pairs, made[1], made[2])

    def run_spans(c, part=0, parts=1, micros=200):
        g = group_of[c]
        made = line.run(
            spans_of, chunks[c], part, parts, micros, head_dim, fronts[c], maps[g][0], col, row, table, spread,
            skips, halves,
        )
        ys.setdefault(c, []).append(made)

    def part(c):
        return (chunks[c], ys[c], exchanges[c].mine, exchanges[c].other)

    partners = list(range(head_size - 1, 1, -1))
    squares = {}
    pieces = {}

    def ship(piece, r):
        return lax.ppermute(piece, "head", [(i, i ^ r) for i in range(head_size)])

    def run_back(mode, some, g, parts, squares, own=None):
        return line.run(
            back, mode, some, where, rows, [part(c) for c in parts], maps[g][0], table, spread, gates, gain_row,
            squares, own=own,
        )

    def arrived(g, index, some):
        line.last += [pieces[g, r][index] for r in some]

    def run_first(g, apart=False):
        squares[g] = []
        for some in [[r] for r in partners] if apart else [partners]:
            *made, square = run_back("first", some, g, [0], None)
            squares[g].append((some, square))
            for r, piece in zip(some, made):
                pieces[g, r] = [ship(piece, r)]

    def run_rest(g, turns):
        for some, square in squares[g][turns]:
            made = run_back("rest", some, g, [1], square)
            for r, piece in zip(some, made):
                pieces[g, r].append(ship(piece, r))

    result = None

    def run_one(g, r):
        (piece,) = run_back("whole", [r], g, of_group[g], None)
        pieces[g, r] = [ship(piece, r)]

    def run_own(g):
        nonlocal result
        before = line.last
        (result,) = run_back("whole", [0], g, of_group[g], None, own=(g, groups, result))
        line.last = before

    def run_put(g, r):
        nonlocal result
        start = (me ^ r) * channels + g * group_width
        zero = jnp.int32(0)
        if len(pieces[g, r]) == 2:
            first, rest = pieces[g, r]
            scale = rest[rows, :rows].astype(F32) + rest[rows + 8, :rows].astype(F32)
            first = (first.astype(F32) * scale[:, None]).astype(BF16)
            result = lax.dynamic_update_slice(result, first, (zero, start))
            result = lax.dynamic_update_slice(result, rest[:rows], (zero, start + width))
        else:
            result = lax.dynamic_update_slice(result, pieces[g, r][0], (zero, start))

    ex = exchanges
    later = range(1, groups)
    run_maps(0)
    run_front(0)
    run_front(1)
    ex[0].pair()
    for g in later:
        run_maps(g)
    ex[0].double()
    ex[1].pair()
    for g in later:
        run_front(g + 1)
    run_spans(0)
    ex[0].finish()
    ex[1].double()
    for g in later:
        ex[g + 1].pair()
    run_first(0, apart=True)
    if groups > 1:
        line.run(mark)
    run_spans(1, micros=1)
    ex[1].finish()
    for g in later:
        ex[g + 1].double()
    for g in later:
        run_spans(g + 1, micros=1)
    arrived(0, 0, partners)
    run_rest(0, slice(0, 1))
    for g in later:
        ex[g + 1].finish()
    run_rest(0, slice(1, None))
    run_one(0, 1)
    for g in later:
        arrived(0, 1, partners[:1])
        run_one(g, partners[0])
        run_one(g, 1)
        arrived(0, 1, partners[1:])
        for r in partners[1:]:
            run_one(g, r)
    run_own(0)
    for r in [*partners, 1]:
        run_put(0, r)
    for g in later:
        run_own(g)
        for r in [partners[0], 1, *partners[1:]]:
            run_put(g, r)
    return result


def solution(mesh):
    in_specs = (
        P("ctx", "head"),
        P("ctx", "head"),
        P("ctx", None, "head"),
        P("head", "ctx"),
        P("head", "ctx"),
        P(None, "head"),
        P(None, None, "head"),
        P("head"),
        P("head"),
    )
    out_specs = P(("ctx", "head"), None)
    return jax.shard_map(shards, mesh=mesh, in_specs=in_specs, out_specs=out_specs, check_vma=False)
```

```python
import functools

import jax
import jax.numpy as jnp
import numpy as np
from jax import lax
from jax.experimental import pallas as pl
from jax.experimental.pallas import tpu as pltpu
from jax.sharding import PartitionSpec as P

STATE = 256
SPAN = 128
HALO = 16
EPS = 1e-05
LOC, ECUM, DEV, EDEV = range(4)
F32 = jnp.float32
BF16 = jnp.bfloat16
VMEM_BYTES = 48 * 1024 * 1024
VMEM_SMALL = 8 * 1024 * 1024
COST_SCALE = 10**9
MSG = STATE + 16
KEPT = STATE + 8


def dot(a, b):
    return jnp.dot(a, b, preferred_element_type=F32)


def silu(v):
    half = 0.5 * v
    return half * jnp.tanh(half) + half


def cost(micros):
    return pl.CostEstimate(flops=int(micros * COST_SCALE), bytes_accessed=1, transcendentals=0)


def params(limit=VMEM_BYTES):
    return pltpu.CompilerParams(vmem_limit_bytes=limit)


def lanes_of(heads):
    return -(-2 * heads // 128) * 128


def spread_table(heads, head_dim):
    row = np.arange(lanes_of(heads))
    head = np.where(row < 2 * heads, row % heads, heads)
    return (head[:, None] == (np.arange(heads * head_dim) // head_dim)[None, :]).astype(np.float32)


def decay_kernel(log_ref, step_ref, skip_ref, col_ref, row_ref, table_ref, skips_ref):
    heads, tokens = log_ref.shape
    lanes = lanes_of(heads)
    spans = tokens // SPAN
    r = lax.broadcasted_iota(jnp.int32, (SPAN, SPAN), 0)
    c = lax.broadcasted_iota(jnp.int32, (SPAN, SPAN), 1)
    upper = (r <= c).astype(F32)
    cums = []
    for k in range(spans):
        cums.append(
            jnp.dot(
                log_ref[:, k * SPAN : (k + 1) * SPAN],
                upper,
                precision=lax.Precision.HIGHEST,
                preferred_element_type=F32,
            )
        )
    totals = [cum[:, SPAN - 1 :] for cum in cums]
    before = [jnp.zeros_like(totals[0])]
    for k in range(spans - 1):
        before.append(before[-1] + totals[k])
    after = [jnp.zeros_like(totals[0])]
    for k in range(spans - 1, 0, -1):
        after.insert(0, after[0] + totals[k])

    def put(index, k, value):
        high = value.astype(BF16).astype(F32)
        rest = [jnp.zeros((lanes - 2 * heads, SPAN), F32)] if lanes > 2 * heads else []
        both = jnp.concatenate([high, value - high, *rest], axis=0)
        table_ref[k * SPAN : (k + 1) * SPAN, index * lanes : (index + 1) * lanes] = both.T.astype(BF16)

    skip = skip_ref[...]
    high = skip.astype(BF16).astype(F32)
    none = [jnp.zeros((1, lanes - 2 * heads), F32)] if lanes > 2 * heads else []
    parts = jnp.concatenate([high, skip - high, *none], axis=1)
    skips_ref[...] = jnp.broadcast_to(parts, skips_ref.shape).astype(BF16)
    for k in range(spans):
        cum = cums[k]
        step = step_ref[:, k * SPAN : (k + 1) * SPAN]
        col_ref[k * SPAN : (k + 1) * SPAN, :] = jnp.concatenate([cum] * (lanes // heads), axis=0).T
        row_ref[:, k * SPAN : (k + 1) * SPAN] = cum - jnp.log(step)
        to_end = totals[k] - cum
        put(LOC, k, jnp.exp(to_end) * step)
        put(DEV, k, jnp.exp(to_end + after[k]) * step)
        put(ECUM, k, jnp.exp(cum))
        put(EDEV, k, jnp.exp(cum + before[k]))


def behind(count):
    return [pl.BlockSpec(memory_space=pl.ANY)] * count


def decay_tables(log_decay, step_size, skip_gain):
    heads, tokens = log_decay.shape
    lanes = lanes_of(heads)
    return pl.pallas_call(
        decay_kernel,
        out_shape=(
            jax.ShapeDtypeStruct((tokens, lanes), F32),
            jax.ShapeDtypeStruct((heads, tokens), F32),
            jax.ShapeDtypeStruct((tokens, 4 * lanes), BF16),
            jax.ShapeDtypeStruct((16, lanes), BF16),
        ),
        compiler_params=params(),
        name="decays",
        cost_estimate=cost(50),
    )(log_decay, step_size, skip_gain[None])


def conv_rows(read, rows, halo, taps, store):
    count, width = taps.shape
    tile = SPAN
    for b in range(rows // tile):
        for c in range(1):
            cols = slice(0, width)
            own = read(b * tile, (b + 1) * tile, cols).astype(F32)
            prev = (halo[:, cols] if b == 0 else read(b * tile - HALO, b * tile, cols)).astype(F32)
            both = jnp.concatenate([prev[HALO - 8 :], own], axis=0)
            total = own * taps[count - 1 : count, cols]
            for k in range(1, count):
                total = total + both[8 - k : 8 - k + tile] * taps[count - 1 - k : count - k, cols]
            store(slice(b * tile, (b + 1) * tile), cols, silu(total))


def read_state(ref):
    if ref.dtype == F32:
        return ref[:STATE, :], ref[STATE : STATE + 1, :]
    tail = ref[STATE:MSG, :].astype(F32)
    return ref[:STATE, :].astype(F32), tail[0:1] + tail[8:9]


def write_kept(ref, value, decay):
    ref[:STATE, :] = value
    ref[STATE:KEPT, :] = jnp.broadcast_to(decay, (KEPT - STATE, decay.shape[1]))


def write_sent(ref, value, decay):
    ref[:STATE, :] = value.astype(BF16)
    high = decay.astype(BF16).astype(F32)
    shape = (8, decay.shape[1])
    rows = jnp.concatenate([jnp.broadcast_to(high, shape), jnp.broadcast_to(decay - high, shape)], axis=0)
    ref[STATE:MSG, :] = rows.astype(BF16)


def maps_kernel(order, io_ref, halo_ref, taps_ref, *refs):
    map_ref, turned_ref = refs[order:]

    def put_in(rows, cols, value):
        map_ref[rows, :STATE] = value.astype(BF16)

    def put_out(rows, cols, value):
        map_ref[rows, STATE:] = value.astype(BF16)

    tokens = io_ref.shape[0]
    for i, put in ((0, put_in), (1, put_out)):
        conv_rows(
            lambda lo, hi, cols: io_ref[lo:hi, i, cols], tokens, halo_ref[:, i, :], taps_ref[:, i, :].astype(F32), put
        )
    for b in range(tokens // SPAN):
        rows = slice(b * SPAN, (b + 1) * SPAN)
        turned_ref[:, rows] = map_ref[rows, :STATE].T


def maps_of(group, state_io, halo, conv_state, after):
    tokens = state_io.shape[0]
    count = conv_state.shape[0]

    def mine(j):
        return (0, 0, group)

    return pl.pallas_call(
        functools.partial(maps_kernel, len(after)),
        grid=(1,),
        in_specs=[
            pl.BlockSpec((tokens, 2, STATE), mine),
            pl.BlockSpec((HALO, 2, STATE), mine),
            pl.BlockSpec((count, 2, STATE), mine),
            *behind(len(after)),
        ],
        out_specs=[
            pl.BlockSpec((tokens, 2 * STATE), lambda j: (0, 0)),
            pl.BlockSpec((STATE, tokens), lambda j: (0, 0)),
        ],
        out_shape=[
            jax.ShapeDtypeStruct((tokens, 2 * STATE), BF16),
            jax.ShapeDtypeStruct((STATE, tokens), BF16),
        ],
        compiler_params=params(),
        name="maps",
        cost_estimate=cost(3),
    )(state_io, halo, conv_state, *after)


def front_kernel(order, blocks, where_ref, feat_ref, halo_ref, taps_ref, dev_ref, edev_ref, spread_ref, turned_ref, *refs):
    xh_ref, sent_ref, kept_ref, scaled, wide = refs[order:]
    j = pl.program_id(0)
    spread = spread_ref[...]
    wide[...] = dot(dev_ref[...], spread)

    def put_feat(rows, cols, value):
        value = value.astype(BF16)
        xh_ref[rows, cols] = value
        scaled[rows, cols] = (value.astype(F32) * wide[rows, cols]).astype(BF16)

    conv_rows(
        lambda lo, hi, cols: feat_ref[lo:hi, cols], feat_ref.shape[0], halo_ref[...], taps_ref[...].astype(F32), put_feat
    )
    state = dot(turned_ref[...], scaled[...])
    decay = dot(edev_ref[...], spread)[15:16]

    @pl.when(j < blocks)
    def _():
        write_sent(sent_ref, state, decay)

    @pl.when(j >= blocks)
    def _():
        write_kept(kept_ref, state, decay)


def front(chunk, where, features, halo, conv_feat, table, spread, turned, after):
    tokens = features.shape[0]
    start, width = chunk
    half = width // 2
    block = min(512, half)
    blocks = half // block
    base = start // block
    count = conv_feat.shape[0]
    heads2 = spread.shape[0]

    def place(j, where):
        sending = (j < blocks).astype(jnp.int32)
        which = sending * (1 - where[1]) + (1 - sending) * where[1]
        return which * blocks + j - (1 - sending) * blocks

    def cols(j, where):
        return (0, base + place(j, where))

    def same(j, where):
        return (0, 0)

    return pl.pallas_call(
        functools.partial(front_kernel, len(after), blocks),
        grid_spec=pltpu.PrefetchScalarGridSpec(
            num_scalar_prefetch=1,
            grid=(2 * blocks,),
            in_specs=[
                pl.BlockSpec((tokens, block), cols),
                pl.BlockSpec((HALO, block), cols),
                pl.BlockSpec((count, block), cols),
                pl.BlockSpec((tokens, heads2), lambda j, where: (0, DEV)),
                pl.BlockSpec((16, heads2), lambda j, where: (tokens // 16 - 1, EDEV)),
                pl.BlockSpec((heads2, block), cols),
                pl.BlockSpec((STATE, tokens), same),
                *behind(len(after)),
            ],
            out_specs=[
                pl.BlockSpec((tokens, block), lambda j, where: (0, place(j, where))),
                pl.BlockSpec((MSG, block), lambda j, where: (0, jnp.minimum(j, blocks - 1))),
                pl.BlockSpec((KEPT, block), lambda j, where: (0, jnp.maximum(j - blocks, 0))),
            ],
            scratch_shapes=[pltpu.VMEM((tokens, block), BF16), pltpu.VMEM((tokens, block), F32)],
        ),
        out_shape=[
            jax.ShapeDtypeStruct((tokens, width), BF16),
            jax.ShapeDtypeStruct((MSG, half), BF16),
            jax.ShapeDtypeStruct((KEPT, half), F32),
        ],
        compiler_params=params(),
        name="front",
        cost_estimate=cost(4),
    )(where, features, halo, conv_feat, table, table, spread, turned, *after)


def span_kernel(
    first_head, order, xh_ref, map_ref, col_ref, row_ref, table_ref, spread_ref, skips_ref, halves_ref,
    *refs,
):
    y_ref, state = refs[order:]
    width = xh_ref.shape[1]
    head_dim = width // row_ref.shape[0]
    heads2 = spread_ref.shape[0]

    @pl.when(pl.program_id(0) == 0)
    def _():
        state[...] = jnp.zeros_like(state)

    t = lax.broadcasted_iota(jnp.int32, (SPAN, SPAN), 0)
    s = lax.broadcasted_iota(jnp.int32, (SPAN, SPAN), 1)
    first = halves_ref[0:1, :]
    second = halves_ref[1:2, :]
    block = 256
    for k in range(xh_ref.shape[0] // SPAN):
        rows = slice(k * SPAN, (k + 1) * SPAN)
        in_map = map_ref[rows, :STATE]
        out_map = map_ref[rows, STATE:]
        scores = lax.dot_general(out_map, in_map, (((1,), (1,)), ((), ())), preferred_element_type=F32)
        scores = jnp.where(s <= t, scores, 0.0)
        in_turned = in_map.T
        tables = jnp.concatenate([table_ref[rows, :heads2], table_ref[rows, heads2:], skips_ref[...]], axis=0)
        for q in range(width // block):
            cols = slice(q * block, (q + 1) * block)
            feats = xh_ref[rows, cols]
            feats32 = feats.astype(F32)
            wide = dot(tables, spread_ref[:, cols])
            scaled = (feats32 * wide[:SPAN]).astype(BF16)
            ecum = wide[SPAN : 2 * SPAN]
            skip = wide[2 * SPAN : 2 * SPAN + 1]
            pairs = []
            for p in range(block // 128):
                weights = []
                for i in range(2):
                    h = (q * block + p * 128) // head_dim + i
                    gap = col_ref[rows, first_head + h : first_head + h + 1] - row_ref[h : h + 1, rows]
                    weights.append((scores * jnp.exp(jnp.minimum(gap, 0.0))).astype(BF16))
                pair = feats[:, p * 128 : (p + 1) * 128]
                stacked = jnp.concatenate([pair * first, pair * second], axis=0)
                pairs.append(dot(jnp.concatenate(weights, axis=1), stacked))
            diag = jnp.concatenate(pairs, axis=1)
            held = state[:, cols]
            carried = dot(out_map, held.astype(BF16)) * ecum
            y_ref[rows, cols] = (diag + carried + skip * feats32).astype(BF16)
            state[:, cols] = ecum[SPAN - 1 :] * held + dot(in_turned, scaled)


def spans_of(chunk, part, parts, micros, head_dim, xh, both_maps, col, row, table, spread, skips, halves, after):
    tokens = xh.shape[0]
    width = chunk[1] // parts
    index = chunk[0] // width + part
    some = width // head_dim
    heads2 = spread.shape[0]
    tile = 2 * SPAN
    return pl.pallas_call(
        functools.partial(span_kernel, index * some, len(after)),
        grid=(tokens // tile,),
        in_specs=[
            pl.BlockSpec((tile, width), lambda k: (k, part)),
            pl.BlockSpec((tile, 2 * STATE), lambda k: (k, 0)),
            pl.BlockSpec((tile, heads2), lambda k: (k, 0)),
            pl.BlockSpec((some, tile), lambda k: (index, k)),
            pl.BlockSpec((tile, 2 * heads2), lambda k: (k, 0)),
            pl.BlockSpec((heads2, width), lambda k: (0, index)),
            pl.BlockSpec(skips.shape, lambda k: (0, 0)),
            pl.BlockSpec(halves.shape, lambda k: (0, 0)),
            *behind(len(after)),
        ],
        out_specs=pl.BlockSpec((tile, width), lambda k: (k, 0)),
        out_shape=jax.ShapeDtypeStruct((tokens, width), BF16),
        scratch_shapes=[pltpu.VMEM((STATE, width), F32)],
        compiler_params=params(),
        name="spans",
        cost_estimate=cost(micros),
    )(xh, both_maps, col, row, table, spread, skips, halves, *after)


def pair_kernel(where_ref, kept_ref, got_ref, *refs):
    total_ref, sent_ref = refs[-2:]
    kept, kept_decay = read_state(kept_ref)
    got, got_decay = read_state(got_ref)

    def put(first, second, decay):
        total = decay * first + second
        write_kept(total_ref, total, kept_decay * got_decay)
        write_sent(sent_ref, total, kept_decay * got_decay)

    @pl.when(where_ref[1] == 0)
    def _():
        put(kept, got, got_decay)

    @pl.when(where_ref[1] == 1)
    def _():
        put(got, kept, kept_decay)


def inclusive_kernel(total_ref, before_ref, *refs):
    sent_ref = refs[-1]
    total, decay = read_state(total_ref)
    before, before_decay = read_state(before_ref)
    write_sent(sent_ref, total + decay * before, decay * before_decay)


def extend_kernel(before_ref, far_ref, *refs):
    before, decay = read_state(before_ref)
    far, far_decay = read_state(far_ref)
    write_kept(refs[-1], before + decay * far, decay * far_decay)


def last_kernel(where_ref, before_ref, far_ref, kept_ref, got_ref, *refs):
    mine_ref, sent_ref = refs[-2:]
    before, before_decay = read_state(before_ref)
    far, _ = read_state(far_ref)
    carried = before + before_decay * far

    @pl.when(where_ref[1] == 0)
    def _():
        kept, decay = read_state(kept_ref)
        mine_ref[...] = carried.astype(BF16)
        sent_ref[...] = (decay * carried + kept).astype(BF16)

    @pl.when(where_ref[1] == 1)
    def _():
        got, decay = read_state(got_ref)
        mine_ref[...] = (decay * carried + got).astype(BF16)
        sent_ref[...] = carried.astype(BF16)


def join(kernel, name, where, operands, outs, after):
    width = operands[0].shape[1]
    shapes = {
        "kept": jax.ShapeDtypeStruct((KEPT, width), F32),
        "sent": jax.ShapeDtypeStruct((MSG, width), BF16),
        "state": jax.ShapeDtypeStruct((STATE, width), BF16),
    }
    scalars = [] if where is None else [where]
    return pl.pallas_call(
        kernel,
        in_specs=[pl.BlockSpec(memory_space=pltpu.SMEM)] * len(scalars)
        + [pl.BlockSpec(memory_space=pltpu.VMEM)] * len(operands)
        + behind(len(after)),
        out_specs=[pl.BlockSpec(memory_space=pltpu.VMEM)] * len(outs),
        out_shape=[shapes[out] for out in outs],
        compiler_params=params(VMEM_SMALL),
        name=name,
        cost_estimate=cost(0.7),
    )(*scalars, *operands, *after)


def back_kernel(mode, counts, partners, order, where_ref, out_ref, edev_ref, *refs):
    chunks = []
    for pieces in counts:
        chunks.append((refs[:pieces], *refs[pieces : pieces + 5]))
        refs = refs[pieces + 5 :]
    if mode == "rest":
        squares_ref, *refs = refs
    refs = refs[order:]
    o_refs = refs[:partners]
    if mode == "first":
        squares_ref = refs[partners]
    gated, sums = refs[-2:]
    out_map = out_ref[...]
    edev = edev_ref[...]
    rows = out_map.shape[0]
    block = 256
    steps = pl.num_programs(0) // partners
    odd = where_ref[1] == 1
    sums[...] = squares_ref[...] if mode == "rest" else jnp.zeros((rows, 128), F32)
    at = 0
    for y_refs, mine_ref, other_ref, spread_ref, gate_ref, gain_ref in chunks:
        half = mine_ref.shape[1]
        for q in range(2 * half // block):
            cols = slice(q * block, (q + 1) * block)
            inner = slice(q * block % half, q * block % half + block)
            mine = mine_ref[:, inner]
            other = other_ref[:, inner]
            state = jnp.where(odd, other, mine) if q * block < half else jnp.where(odd, mine, other)
            gated[:, at : at + block] = dot(out_map, state) * dot(edev, spread_ref[:, cols])
            y_ref = y_refs[q * block // y_refs[0].shape[1]]
            y_at = q * block % y_refs[0].shape[1]
            for c in range(block // 128):
                y_cols = slice(y_at + c * 128, y_at + (c + 1) * 128)
                to = slice(at + c * 128, at + (c + 1) * 128)
                cols = slice(q * block + c * 128, q * block + (c + 1) * 128)
                gain = gain_ref[:, cols]
                for b in range(rows // 64):
                    part = slice(b * 64, (b + 1) * 64)
                    value = (y_ref[part, y_cols].astype(F32) + gated[part, to]) * silu(gate_ref[part, cols].astype(F32))
                    sums[part, :] = sums[part, :] + value * value
                    gated[part, to] = value * gain
            at += block
    if mode == "first":
        squares_ref[...] = sums[...]
    else:
        width = at if mode == "whole" else 2 * at
        mean = jnp.sum(sums[...], axis=1, keepdims=True) * (1.0 / width)
        scale = lax.rsqrt(mean + EPS)
    for p in range(partners):

        @pl.when(pl.program_id(0) // steps == p)
        def _(o_ref=o_refs[p]):
            if mode == "rest":
                step = pl.program_id(0) - p * steps
                start = pl.multiple_of(step * rows, rows)
                high = scale.astype(BF16).astype(F32)
                parts = [jnp.broadcast_to(part, (rows, 128)).T[:8] for part in (high, scale - high)]
                o_ref[steps * rows :, pl.ds(start, rows)] = jnp.concatenate(parts, axis=0).astype(BF16)
            for q in range(at // block):
                cols = slice(q * block, (q + 1) * block)
                value = gated[:, cols] if mode == "first" else gated[:, cols] * scale
                if mode == "rest":
                    o_ref[pl.ds(start, rows), cols] = value.astype(BF16)
                else:
                    o_ref[:, cols] = value.astype(BF16)


def back(mode, some, where, rows, chunks, both_maps, table, spread, gates, gain_row, squares, after, own=None):
    heads2 = spread.shape[0]
    tile = 128
    steps = rows // tile
    partners = len(some)

    def at(i, where):
        turn = some[0]
        for p in range(1, partners):
            turn = jnp.where(i >= p * steps, some[p], turn)
        return ((where[0] ^ turn) * steps + i % steps, 0)

    specs = [
        pl.BlockSpec((tile, STATE), lambda i, where: (at(i, where)[0], 1)),
        pl.BlockSpec((tile, heads2), lambda i, where: (at(i, where)[0], EDEV)),
    ]
    operands = [both_maps, table]
    total = 0
    for (start, width), ys, mine, other in chunks:
        index = start // width
        half = width // 2
        total += width
        specs += [pl.BlockSpec((tile, y.shape[1]), at) for y in ys]
        specs += [
            pl.BlockSpec((STATE, half), lambda i, where: (0, 0)),
            pl.BlockSpec((STATE, half), lambda i, where: (0, 0)),
            pl.BlockSpec((heads2, width), lambda i, where, index=index: (0, index)),
            pl.BlockSpec((tile, width), lambda i, where, index=index: (at(i, where)[0], index)),
            pl.BlockSpec((1, width), lambda i, where, index=index: (0, index)),
        ]
        operands += [*ys, mine, other, spread, gates, gain_row]
    if mode == "rest":
        specs.append(pl.BlockSpec((tile, 128), lambda i, where: (i, 0)))
        operands.append(squares)
    aliases = {}
    if own is not None and own[2] is not None:
        after = [own[2], *after]
        aliases = {1 + len(operands): partners - 1}
    specs += behind(len(after))
    operands += after
    sent = rows + 16 if mode == "rest" else rows
    part = sent if mode == "rest" else tile

    def part_of(p):
        if mode == "rest":
            return lambda i, where: (0, 0)
        return lambda i, where: (jnp.clip(i - p * steps, 0, steps - 1), 0)

    out_specs = [pl.BlockSpec((part, total), part_of(p)) for p in range(partners)]
    out_shape = [jax.ShapeDtypeStruct((sent, total), BF16)] * partners
    if own is not None:
        group, groups, _ = own
        out_specs[-1] = pl.BlockSpec(
            (tile, total),
            lambda i, where: (jnp.clip(i - (partners - 1) * steps, 0, steps - 1), (where[0] ^ some[-1]) * groups + group),
        )
        out_shape[-1] = jax.ShapeDtypeStruct((rows, groups * total * (gates.shape[0] // rows)), BF16)
    if mode == "first":
        out_specs.append(pl.BlockSpec((tile, 128), lambda i, where: (i, 0)))
        out_shape.append(jax.ShapeDtypeStruct((partners * rows, 128), F32))
    return pl.pallas_call(
        functools.partial(back_kernel, mode, [len(ys) for _, ys, _, _ in chunks], partners, len(after)),
        grid_spec=pltpu.PrefetchScalarGridSpec(
            num_scalar_prefetch=1,
            grid=(partners * steps,),
            in_specs=specs,
            out_specs=out_specs,
            scratch_shapes=[pltpu.VMEM((tile, total), F32), pltpu.VMEM((tile, 128), F32)],
        ),
        out_shape=out_shape,
        input_output_aliases=aliases,
        compiler_params=params(),
        name=f"back_{mode}",
        cost_estimate=cost(1),
    )(where, *operands)


def mark_kernel(order, *refs):
    refs[order][...] = jnp.zeros((8, 128), F32)


def mark(after):
    return pl.pallas_call(
        functools.partial(mark_kernel, len(after)),
        grid=(1,),
        in_specs=behind(len(after)),
        out_specs=pl.BlockSpec((8, 128), lambda i: (0, 0)),
        out_shape=jax.ShapeDtypeStruct((8, 128), F32),
        compiler_params=params(VMEM_SMALL),
        name="mark",
        cost_estimate=cost(200),
    )(*after)


def shifted(value, pairs, steps):
    return lax.ppermute(
        value,
        "ctx",
        [(2 * q + y, 2 * (q + steps) + y) for q in range(pairs - steps) for y in range(2)],
    )


def swapped(value, pairs):
    return lax.ppermute(value, "ctx", [(2 * q + y, 2 * q + 1 - y) for q in range(pairs) for y in range(2)])


class Line:
    def __init__(self):
        self.last = []

    def run(self, make, *args, **kwargs):
        made = make(*args, after=self.last, **kwargs)
        self.last = [made[0] if isinstance(made, (list, tuple)) else made]
        return made


class Exchange:
    def __init__(self, line, where, pairs, sent, kept):
        self.line = line
        self.where = where
        self.pairs = pairs
        self.kept = kept
        self.got = swapped(sent, pairs)

    def pair(self):
        self.total, sent = self.line.run(
            join, pair_kernel, "pair", self.where, [self.kept, self.got], ["kept", "sent"]
        )
        self.before = shifted(sent, self.pairs, 1)
        self.reach = 1

    def double(self):
        (sent,) = self.line.run(join, inclusive_kernel, "inclusive", None, [self.total, self.before], ["sent"])
        self.far = shifted(sent, self.pairs, self.reach + 1)
        self.reach = 2 * self.reach + 1

    def extend(self):
        while self.reach < self.pairs - 1:
            (self.before,) = self.line.run(join, extend_kernel, "extend", None, [self.before, self.far], ["kept"])
            self.double()

    def finish(self):
        self.extend()
        self.mine, sent = self.line.run(
            join, last_kernel, "last", self.where, [self.before, self.far, self.kept, self.got], ["state", "state"]
        )
        self.other = lax.ppermute(
            sent, "ctx", [(2 * q + y, 2 * q + 1 - y) for q in range(self.pairs) for y in range(2) if q or not y]
        )


def shards(
    features, gates, state_io, step_size, log_decay, conv_feat, conv_state, skip_gain, norm_gain
):
    tokens, channels = features.shape
    heads = step_size.shape[0]
    head_dim = channels // heads
    groups = state_io.shape[2] // STATE
    group_width = channels // groups
    width = group_width // 2
    count = conv_feat.shape[0]
    rim = count - 1
    ctx_size = lax.axis_size("ctx")
    head_size = lax.axis_size("head")
    pairs = ctx_size // 2
    rows = tokens // head_size
    me = lax.axis_index("head").astype(jnp.int32)
    where = jnp.stack([me, lax.axis_index("ctx").astype(jnp.int32) % 2])

    onward = [(i, i + 1) for i in range(ctx_size - 1)]
    pad = HALO - rim
    halo = jnp.pad(lax.ppermute(features[tokens - rim :], "ctx", onward), ((pad, 0), (0, 0)))
    io_halo = jnp.pad(lax.ppermute(state_io[tokens - rim :], "ctx", onward), ((pad, 0), (0, 0), (0, 0)))
    spread = jnp.asarray(spread_table(heads, head_dim), BF16)
    halves = jnp.asarray(np.arange(128)[None, :] // head_dim == np.arange(2)[:, None], BF16)
    col, row, table, skips = decay_tables(log_decay, step_size, skip_gain)
    gain_row = norm_gain[None]

    line = Line()
    chunks = [(0, width), (width, width)] + [(g * group_width, group_width) for g in range(1, groups)]
    of_group = [[0, 1]] + [[g + 1] for g in range(1, groups)]
    group_of = [0, 0] + list(range(1, groups))
    fronts = {}
    maps = {}
    exchanges = {}
    ys = {}

    def run_maps(g):
        maps[g] = line.run(maps_of, g, state_io, io_halo, conv_state)

    def run_front(c):
        made = line.run(
            front, chunks[c], where, features, halo, conv_feat, table, spread, maps[group_of[c]][1]
        )
        fronts[c] = made[0]
        exchanges[c] = Exchange(line, where, pairs, made[1], made[2])

    def run_spans(c, part=0, parts=1, micros=200):
        g = group_of[c]
        made = line.run(
            spans_of, chunks[c], part, parts, micros, head_dim, fronts[c], maps[g][0], col, row, table, spread,
            skips, halves,
        )
        ys.setdefault(c, []).append(made)

    def part(c):
        return (chunks[c], ys[c], exchanges[c].mine, exchanges[c].other)

    partners = list(range(head_size - 1, 1, -1))
    squares = {}
    pieces = {}

    def ship(piece, r):
        return lax.ppermute(piece, "head", [(i, i ^ r) for i in range(head_size)])

    def run_back(mode, some, g, parts, squares, own=None):
        return line.run(
            back, mode, some, where, rows, [part(c) for c in parts], maps[g][0], table, spread, gates, gain_row,
            squares, own=own,
        )

    def arrived(g, index, some):
        line.last += [pieces[g, r][index] for r in some]

    def run_first(g, apart=False):
        squares[g] = []
        for some in [[r] for r in partners] if apart else [partners]:
            *made, square = run_back("first", some, g, [0], None)
            squares[g].append((some, square))
            for r, piece in zip(some, made):
                pieces[g, r] = [ship(piece, r)]

    def run_rest(g, turns):
        for some, square in squares[g][turns]:
            made = run_back("rest", some, g, [1], square)
            for r, piece in zip(some, made):
                pieces[g, r].append(ship(piece, r))

    result = None

    def run_one(g, r):
        (piece,) = run_back("whole", [r], g, of_group[g], None)
        pieces[g, r] = [ship(piece, r)]

    def run_own(g):
        nonlocal result
        before = line.last
        (result,) = run_back("whole", [0], g, of_group[g], None, own=(g, groups, result))
        line.last = before

    def run_put(g, r):
        nonlocal result
        start = (me ^ r) * channels + g * group_width
        zero = jnp.int32(0)
        if len(pieces[g, r]) == 2:
            first, rest = pieces[g, r]
            scale = rest[rows, :rows].astype(F32) + rest[rows + 8, :rows].astype(F32)
            first = (first.astype(F32) * scale[:, None]).astype(BF16)
            result = lax.dynamic_update_slice(result, first, (zero, start))
            result = lax.dynamic_update_slice(result, rest[:rows], (zero, start + width))
        else:
            result = lax.dynamic_update_slice(result, pieces[g, r][0], (zero, start))

    ex = exchanges
    later = range(1, groups)
    run_maps(0)
    run_front(0)
    run_front(1)
    ex[0].pair()
    for g in later:
        run_maps(g)
    ex[0].double()
    ex[1].pair()
    for g in later:
        run_front(g + 1)
    run_spans(0)
    ex[0].finish()
    ex[1].double()
    for g in later:
        ex[g + 1].pair()
    run_first(0, apart=True)
    if groups > 1:
        line.run(mark)
    run_spans(1, micros=1)
    ex[1].finish()
    for g in later:
        ex[g + 1].double()
    for g in later:
        run_spans(g + 1, micros=1)
    arrived(0, 0, partners)
    run_rest(0, slice(0, 1))
    for g in later:
        ex[g + 1].finish()
    run_rest(0, slice(1, None))
    run_one(0, 1)
    for g in later:
        arrived(0, 1, partners[:1])
        run_one(g, partners[0])
        run_one(g, 1)
        arrived(0, 1, partners[1:])
        for r in partners[1:]:
            run_one(g, r)
    run_own(0)
    for r in [*partners, 1]:
        run_put(0, r)
    for g in later:
        run_own(g)
        for r in [partners[0], 1, *partners[1:]]:
            run_put(g, r)
    return result


def solution(mesh):
    in_specs = (
        P("ctx", "head"),
        P("ctx", "head"),
        P("ctx", None, "head"),
        P("head", "ctx"),
        P("head", "ctx"),
        P(None, "head"),
        P(None, None, "head"),
        P("head"),
        P("head"),
    )
    out_specs = P(("ctx", "head"), None)
    return jax.shard_map(shards, mesh=mesh, in_specs=in_specs, out_specs=out_specs, check_vma=False)
```
